32 devices in a mesh: space: 8 (over z, y), pairs: 4 (over x, core).
Axes of the slice: x: 2, y: 2, z: 4, core: 2. Of those that a mesh axis runs over, the one named last changes fastest.
Arguments:
- positions: float32 [2048, 3, 512], P(('space', 'pairs')), may hold values from -3 to 25.2, as said below
- forces: float32 [2048, 3, 512], P(('space', 'pairs')), may hold values from -6 to 6
- pair_cells: int32 [2, 1536], P(None, ('space', 'pairs')), may hold values from 0 to 2047, as said below
- pair_count: int32 [32], P(('space', 'pairs')), may hold values from 6 to 48, as said below
Outputs:
- velocity: float32 [2048, 3, 512], P(('space', 'pairs'))
The draws below stay inside these ranges and needn't reach their ends.
Inputs may be any that keep to these rules, and one draw needn't show every extreme that they name: `pair_cells`: device g holds cells [g * 64, (g + 1) * 64). Row 0 of its slot columns names one of its own cells. Row 1 names a cell other than row 0's; over the 48 slots of one device it names cells of each of the 12 devices of the device's region and of the two regions beside it exactly 4 times, the first and the last region counting as beside each other. Slots at or past a device's count hold pairs too but are not in its list. `pair_count`: in every region one device holds 48 live slots. `positions`: the cells of region r have their first coordinates within 1.2 of [3 r, 3 r + 3); the other two coordinates lie within -3 to 5.
All inputs are finite; a program needn't handle non-finite values.
Results may differ from the reference program's by a relative error of at most 0.0003.
Values sent between devices are 32-bit elements; how exact they have to be, the bound alone decides.
No kernel may reach another device: no remote copies, remote signals or barrier semaphores. Data moves between devices by JAX's collectives and lax.ppermute only.
A program may use at most 128 MiB of HBM per device.

```python
import math
import jax
import jax.numpy as jnp
from jax import lax

P_SIZE = 512
CELL_DEV = 64
PAIR_SLOTS = 48
REGION = 256
CELLS = 2048
N_SPACE = 8
N_PAIRS = 4


def draw_positions(key, part):
    key = jax.random.fold_in(key, 13)
    key_centre, key_across, key_dirs, key_radius = jax.random.split(key, 4)
    extent = 2.0
    spread = 0.1
    breadth = 2.0
    region_of = (jnp.arange(CELLS, dtype=jnp.int32) // REGION).astype(jnp.float32)
    along = (region_of[:, None, None] + jax.random.uniform(key_centre, (CELLS, 1, 1), jnp.float32, 0.0, 1.0)) * 3.0
    across = jax.random.uniform(key_across, (CELLS, 2, 1), jnp.float32, 0.0, extent)
    centres = jnp.concatenate([along, across], axis=1)
    directions = jax.random.normal(key_dirs, (CELLS, 3, P_SIZE), jnp.float32)
    directions = directions / jnp.sqrt(jnp.sum(directions * directions, axis=1, keepdims=True) + 1e-06)
    axes_scale = jnp.array([1.0, breadth, breadth], jnp.float32).reshape(1, 3, 1)
    radius = 1.0 + spread * jax.random.uniform(key_radius, (CELLS, 1, P_SIZE), jnp.float32, -1.0, 1.0)
    return centres + radius * axes_scale * directions


def draw_pair_cells(key, part):
    key = jax.random.fold_in(key, 11)
    key_first, key_order, key_second = jax.random.split(key, 3)
    devices = N_SPACE * N_PAIRS
    owners = 3 * N_PAIRS
    share = PAIR_SLOTS // owners
    device = jnp.arange(devices, dtype=jnp.int32)
    home = device // N_PAIRS
    first = device[:, None] * CELL_DEV + jax.random.randint(key_first, (devices, PAIR_SLOTS), 0, CELL_DEV)
    scores = jax.random.randint(key_order, (devices, PAIR_SLOTS), 0, 1 << 20) * PAIR_SLOTS + jnp.arange(PAIR_SLOTS, dtype=jnp.int32)[None, :]
    order = jnp.argsort(scores, axis=1).astype(jnp.int32)
    bucket = order // share
    relative = bucket // N_PAIRS
    region_of = (home[:, None] + relative - 1 + N_SPACE) % N_SPACE
    owner = region_of * N_PAIRS + bucket % N_PAIRS
    local = jax.random.randint(key_second, (devices, PAIR_SLOTS), 0, CELL_DEV)
    second = owner * CELL_DEV + local
    second = jnp.where(second == first, owner * CELL_DEV + (local + 1) % CELL_DEV, second)
    return jnp.stack([first.reshape(-1), second.reshape(-1)]).astype(jnp.int32)


def draw_pair_count(key, part):
    key = jax.random.fold_in(key, 12)
    key_count, key_busy = jax.random.split(key, 2)
    devices = N_SPACE * N_PAIRS
    counts = jax.random.randint(key_count, (devices,), PAIR_SLOTS // 8, PAIR_SLOTS // 2 + 1)
    busiest = jax.random.randint(key_busy, (N_SPACE,), 0, N_PAIRS)
    device = jnp.arange(devices, dtype=jnp.int32)
    chosen = device % N_PAIRS == busiest[device // N_PAIRS]
    return jnp.where(chosen, PAIR_SLOTS, counts).astype(jnp.int32)


def level_of(stream_key, shape, shards, least, top_value):
    def one(dim, parts):
        steps = jax.random.uniform(jax.random.fold_in(jax.random.fold_in(stream_key, 6), dim), (parts,), jnp.float32, least / len(shards), top_value / len(shards))
        return jnp.repeat(jnp.exp(steps), shape[dim] // parts).reshape((-1,) + (1,) * (len(shape) - dim - 1))

    level = one(*shards[0])
    for cut in shards[1:]:
        level = level * one(*cut)
    return level


def gaussian(rng, shape, width, most, pieces=(), held_as=jnp.bfloat16):
    values = width * jax.random.normal(rng, shape, jnp.float32)
    if pieces:
        values = values * level_of(rng, shape, pieces, -0.22, 0.18)
    return jnp.clip(values, -most, most).astype(held_as)


def setup_inputs(seed: int = 0) -> dict:
    key_of = jax.random.split(jax.random.key(seed), 5)
    positions = draw_positions(jax.random.fold_in(key_of[4], 71), 0)
    forces = gaussian(key_of[1], (CELLS, 3, P_SIZE), 1.0, 6.0, ((0, 32),), jnp.float32)
    pair_cells = draw_pair_cells(jax.random.fold_in(key_of[4], 71), 0)
    pair_count = draw_pair_count(jax.random.fold_in(key_of[4], 71), 0)
    return {"positions": positions, "forces": forces, "pair_cells": pair_cells, "pair_count": pair_count}


stokes_coef = 1.0 / (8.0 * math.pi)
eps_sq = 0.01
slab_width = 3.0

def pair_velocities(first_cell, second_cell, period):
    deltas = [first_cell[component][:, None] - second_cell[component][None, :] for component in range(3)]
    half = 0.5 * period
    deltas[0] = jnp.where(deltas[0] > half, deltas[0] - period, jnp.where(deltas[0] < -half, deltas[0] + period, deltas[0]))
    dist_sq = deltas[0] * deltas[0] + deltas[1] * deltas[1] + deltas[2] * deltas[2]
    inverse = lax.rsqrt(dist_sq + eps_sq)
    cubed = inverse * inverse * inverse * stokes_coef
    direct = (dist_sq + 2.0 * eps_sq) * cubed
    along_second = sum((deltas[component] * second_cell[3 + component][None, :] for component in range(3)))
    along_first = sum((deltas[component] * first_cell[3 + component][:, None] for component in range(3)))
    weight_second = cubed * along_second
    weight_first = cubed * along_first
    first_velocity = jnp.stack([lax.optimization_barrier(jnp.sum(direct * second_cell[3 + component][None, :] + weight_second * deltas[component], axis=1)) for component in range(3)])
    second_velocity = jnp.stack([lax.optimization_barrier(jnp.sum(direct * first_cell[3 + component][:, None] + weight_first * deltas[component], axis=0)) for component in range(3)])
    return (first_velocity, second_velocity)

def add_pair(velocity, cell_data, first_id, second_id, period):
    first_cell = lax.dynamic_slice_in_dim(cell_data, first_id, 1, 0)[0]
    second_cell = lax.dynamic_slice_in_dim(cell_data, second_id, 1, 0)[0]
    first_velocity, second_velocity = pair_velocities(first_cell, second_cell, period)
    current = lax.dynamic_slice_in_dim(velocity, first_id, 1, 0)
    velocity = lax.dynamic_update_slice_in_dim(velocity, current + first_velocity[None], first_id, 0)
    current = lax.dynamic_slice_in_dim(velocity, second_id, 1, 0)
    velocity = lax.dynamic_update_slice_in_dim(velocity, current + second_velocity[None], second_id, 0)
    return velocity

def reference(positions, forces, pair_cells, pair_count):
    cell_data = jnp.concatenate([positions, forces], axis=1)
    velocity = jnp.zeros(positions.shape, jnp.float32)
    slots = pair_cells.shape[1] // pair_count.shape[0]
    period = slab_width * N_SPACE

    def step(number, velocity):
        device = number // slots
        live = number - device * slots < pair_count[device]
        first_id = pair_cells[0, number].astype(jnp.int32)
        second_id = pair_cells[1, number].astype(jnp.int32)
        return lax.cond(live, lambda vel_in: add_pair(vel_in, cell_data, first_id, second_id, period), lambda vel_in: vel_in, velocity)
    return lax.fori_loop(0, pair_cells.shape[1], step, velocity)
```

```python
import functools
import math

import jax
import jax.numpy as jnp
from jax import lax
from jax.experimental import pallas as pl
from jax.experimental.pallas import tpu as pltpu
from jax.sharding import PartitionSpec as P

stokes_coef = 1.0 / (8.0 * math.pi)
eps_sq = 0.01
slab_width = 3.0
across_middle = 1.0
LANES = 128
FEATURES = 16

f32 = jnp.float32
bf16 = jnp.bfloat16


def split(value, terms):
    parts = []
    for _ in range(terms - 1):
        part = value.astype(bf16).astype(f32)
        parts.append(part)
        value = value - part
    parts.append(value)
    return parts


def features(x, f):
    norm = jnp.sum(x * x, axis=0, keepdims=True)
    along = jnp.sum(x * f, axis=0, keepdims=True)
    rows = [f] + [x[k : k + 1] * f for k in range(3)] + [norm * f + x * along]
    rows.append(jnp.zeros_like(norm))
    stacked = jnp.concatenate(rows, axis=0)
    return jnp.concatenate([part.astype(bf16) for part in split(stacked, 3)], axis=0)


def combine(sums, y):
    force = sums[0:3]
    moment = [sums[3 + 3 * k : 6 + 3 * k] for k in range(3)]
    second = sums[12:15]
    norm = jnp.sum(y * y, axis=0, keepdims=True)
    trace = moment[0][0:1] + moment[1][1:2] + moment[2][2:3]
    along = jnp.sum(y * force, axis=0, keepdims=True) - trace
    turned = jnp.concatenate(
        [jnp.sum(y * moment[k], axis=0, keepdims=True) for k in range(3)], axis=0
    )
    mixed = y[0:1] * moment[0] + y[1:2] * moment[1] + y[2:3] * moment[2]
    velocity = (norm + 2.0 * eps_sq) * force + second - 2.0 * mixed + y * along - turned
    return velocity * stokes_coef


def gram_factors(x, y):
    one = jnp.ones((1, x.shape[1]), f32)
    none = jnp.zeros((3, x.shape[1]), f32)
    norm_x = jnp.sum(x * x, axis=0, keepdims=True)
    norm_y = jnp.sum(y * y, axis=0, keepdims=True) + eps_sq
    left = split(jnp.concatenate([x, norm_x, one, none], axis=0), 3)
    right = split(jnp.concatenate([-2.0 * y, one, norm_y, none], axis=0), 3)
    order = ((0, 0), (0, 1), (1, 0), (0, 2), (1, 1), (2, 0))
    return (
        jnp.concatenate([left[p] for p, _ in order], axis=0).astype(bf16),
        jnp.concatenate([right[q] for _, q in order], axis=0).astype(bf16),
    )


def dot(left, right, left_dim, right_dim):
    return lax.dot_general(
        left, right, (((left_dim,), (right_dim,)), ((), ())), preferred_element_type=f32
    )


def fold(high, low):
    return (
        high[0:FEATURES]
        + high[FEATURES : 2 * FEATURES]
        + high[2 * FEATURES :]
        + low[0:FEATURES]
        + low[FEATURES:]
    )


def pair_velocities(xa, fa, xb, fb):
    left, right = gram_factors(xa, xb)
    dist_sq = dot(left, right, 0, 0)
    inverse = lax.rsqrt(dist_sq)
    cubed = inverse * inverse * inverse
    high = cubed.astype(bf16)
    low = (cubed - high.astype(f32)).astype(bf16)
    feat_a = features(xa, fa)
    feat_b = features(xb, fb)
    two = 2 * FEATURES
    sums_b = fold(dot(feat_a, high, 1, 0), dot(feat_a[:two], low, 1, 0))
    sums_a = fold(dot(feat_b, high, 1, 1), dot(feat_b[:two], low, 1, 1))
    return combine(sums_a, xa), combine(sums_b, xb)


def pack_kernel(sizes, cells, count, pos, frc, *outs):
    n_space, n_pairs, share, cell_dev, tiles = sizes
    messages, table, slots, used = outs[:-3], outs[-3], outs[-2], outs[-1]
    n_slots = cells.shape[1]
    here = cells[0, 0] // cell_dev
    here_space = here // n_pairs
    here_pairs = lax.rem(here, n_pairs)

    def clear(i, _):
        used[i] = 0
        return 0

    lax.fori_loop(0, len(messages), clear, 0)

    def place(s, _):
        owner = cells[1, s] // cell_dev
        step = lax.rem(owner // n_pairs - here_space + 1 + n_space, n_space)
        turn = lax.rem(lax.rem(owner, n_pairs) - here_pairs + n_pairs, n_pairs)
        bucket = step * n_pairs + turn
        rank = used[bucket]
        used[bucket] = rank + 1
        slots[bucket * share + rank] = s
        return 0

    lax.fori_loop(0, n_slots, place, 0)
    lane = lax.broadcasted_iota(jnp.int32, (1, LANES), 1)
    for m, message in enumerate(messages):
        label = jnp.full((1, LANES), -1.0, f32)
        for k in range(share):
            s = slots[m * share + k]
            a = lax.rem(cells[0, s], cell_dev)
            live = s < count[0]
            b = jnp.where(live, lax.rem(cells[1, s], cell_dev), -1)
            table[m * share + k] = jnp.where(live, a, -1)
            label = jnp.where(lane == k, b.astype(f32), label)
            for c in range(6):
                source = pos if c < 3 else frc
                for t in range(tiles):
                    row = k * 6 * tiles + t * 6 + c
                    place_in = row_of(c % 3, a, t, cell_dev, tiles)
                    message[row : row + 1, :] = source[pl.ds(place_in, 1), :]
        last = share * 6 * tiles
        message[last : last + 1, :] = label


def pair_kernel(sizes, steps, cells, *refs):
    n_space, n_pairs, share, cell_dev, tiles = sizes
    n = len(steps)
    labels, messages = refs[:n], refs[n : 2 * n]
    pos, frc, acc_in, acc = refs[2 * n : 2 * n + 4]
    replies = refs[2 * n + 4 : 3 * n + 4]
    inbox, outbox, todo = refs[3 * n + 4 :]
    rows_in = share * 6 * tiles
    rows_out = share * 3 * tiles
    here_space = cells[0, 0] // (cell_dev * n_pairs)

    acc[...] = acc_in[...]
    number = jnp.int32(0)
    for m in range(n):
        inbox[m * rows_in : (m + 1) * rows_in, :] = messages[m][0:rows_in, :]
        for k in range(share):
            b = labels[m][0, k].astype(jnp.int32)
            todo[0, number] = m * share + k
            todo[1, number] = b
            todo[2, number] = steps[m]
            number = number + jnp.where(b >= 0, 1, 0)

    def one(i, _):
        slot = todo[0, i]
        b = todo[1, i]
        step = todo[2, i]
        from_space = lax.rem(here_space - step + n_space, n_space)
        half = 0.5 * slab_width * step.astype(f32)
        middle_a = slab_width * (from_space.astype(f32) + 0.5) + half
        middle_b = slab_width * (here_space.astype(f32) + 0.5) - half
        base = slot * (6 * tiles)
        block = jnp.concatenate(
            [inbox[pl.ds(base + 6 * t, 6), :] for t in range(tiles)], axis=1
        )
        axis = lax.broadcasted_iota(jnp.int32, (3, 1), 0)
        xa = block[0:3] - jnp.where(axis == 0, middle_a, across_middle)
        fa = block[3:6]
        where = [[row_of(c, b, t, cell_dev, tiles) for t in range(tiles)] for c in range(3)]
        xb, fb = (
            jnp.concatenate(
                [
                    jnp.concatenate([ref[pl.ds(row, 1), :] for row in rows], axis=1)
                    for rows in where
                ],
                axis=0,
            )
            for ref in (pos, frc)
        )
        xb = xb - jnp.where(axis == 0, middle_b, across_middle)
        vel_a, vel_b = pair_velocities(xa, fa, xb, fb)
        for c in range(3):
            for t in range(tiles):
                part = slice(t * LANES, (t + 1) * LANES)
                acc[pl.ds(where[c][t], 1), :] += vel_b[c : c + 1, part]
        base = slot * (3 * tiles)
        for t in range(tiles):
            outbox[pl.ds(base + 3 * t, 3), :] = vel_a[:, t * LANES : (t + 1) * LANES]
        return 0

    lax.fori_loop(0, number, one, 0)
    for m in range(n):
        replies[m][...] = outbox[m * rows_out : (m + 1) * rows_out, :]


def add_kernel(sizes, table, acc, *refs):
    _, _, share, cell_dev, tiles = sizes
    replies, out = refs[:-1], refs[-1]
    out[...] = acc[...]
    for m, reply in enumerate(replies):
        for k in range(share):
            a = table[m * share + k]
            live = a >= 0
            a = jnp.maximum(a, 0)
            for t in range(tiles):
                for c in range(3):
                    row = k * 3 * tiles + t * 3 + c
                    term = jnp.where(live, reply[row : row + 1, :], 0.0)
                    out[pl.ds(row_of(c, a, t, cell_dev, tiles), 1), :] += term


def flat_rows(cells):
    count, _, points = cells.shape
    value = jnp.transpose(cells, (1, 0, 2)).reshape(3, count // 8, 8, points // LANES, LANES)
    return jnp.transpose(value, (0, 1, 3, 2, 4)).reshape(-1, LANES)


def cell_rows(rows, count, points):
    value = rows.reshape(3, count // 8, points // LANES, 8, LANES)
    value = jnp.transpose(value, (0, 1, 3, 2, 4)).reshape(3, count, points)
    return jnp.transpose(value, (1, 0, 2))


def row_of(c, cell, t, cell_dev, tiles):
    return ((c * (cell_dev // 8) + cell // 8) * tiles + t) * 8 + lax.rem(cell, 8)


def body(positions, forces, pair_cells, pair_count):
    n_space = lax.axis_size("space")
    n_pairs = lax.axis_size("pairs")
    cell_dev, _, points = positions.shape
    n_slots = pair_cells.shape[1]
    n_messages = 3 * n_pairs
    share = n_slots // n_messages
    tiles = points // LANES
    sizes = (n_space, n_pairs, share, cell_dev, tiles)
    rows_in = share * 6 * tiles
    rows_out = share * 3 * tiles
    pos = flat_rows(positions)
    frc = flat_rows(forces)
    vmem = pl.BlockSpec(memory_space=pltpu.VMEM)
    smem = pl.BlockSpec(memory_space=pltpu.SMEM)
    limit = pltpu.CompilerParams(vmem_limit_bytes=48 * 1024 * 1024)

    message = jax.ShapeDtypeStruct((rows_in + 8, LANES), f32)
    reply = jax.ShapeDtypeStruct((rows_out, LANES), f32)
    total = jax.ShapeDtypeStruct((3 * cell_dev * tiles, LANES), f32)
    packed = pl.pallas_call(
        functools.partial(pack_kernel, sizes),
        out_shape=[message] * n_messages + [jax.ShapeDtypeStruct((n_slots,), jnp.int32)],
        in_specs=[smem, smem, vmem, vmem],
        out_specs=[vmem] * n_messages + [smem],
        scratch_shapes=[pltpu.SMEM((n_slots,), jnp.int32), pltpu.SMEM((n_messages,), jnp.int32)],
        compiler_params=limit,
        name="pack",
    )(pair_cells, pair_count, pos, frc)
    sent, table = packed[:-1], packed[-1]

    def moved(value, step, turn, back):
        if step == 0 and turn == 0:
            return value
        perm = []
        for i in range(n_space):
            for j in range(n_pairs):
                source = i * n_pairs + j
                target = (i + step) % n_space * n_pairs + (j + turn) % n_pairs
                perm.append((target, source) if back else (source, target))
        return lax.ppermute(value, ("space", "pairs"), perm)

    ways = [(step, turn) for step in (-1, 0, 1) for turn in range(n_pairs)]
    got = [moved(sent[m], *way, False) for m, way in enumerate(ways)]
    acc = jnp.zeros(total.shape, f32)
    replies = [None] * n_messages
    label = pl.BlockSpec((8, LANES), lambda i: (rows_in // 8, 0), memory_space=pltpu.SMEM)
    for wanted in (0, -1, 1):
        group = [m for m, way in enumerate(ways) if way[0] == wanted]
        n = len(group)
        arrived = [got[m] for m in group]
        results = pl.pallas_call(
            functools.partial(pair_kernel, sizes, [ways[m][0] for m in group]),
            out_shape=[total] + [reply] * n,
            grid=(1,),
            in_specs=[smem] + [label] * n + [vmem] * (n + 3),
            out_specs=[vmem] * (n + 1),
            scratch_shapes=[
                pltpu.VMEM((n * rows_in, LANES), f32),
                pltpu.VMEM((n * rows_out, LANES), f32),
                pltpu.SMEM((3, n * share + 1), jnp.int32),
            ],
            compiler_params=limit,
            cost_estimate=pl.CostEstimate(
                flops=4_000_000_000, bytes_accessed=2_000_000, transcendentals=2_000_000
            ),
            name="pairs",
        )(pair_cells, *arrived, *arrived, pos, frc, acc)
        acc = results[0]
        for m, value in zip(group, results[1:]):
            replies[m] = moved(value, *ways[m], True)

    velocity = pl.pallas_call(
        functools.partial(add_kernel, sizes),
        out_shape=total,
        in_specs=[smem] + [vmem] * (n_messages + 1),
        out_specs=vmem,
        compiler_params=limit,
        name="add",
    )(table, acc, *replies)
    return cell_rows(velocity, cell_dev, points)


def solution(mesh):
    placed = (
        P(("space", "pairs"), None, None),
        P(("space", "pairs"), None, None),
        P(None, ("space", "pairs")),
        P(("space", "pairs")),
    )
    return jax.shard_map(
        body,
        mesh=mesh,
        in_specs=placed,
        out_specs=P(("space", "pairs"), None, None),
        check_vma=False,
    )
```

```python
import functools
import math

import jax
import jax.numpy as jnp
from jax import lax
from jax.experimental import pallas as pl
from jax.experimental.pallas import tpu as pltpu
from jax.sharding import PartitionSpec as P

stokes_coef = 1.0 / (8.0 * math.pi)
eps_sq = 0.01
slab_width = 3.0
across_middle = 1.0
LANES = 128
FEATURES = 16

f32 = jnp.float32
bf16 = jnp.bfloat16


def split(value, terms):
    parts = []
    for _ in range(terms - 1):
        part = value.astype(bf16).astype(f32)
        parts.append(part)
        value = value - part
    parts.append(value)
    return parts


def features(x, f):
    norm = jnp.sum(x * x, axis=0, keepdims=True)
    along = jnp.sum(x * f, axis=0, keepdims=True)
    rows = [f] + [x[k : k + 1] * f for k in range(3)] + [norm * f + x * along]
    rows.append(jnp.zeros_like(norm))
    stacked = jnp.concatenate(rows, axis=0)
    return jnp.concatenate([part.astype(bf16) for part in split(stacked, 3)], axis=0)


def combine(sums, y):
    force = sums[0:3]
    moment = [sums[3 + 3 * k : 6 + 3 * k] for k in range(3)]
    second = sums[12:15]
    norm = jnp.sum(y * y, axis=0, keepdims=True)
    trace = moment[0][0:1] + moment[1][1:2] + moment[2][2:3]
    along = jnp.sum(y * force, axis=0, keepdims=True) - trace
    turned = jnp.concatenate(
        [jnp.sum(y * moment[k], axis=0, keepdims=True) for k in range(3)], axis=0
    )
    mixed = y[0:1] * moment[0] + y[1:2] * moment[1] + y[2:3] * moment[2]
    velocity = (norm + 2.0 * eps_sq) * force + second - 2.0 * mixed + y * along - turned
    return velocity * stokes_coef


def gram_factors(x, y):
    one = jnp.ones((1, x.shape[1]), f32)
    none = jnp.zeros((3, x.shape[1]), f32)
    norm_x = jnp.sum(x * x, axis=0, keepdims=True)
    norm_y = jnp.sum(y * y, axis=0, keepdims=True) + eps_sq
    left = split(jnp.concatenate([x, norm_x, one, none], axis=0), 3)
    right = split(jnp.concatenate([-2.0 * y, one, norm_y, none], axis=0), 3)
    order = ((0, 0), (0, 1), (1, 0), (0, 2), (1, 1), (2, 0))
    return (
        jnp.concatenate([left[p] for p, _ in order], axis=0).astype(bf16),
        jnp.concatenate([right[q] for _, q in order], axis=0).astype(bf16),
    )


def dot(left, right, left_dim, right_dim):
    return lax.dot_general(
        left, right, (((left_dim,), (right_dim,)), ((), ())), preferred_element_type=f32
    )


def fold(high, low):
    return (
        high[0:FEATURES]
        + high[FEATURES : 2 * FEATURES]
        + high[2 * FEATURES :]
        + low[0:FEATURES]
        + low[FEATURES:]
    )


def pair_velocities(xa, fa, xb, fb):
    left, right = gram_factors(xa, xb)
    dist_sq = dot(left, right, 0, 0)
    inverse = lax.rsqrt(dist_sq)
    cubed = inverse * inverse * inverse
    high = cubed.astype(bf16)
    low = (cubed - high.astype(f32)).astype(bf16)
    feat_a = features(xa, fa)
    feat_b = features(xb, fb)
    two = 2 * FEATURES
    sums_b = fold(dot(feat_a, high, 1, 0), dot(feat_a[:two], low, 1, 0))
    sums_a = fold(dot(feat_b, high, 1, 1), dot(feat_b[:two], low, 1, 1))
    return combine(sums_a, xa), combine(sums_b, xb)


def row_base(cell, tiles):
    return cell // 8 * (8 * tiles) + lax.rem(cell, 8)


def pack_kernel(sizes, cells, count, pos_hbm, frc_hbm, out_a, out_b, table, slots, used, pos, frc, sems):
    n_space, n_pairs, share, cell_dev, tiles = sizes
    fetches = [
        pltpu.make_async_copy(pos_hbm, pos, sems.at[0]),
        pltpu.make_async_copy(frc_hbm, frc, sems.at[1]),
    ]
    for fetch in fetches:
        fetch.start()
    n_slots = cells.shape[1]
    here = cells[0, 0] // (cell_dev * n_pairs)
    odd = lax.rem(here, 2)
    for bucket in range(3 * n_pairs):
        used[bucket] = 0
    for s in range(n_slots):
        owner = cells[1, s] // cell_dev
        there = owner // n_pairs
        turn = lax.rem(owner, n_pairs)
        first = there // 2 == here // 2
        bucket = jnp.where(first, lax.rem(there, 2), 2) * n_pairs + turn
        rank = used[bucket]
        used[bucket] = rank + 1
        slots[bucket * share + rank] = s
    for fetch in fetches:
        fetch.wait()
    lane = lax.broadcasted_iota(jnp.int32, (1, LANES), 1)
    plane = cell_dev * tiles
    for m in range(3 * n_pairs):
        if m < 2 * n_pairs:
            out, block = out_a, m
        else:
            out, block = out_b, odd * n_pairs + (m - 2 * n_pairs)
        label = jnp.full((1, LANES), -1.0, f32)
        for k in range(share):
            s = slots[m * share + k]
            a = lax.rem(cells[0, s], cell_dev)
            live = s < count[0]
            b = jnp.where(live, lax.rem(cells[1, s], cell_dev), -1)
            table[m * share + k] = jnp.where(live, a, -1)
            label = jnp.where(lane == k, b.astype(f32), label)
            base = row_base(a, tiles)
            for c in range(6):
                source = pos if c < 3 else frc
                for t in range(tiles):
                    row = (k * tiles + t) * 6 + c
                    out[block, row : row + 1, :] = source[
                        pl.ds(base + (c % 3 * plane + t * 8), 1), :
                    ]
        last = share * 6 * tiles
        out[block, last : last + 1, :] = label


def pair_kernel(sizes, second, cells, labels, messages, pos, frc, *refs):
    n_space, n_pairs, share, cell_dev, tiles = sizes
    acc, reply, todo = refs[-3:]
    here = cells[0, 0] // (cell_dev * n_pairs)
    odd = lax.rem(here, 2)
    if second:
        acc[...] = refs[0][...]
        blocks = [odd * n_pairs + turn for turn in range(n_pairs)]
    else:
        acc[...] = jnp.zeros_like(acc)
        blocks = list(range(2 * n_pairs))
    number = jnp.int32(0)
    for block in blocks:
        for k in range(share):
            b = labels[block, 0, k].astype(jnp.int32)
            todo[0, number] = block
            todo[1, number] = b
            todo[2, number] = k
            number = number + jnp.where(b >= 0, 1, 0)
    plane = cell_dev * tiles

    def one(i, _):
        block = todo[0, i]
        b = todo[1, i]
        k = todo[2, i]
        if second:
            away = 2 * odd - 1
        else:
            away = block // n_pairs - odd
        there = lax.rem(here + away + n_space, n_space)
        half = 0.5 * slab_width * away.astype(f32)
        middle_a = slab_width * (there.astype(f32) + 0.5) - half
        middle_b = slab_width * (here.astype(f32) + 0.5) + half
        base = k * (6 * tiles)
        data = jnp.concatenate(
            [messages[block, pl.ds(base + 6 * t, 6), :] for t in range(tiles)], axis=1
        )
        axis = lax.broadcasted_iota(jnp.int32, (3, 1), 0)
        xa = data[0:3] - jnp.where(axis == 0, middle_a, across_middle)
        fa = data[3:6]
        start = row_base(b, tiles)
        where = [[start + (c * plane + t * 8) for t in range(tiles)] for c in range(3)]
        xb, fb = (
            jnp.concatenate(
                [
                    jnp.concatenate([ref[pl.ds(row, 1), :] for row in rows], axis=1)
                    for rows in where
                ],
                axis=0,
            )
            for ref in (pos, frc)
        )
        xb = xb - jnp.where(axis == 0, middle_b, across_middle)
        vel_a, vel_b = pair_velocities(xa, fa, xb, fb)
        base = k * (3 * tiles)
        for t in range(tiles):
            part = slice(t * LANES, (t + 1) * LANES)
            for c in range(3):
                acc[pl.ds(where[c][t], 1), :] += vel_b[c : c + 1, part]
            reply[block, pl.ds(base + 3 * t, 3), :] = vel_a[:, part]
        return 0

    lax.fori_loop(0, number, one, 0)


def add_kernel(sizes, cells, table, acc, reply_a, reply_b, out):
    n_space, n_pairs, share, cell_dev, tiles = sizes
    odd = lax.rem(cells[0, 0] // (cell_dev * n_pairs), 2)
    plane = cell_dev * tiles
    out[...] = acc[...]
    for m in range(3 * n_pairs):
        if m < 2 * n_pairs:
            reply, block = reply_a, m
        else:
            reply, block = reply_b, odd * n_pairs + (m - 2 * n_pairs)
        for k in range(share):
            a = table[m * share + k]
            live = a >= 0
            base = row_base(jnp.maximum(a, 0), tiles)
            for t in range(tiles):
                for c in range(3):
                    row = (k * tiles + t) * 3 + c
                    term = jnp.where(live, reply[block, row : row + 1, :], 0.0)
                    out[pl.ds(base + (c * plane + t * 8), 1), :] += term


def flat_rows(cells):
    count, _, points = cells.shape
    value = jnp.transpose(cells, (1, 0, 2)).reshape(3, count // 8, 8, points // LANES, LANES)
    return jnp.transpose(value, (0, 1, 3, 2, 4)).reshape(-1, LANES)


def cell_rows(rows, count, points):
    value = rows.reshape(3, count // 8, points // LANES, 8, LANES)
    value = jnp.transpose(value, (0, 1, 3, 2, 4)).reshape(3, count, points)
    return jnp.transpose(value, (1, 0, 2))


def body(positions, forces, pair_cells, pair_count):
    n_space = lax.axis_size("space")
    n_pairs = lax.axis_size("pairs")
    cell_dev, _, points = positions.shape
    n_slots = pair_cells.shape[1]
    share = n_slots // (3 * n_pairs)
    tiles = points // LANES
    sizes = (n_space, n_pairs, share, cell_dev, tiles)
    rows_in = share * 6 * tiles
    rows_out = share * 3 * tiles
    pos = flat_rows(positions)
    frc = flat_rows(forces)
    vmem = pl.BlockSpec(memory_space=pltpu.VMEM)
    smem = pl.BlockSpec(memory_space=pltpu.SMEM)
    hbm = pl.BlockSpec(memory_space=pltpu.HBM)
    limit = pltpu.CompilerParams(vmem_limit_bytes=48 * 1024 * 1024)
    message = jax.ShapeDtypeStruct((2 * n_pairs, rows_in + 8, LANES), f32)
    reply = jax.ShapeDtypeStruct((2 * n_pairs, rows_out, LANES), f32)
    total = jax.ShapeDtypeStruct((3 * cell_dev * tiles, LANES), f32)

    def exchange(value, first):
        groups = [
            [(i + j) % n_space * n_pairs + k for j in range(2) for k in range(n_pairs)]
            for i in range(1 - first, n_space, 2)
        ]
        return lax.all_to_all(value, ("space", "pairs"), 0, 0, axis_index_groups=groups)

    sent_a, sent_b, table = pl.pallas_call(
        functools.partial(pack_kernel, sizes),
        out_shape=[message, message, jax.ShapeDtypeStruct((n_slots,), jnp.int32)],
        in_specs=[smem, smem, hbm, hbm],
        out_specs=[vmem, vmem, smem],
        scratch_shapes=[
            pltpu.SMEM((n_slots,), jnp.int32),
            pltpu.SMEM((3 * n_pairs,), jnp.int32),
            pltpu.VMEM(total.shape, f32),
            pltpu.VMEM(total.shape, f32),
            pltpu.SemaphoreType.DMA((2,)),
        ],
        compiler_params=limit,
        name="pack",
    )(pair_cells, pair_count, pos, frc)
    got_a = exchange(sent_a, 1)
    got_b = exchange(sent_b, 0)
    label = pl.BlockSpec(
        (2 * n_pairs, 8, LANES), lambda i: (0, rows_in // 8, 0), memory_space=pltpu.SMEM
    )

    def pairs(got, before, work):
        return pl.pallas_call(
            functools.partial(pair_kernel, sizes, len(before) == 1),
            out_shape=[total, reply],
            grid=(1,),
            in_specs=[smem, label] + [vmem] * (3 + len(before)),
            out_specs=[vmem] * 2,
            scratch_shapes=[pltpu.SMEM((3, 2 * n_pairs * share + 1), jnp.int32)],
            compiler_params=limit,
            cost_estimate=pl.CostEstimate(
                flops=work * 2_000_000_000, bytes_accessed=2_000_000, transcendentals=2_000_000
            ),
            name="pairs",
        )(pair_cells, got, got, pos, frc, *before)

    acc, reply_a = pairs(got_a, [], 2)
    back_a = exchange(reply_a, 1)
    acc, reply_b = pairs(got_b, [acc], 1)
    back_b = exchange(reply_b, 0)
    velocity = pl.pallas_call(
        functools.partial(add_kernel, sizes),
        out_shape=total,
        in_specs=[smem, smem, vmem, vmem, vmem],
        out_specs=vmem,
        compiler_params=limit,
        name="add",
    )(pair_cells, table, acc, back_a, back_b)
    return cell_rows(velocity, cell_dev, points)


def solution(mesh):
    placed = (
        P(("space", "pairs"), None, None),
        P(("space", "pairs"), None, None),
        P(None, ("space", "pairs")),
        P(("space", "pairs")),
    )
    return jax.shard_map(
        body,
        mesh=mesh,
        in_specs=placed,
        out_specs=P(("space", "pairs"), None, None),
        check_vma=False,
    )
```

```python
import functools
import math

import jax
import jax.numpy as jnp
from jax import lax
from jax.experimental import pallas as pl
from jax.experimental.pallas import tpu as pltpu
from jax.sharding import PartitionSpec as P

stokes_coef = 1.0 / (8.0 * math.pi)
eps_sq = 0.01
slab_width = 3.0
across_middle = 1.0
LANES = 128
FEATURES = 16

f32 = jnp.float32
bf16 = jnp.bfloat16


def split(value, terms):
    parts = []
    for _ in range(terms - 1):
        part = value.astype(bf16).astype(f32)
        parts.append(part)
        value = value - part
    parts.append(value)
    return parts


def features(x, f):
    norm = jnp.sum(x * x, axis=0, keepdims=True)
    along = jnp.sum(x * f, axis=0, keepdims=True)
    rows = [f] + [x[k : k + 1] * f for k in range(3)] + [norm * f + x * along]
    rows.append(jnp.zeros_like(norm))
    stacked = jnp.concatenate(rows, axis=0)
    return jnp.concatenate([part.astype(bf16) for part in split(stacked, 3)], axis=0)


def combine(sums, y):
    force = sums[0:3]
    moment = [sums[3 + 3 * k : 6 + 3 * k] for k in range(3)]
    second = sums[12:15]
    norm = jnp.sum(y * y, axis=0, keepdims=True)
    trace = moment[0][0:1] + moment[1][1:2] + moment[2][2:3]
    along = jnp.sum(y * force, axis=0, keepdims=True) - trace
    turned = jnp.concatenate(
        [jnp.sum(y * moment[k], axis=0, keepdims=True) for k in range(3)], axis=0
    )
    mixed = y[0:1] * moment[0] + y[1:2] * moment[1] + y[2:3] * moment[2]
    velocity = (norm + 2.0 * eps_sq) * force + second - 2.0 * mixed + y * along - turned
    return velocity * stokes_coef


def gram_factors(x, y):
    one = jnp.ones((1, x.shape[1]), f32)
    none = jnp.zeros((3, x.shape[1]), f32)
    norm_x = jnp.sum(x * x, axis=0, keepdims=True)
    norm_y = jnp.sum(y * y, axis=0, keepdims=True) + eps_sq
    left = split(jnp.concatenate([x, norm_x, one, none], axis=0), 3)
    right = split(jnp.concatenate([-2.0 * y, one, norm_y, none], axis=0), 3)
    order = ((0, 0), (0, 1), (1, 0), (0, 2), (1, 1), (2, 0))
    return (
        jnp.concatenate([left[p] for p, _ in order], axis=0).astype(bf16),
        jnp.concatenate([right[q] for _, q in order], axis=0).astype(bf16),
    )


def dot(left, right, left_dim, right_dim):
    return lax.dot_general(
        left, right, (((left_dim,), (right_dim,)), ((), ())), preferred_element_type=f32
    )


def fold(high, low):
    return (
        high[0:FEATURES]
        + high[FEATURES : 2 * FEATURES]
        + high[2 * FEATURES :]
        + low[0:FEATURES]
        + low[FEATURES:]
    )


def pair_velocities(xa, fa, xb, fb):
    left, right = gram_factors(xa, xb)
    dist_sq = dot(left, right, 0, 0)
    inverse = lax.rsqrt(dist_sq)
    cubed = inverse * inverse * inverse
    high = cubed.astype(bf16)
    low = (cubed - high.astype(f32)).astype(bf16)
    feat_a = features(xa, fa)
    feat_b = features(xb, fb)
    two = 2 * FEATURES
    sums_b = fold(dot(feat_a, high, 1, 0), dot(feat_a[:two], low, 1, 0))
    sums_a = fold(dot(feat_b, high, 1, 1), dot(feat_b[:two], low, 1, 1))
    return combine(sums_a, xa), combine(sums_b, xb)


def row_base(cell, tiles):
    return cell // 8 * (8 * tiles) + lax.rem(cell, 8)


def away_of(kind, odd):
    return (0, 1 - 2 * odd, 2 * odd - 1)[kind]


def pack_kernel(sizes, cells, count, pos_hbm, frc_hbm, *refs):
    n_space, n_pairs, share, cell_dev, tiles = sizes
    outs, table = refs[:n_pairs], refs[n_pairs]
    slots, used, pos, frc, sems = refs[n_pairs + 1 :]
    fetches = [
        pltpu.make_async_copy(pos_hbm, pos, sems.at[0]),
        pltpu.make_async_copy(frc_hbm, frc, sems.at[1]),
    ]
    for fetch in fetches:
        fetch.start()
    n_slots = cells.shape[1]
    owner = cells[0, 0] // cell_dev
    here = owner // n_pairs
    here_turn = lax.rem(owner, n_pairs)
    table[n_slots] = here
    for bucket in range(3 * n_pairs):
        used[bucket] = 0
    for s in range(n_slots):
        owner = cells[1, s] // cell_dev
        there = owner // n_pairs
        turn = lax.rem(owner, n_pairs) ^ here_turn
        kind = jnp.where(there == here, 0, jnp.where(there // 2 == here // 2, 1, 2))
        bucket = kind * n_pairs + turn
        rank = used[bucket]
        used[bucket] = rank + 1
        slots[bucket * share + rank] = s
    for fetch in fetches:
        fetch.wait()
    lane = lax.broadcasted_iota(jnp.int32, (1, LANES), 1)
    plane = cell_dev * tiles
    for m in range(3 * n_pairs):
        kind, turn = m // n_pairs, m % n_pairs
        out = outs[turn]
        label = jnp.full((1, LANES), -1.0, f32)
        for k in range(share):
            s = slots[m * share + k]
            a = lax.rem(cells[0, s], cell_dev)
            live = s < count[0]
            b = jnp.where(live, lax.rem(cells[1, s], cell_dev), -1)
            table[m * share + k] = jnp.where(live, a, -1)
            label = jnp.where(lane == k, b.astype(f32), label)
            base = row_base(a, tiles)
            for c in range(6):
                source = pos if c < 3 else frc
                for t in range(tiles):
                    row = (k * tiles + t) * 6 + c
                    out[kind, row : row + 1, :] = source[
                        pl.ds(base + (c % 3 * plane + t * 8), 1), :
                    ]
        last = share * 6 * tiles
        out[kind, last : last + 1, :] = label


def pair_kernel(sizes, kind, n, started, table, *refs):
    n_space, n_pairs, share, cell_dev, tiles = sizes
    labels, messages = refs[:n], refs[n : 2 * n]
    pos, frc = refs[2 * n : 2 * n + 2]
    acc, reply, inbox, todo = refs[-4:]
    here = table[3 * n_pairs * share]
    away = jnp.int32(away_of(kind, lax.rem(here, 2)))
    there = lax.rem(here + away + n_space, n_space)
    half = 0.5 * slab_width * away.astype(f32)
    middle_a = slab_width * (there.astype(f32) + 0.5) - half
    middle_b = slab_width * (here.astype(f32) + 0.5) + half
    rows_in = share * 6 * tiles
    plane = cell_dev * tiles
    if started:
        acc[...] = refs[2 * n + 2][...]
    else:
        acc[...] = jnp.zeros_like(acc)
    number = jnp.int32(0)
    first = 0
    for label, message in zip(labels, messages):
        for block in range(message.shape[0]):
            inbox[first * rows_in : (first + 1) * rows_in, :] = message[block, 0:rows_in, :]
            for k in range(share):
                b = label[block, 0, k].astype(jnp.int32)
                todo[0, number] = first * share + k
                todo[1, number] = b
                number = number + jnp.where(b >= 0, 1, 0)
            first += 1

    def one(i, _):
        slot = todo[0, i]
        b = todo[1, i]
        base = slot * (6 * tiles)
        data = jnp.concatenate(
            [inbox[pl.ds(base + 6 * t, 6), :] for t in range(tiles)], axis=1
        )
        axis = lax.broadcasted_iota(jnp.int32, (3, 1), 0)
        xa = data[0:3] - jnp.where(axis == 0, middle_a, across_middle)
        fa = data[3:6]
        start = row_base(b, tiles)
        where = [[start + (c * plane + t * 8) for t in range(tiles)] for c in range(3)]
        xb, fb = (
            jnp.concatenate(
                [
                    jnp.concatenate([ref[pl.ds(row, 1), :] for row in rows], axis=1)
                    for rows in where
                ],
                axis=0,
            )
            for ref in (pos, frc)
        )
        xb = xb - jnp.where(axis == 0, middle_b, across_middle)
        vel_a, vel_b = pair_velocities(xa, fa, xb, fb)
        base = slot * (3 * tiles)
        for t in range(tiles):
            part = slice(t * LANES, (t + 1) * LANES)
            for c in range(3):
                acc[pl.ds(where[c][t], 1), :] += vel_b[c : c + 1, part]
            reply[pl.ds(base + 3 * t, 3), :] = vel_a[:, part]
        return 0

    lax.fori_loop(0, number, one, 0)


def add_kernel(sizes, table, acc, *refs):
    n_space, n_pairs, share, cell_dev, tiles = sizes
    replies, out = refs[:-1], refs[-1]
    plane = cell_dev * tiles
    out[...] = acc[...]
    for m in range(3 * n_pairs):
        kind, turn = m // n_pairs, m % n_pairs
        for k in range(share):
            a = table[m * share + k]
            live = a >= 0
            base = row_base(jnp.maximum(a, 0), tiles)
            for t in range(tiles):
                for c in range(3):
                    row = (k * tiles + t) * 3 + c
                    term = jnp.where(live, replies[turn][kind, row : row + 1, :], 0.0)
                    out[pl.ds(base + (c * plane + t * 8), 1), :] += term


def flat_rows(cells):
    count, _, points = cells.shape
    value = jnp.transpose(cells, (1, 0, 2)).reshape(3, count // 8, 8, points // LANES, LANES)
    return jnp.transpose(value, (0, 1, 3, 2, 4)).reshape(-1, LANES)


def cell_rows(rows, count, points):
    value = rows.reshape(3, count // 8, points // LANES, 8, LANES)
    value = jnp.transpose(value, (0, 1, 3, 2, 4)).reshape(3, count, points)
    return jnp.transpose(value, (1, 0, 2))


def body(positions, forces, pair_cells, pair_count):
    n_space = lax.axis_size("space")
    n_pairs = lax.axis_size("pairs")
    cell_dev, _, points = positions.shape
    n_slots = pair_cells.shape[1]
    share = n_slots // (3 * n_pairs)
    tiles = points // LANES
    sizes = (n_space, n_pairs, share, cell_dev, tiles)
    rows_in = share * 6 * tiles
    rows_out = share * 3 * tiles
    pos = flat_rows(positions)
    frc = flat_rows(forces)
    vmem = pl.BlockSpec(memory_space=pltpu.VMEM)
    smem = pl.BlockSpec(memory_space=pltpu.SMEM)
    hbm = pl.BlockSpec(memory_space=pltpu.HBM)
    message = jax.ShapeDtypeStruct((3, rows_in + 8, LANES), f32)
    total = jax.ShapeDtypeStruct((3 * cell_dev * tiles, LANES), f32)

    def across(value, turn):
        return lax.ppermute(value, "pairs", [(j, j ^ turn) for j in range(n_pairs)])

    def beyond(value, kind):
        moves = [(i, (i + away_of(kind, i % 2)) % n_space) for i in range(n_space)]
        return lax.ppermute(value, "space", moves)

    packed = pl.pallas_call(
        functools.partial(pack_kernel, sizes),
        out_shape=[message] * n_pairs + [jax.ShapeDtypeStruct((n_slots + 1,), jnp.int32)],
        in_specs=[smem, smem, hbm, hbm],
        out_specs=[vmem] * n_pairs + [smem],
        scratch_shapes=[
            pltpu.SMEM((n_slots,), jnp.int32),
            pltpu.SMEM((3 * n_pairs,), jnp.int32),
            pltpu.VMEM(total.shape, f32),
            pltpu.VMEM(total.shape, f32),
            pltpu.SemaphoreType.DMA((2,)),
        ],
        compiler_params=pltpu.CompilerParams(vmem_limit_bytes=60 * 1024 * 1024),
        name="pack",
    )(pair_cells, pair_count, pos, frc)
    sent, table = packed[:n_pairs], packed[n_pairs]
    got = [sent[0]] + [across(sent[turn], turn) for turn in range(1, n_pairs)]

    def pairs(kind, arrived, before, own=False):
        n = len(arrived)
        blocks = 1 if kind == 0 else n_pairs
        part = kind if kind == 0 else 0
        label = pl.BlockSpec(
            (blocks, 8, LANES), lambda i: (part, rows_in // 8, 0), memory_space=pltpu.SMEM
        )
        data = pl.BlockSpec((blocks, rows_in + 8, LANES), lambda i: (part, 0, 0))
        work = 1 if own else 4
        return pl.pallas_call(
            functools.partial(pair_kernel, sizes, kind, n, len(before) == 1),
            out_shape=[total, jax.ShapeDtypeStruct((n * blocks * rows_out, LANES), f32)],
            grid=(1,),
            in_specs=[smem] + [label] * n + [data] * n + [vmem] * (2 + len(before)),
            out_specs=[vmem] * 2,
            scratch_shapes=[
                pltpu.VMEM((n * blocks * rows_in, LANES), f32),
                pltpu.SMEM((2, n * blocks * share + 1), jnp.int32),
            ],
            compiler_params=pltpu.CompilerParams(vmem_limit_bytes=48 * 1024 * 1024),
            cost_estimate=pl.CostEstimate(
                flops=work * 1_000_000_000, bytes_accessed=2_000_000, transcendentals=2_000_000
            ),
            name="pairs",
        )(table, *arrived, *arrived, pos, frc, *before)

    acc, reply_own = pairs(0, got[:1], [], True)
    out_1 = beyond(jnp.stack([value[1] for value in got]), 1)
    out_2 = beyond(jnp.stack([value[2] for value in got]), 2)
    acc, reply_0 = pairs(0, got[1:], [acc])
    acc, reply_1 = pairs(1, [out_1], [acc])
    back_1 = beyond(reply_1, 1)
    acc, reply_2 = pairs(2, [out_2], [acc])
    back_2 = beyond(reply_2, 2)
    back_0 = jnp.concatenate([reply_own, reply_0], axis=0)
    shape = (n_pairs, rows_out, LANES)
    back_0, back_1, back_2 = (value.reshape(shape) for value in (back_0, back_1, back_2))
    back = []
    for turn in range(n_pairs):
        value = jnp.stack([back_0[turn], back_1[turn], back_2[turn]])
        back.append(across(value, turn) if turn else value)
    velocity = pl.pallas_call(
        functools.partial(add_kernel, sizes),
        out_shape=total,
        in_specs=[smem] + [vmem] * (1 + n_pairs),
        out_specs=vmem,
        compiler_params=pltpu.CompilerParams(vmem_limit_bytes=48 * 1024 * 1024),
        name="add",
    )(table, acc, *back)
    return cell_rows(velocity, cell_dev, points)


def solution(mesh):
    placed = (
        P(("space", "pairs"), None, None),
        P(("space", "pairs"), None, None),
        P(None, ("space", "pairs")),
        P(("space", "pairs")),
    )
    return jax.shard_map(
        body,
        mesh=mesh,
        in_specs=placed,
        out_specs=P(("space", "pairs"), None, None),
        check_vma=False,
    )
```

```python
import functools
import math

import jax
import jax.numpy as jnp
from jax import lax
from jax.experimental import pallas as pl
from jax.experimental.pallas import tpu as pltpu
from jax.sharding import PartitionSpec as P

stokes_coef = 1.0 / (8.0 * math.pi)
eps_sq = 0.01
slab_width = 3.0
across_middle = 1.0
LANES = 128
FEATURES = 16

f32 = jnp.float32
bf16 = jnp.bfloat16


def split(value, terms):
    parts = []
    for _ in range(terms - 1):
        part = value.astype(bf16).astype(f32)
        parts.append(part)
        value = value - part
    parts.append(value)
    return parts


def features(x, f):
    norm = jnp.sum(x * x, axis=0, keepdims=True)
    along = jnp.sum(x * f, axis=0, keepdims=True)
    rows = [f] + [x[k : k + 1] * f for k in range(3)] + [norm * f + x * along]
    rows.append(jnp.zeros_like(norm))
    stacked = jnp.concatenate(rows, axis=0)
    return jnp.concatenate([part.astype(bf16) for part in split(stacked, 3)], axis=0)


def combine(sums, y):
    force = sums[0:3]
    moment = [sums[3 + 3 * k : 6 + 3 * k] for k in range(3)]
    second = sums[12:15]
    norm = jnp.sum(y * y, axis=0, keepdims=True)
    trace = moment[0][0:1] + moment[1][1:2] + moment[2][2:3]
    along = jnp.sum(y * force, axis=0, keepdims=True) - trace
    turned = jnp.concatenate(
        [jnp.sum(y * moment[k], axis=0, keepdims=True) for k in range(3)], axis=0
    )
    mixed = y[0:1] * moment[0] + y[1:2] * moment[1] + y[2:3] * moment[2]
    velocity = (norm + 2.0 * eps_sq) * force + second - 2.0 * mixed + y * along - turned
    return velocity * stokes_coef


def gram_factors(x, y):
    one = jnp.ones((1, x.shape[1]), f32)
    none = jnp.zeros((3, x.shape[1]), f32)
    norm_x = jnp.sum(x * x, axis=0, keepdims=True)
    norm_y = jnp.sum(y * y, axis=0, keepdims=True) + eps_sq
    left = split(jnp.concatenate([x, norm_x, one, none], axis=0), 3)
    right = split(jnp.concatenate([-2.0 * y, one, norm_y, none], axis=0), 3)
    order = ((0, 0), (0, 1), (1, 0), (0, 2), (1, 1), (2, 0))
    return (
        jnp.concatenate([left[p] for p, _ in order], axis=0).astype(bf16),
        jnp.concatenate([right[q] for _, q in order], axis=0).astype(bf16),
    )


def dot(left, right, left_dim, right_dim):
    return lax.dot_general(
        left, right, (((left_dim,), (right_dim,)), ((), ())), preferred_element_type=f32
    )


def fold(sums):
    return sums[0:FEATURES] + sums[FEATURES : 2 * FEATURES] + sums[2 * FEATURES :]


def pair_velocities(xa, fa, xb, fb):
    left, right = gram_factors(xa, xb)
    dist_sq = dot(left, right, 0, 0)
    inverse = lax.rsqrt(dist_sq)
    cubed = inverse * inverse * inverse
    high = cubed.astype(bf16)
    low = (cubed - high.astype(f32)).astype(bf16)
    feat_a = features(xa, fa)
    feat_b = features(xb, fb)
    sums_b = fold(dot(feat_a, high, 1, 0) + dot(feat_a, low, 1, 0))
    columns = dot(high, feat_b, 1, 1) + dot(low, feat_b, 1, 1)
    sums_a = fold(jnp.transpose(columns))
    return combine(sums_a, xa), combine(sums_b, xb)


def row_base(cell, tiles):
    return cell // 8 * (8 * tiles) + lax.rem(cell, 8)


def away_of(kind, odd):
    return (0, 1 - 2 * odd, 2 * odd - 1)[kind]


def pack_kernel(sizes, cells, count, pos_hbm, frc_hbm, *refs):
    n_space, n_pairs, share, cell_dev, tiles = sizes
    outs, table = refs[:n_pairs], refs[n_pairs]
    slots, used, pos, frc, sems = refs[n_pairs + 1 :]
    fetches = [
        pltpu.make_async_copy(pos_hbm, pos, sems.at[0]),
        pltpu.make_async_copy(frc_hbm, frc, sems.at[1]),
    ]
    for fetch in fetches:
        fetch.start()
    n_slots = cells.shape[1]
    owner = cells[0, 0] // cell_dev
    here = owner // n_pairs
    here_turn = lax.rem(owner, n_pairs)
    table[n_slots] = here
    for bucket in range(3 * n_pairs):
        used[bucket] = 0
    for s in range(n_slots):
        owner = cells[1, s] // cell_dev
        there = owner // n_pairs
        turn = lax.rem(owner, n_pairs) ^ here_turn
        kind = jnp.where(there == here, 0, jnp.where(there // 2 == here // 2, 1, 2))
        bucket = kind * n_pairs + turn
        rank = used[bucket]
        used[bucket] = rank + 1
        slots[bucket * share + rank] = s
    for fetch in fetches:
        fetch.wait()
    lane = lax.broadcasted_iota(jnp.int32, (1, LANES), 1)
    plane = cell_dev * tiles
    for m in range(3 * n_pairs):
        kind, turn = m // n_pairs, m % n_pairs
        out = outs[turn]
        label = jnp.full((1, LANES), -1.0, f32)
        for k in range(share):
            s = slots[m * share + k]
            a = lax.rem(cells[0, s], cell_dev)
            live = s < count[0]
            b = jnp.where(live, lax.rem(cells[1, s], cell_dev), -1)
            table[m * share + k] = jnp.where(live, a, -1)
            label = jnp.where(lane == k, b.astype(f32), label)
            base = row_base(a, tiles)
            for c in range(6):
                source = pos if c < 3 else frc
                for t in range(tiles):
                    row = (k * tiles + t) * 6 + c
                    out[kind, row : row + 1, :] = source[
                        pl.ds(base + (c % 3 * plane + t * 8), 1), :
                    ]
        last = share * 6 * tiles
        out[kind, last : last + 1, :] = label


def pair_kernel(sizes, kind, n, started, table, *refs):
    n_space, n_pairs, share, cell_dev, tiles = sizes
    labels, messages = refs[:n], refs[n : 2 * n]
    pos, frc = refs[2 * n : 2 * n + 2]
    acc, reply, inbox, todo = refs[-4:]
    here = table[3 * n_pairs * share]
    away = jnp.int32(away_of(kind, lax.rem(here, 2)))
    there = lax.rem(here + away + n_space, n_space)
    half = 0.5 * slab_width * away.astype(f32)
    middle_a = slab_width * (there.astype(f32) + 0.5) - half
    middle_b = slab_width * (here.astype(f32) + 0.5) + half
    rows_in = share * 6 * tiles
    plane = cell_dev * tiles
    if started:
        acc[...] = refs[2 * n + 2][...]
    else:
        acc[...] = jnp.zeros_like(acc)
    number = jnp.int32(0)
    first = 0
    for label, message in zip(labels, messages):
        for block in range(message.shape[0]):
            inbox[first * rows_in : (first + 1) * rows_in, :] = message[block, 0:rows_in, :]
            for k in range(share):
                b = label[block, 0, k].astype(jnp.int32)
                todo[0, number] = first * share + k
                todo[1, number] = b
                number = number + jnp.where(b >= 0, 1, 0)
            first += 1

    def one(i, _):
        slot = todo[0, i]
        b = todo[1, i]
        base = slot * (6 * tiles)
        data = jnp.concatenate(
            [inbox[pl.ds(base + 6 * t, 6), :] for t in range(tiles)], axis=1
        )
        axis = lax.broadcasted_iota(jnp.int32, (3, 1), 0)
        xa = data[0:3] - jnp.where(axis == 0, middle_a, across_middle)
        fa = data[3:6]
        start = row_base(b, tiles)
        where = [[start + (c * plane + t * 8) for t in range(tiles)] for c in range(3)]
        xb, fb = (
            jnp.concatenate(
                [
                    jnp.concatenate([ref[pl.ds(row, 1), :] for row in rows], axis=1)
                    for rows in where
                ],
                axis=0,
            )
            for ref in (pos, frc)
        )
        xb = xb - jnp.where(axis == 0, middle_b, across_middle)
        vel_a, vel_b = pair_velocities(xa, fa, xb, fb)
        base = slot * (3 * tiles)
        for t in range(tiles):
            part = slice(t * LANES, (t + 1) * LANES)
            for c in range(3):
                acc[pl.ds(where[c][t], 1), :] += vel_b[c : c + 1, part]
            reply[pl.ds(base + 3 * t, 3), :] = vel_a[:, part]
        return 0

    lax.fori_loop(0, number, one, 0)


def add_kernel(sizes, table, acc, *refs):
    n_space, n_pairs, share, cell_dev, tiles = sizes
    replies, out = refs[:-1], refs[-1]
    plane = cell_dev * tiles
    out[...] = acc[...]
    for m in range(3 * n_pairs):
        kind, turn = m // n_pairs, m % n_pairs
        for k in range(share):
            a = table[m * share + k]
            live = a >= 0
            base = row_base(jnp.maximum(a, 0), tiles)
            for t in range(tiles):
                for c in range(3):
                    row = (k * tiles + t) * 3 + c
                    term = jnp.where(live, replies[turn][kind, row : row + 1, :], 0.0)
                    out[pl.ds(base + (c * plane + t * 8), 1), :] += term


def flat_rows(cells):
    count, _, points = cells.shape
    value = jnp.transpose(cells, (1, 0, 2)).reshape(3, count // 8, 8, points // LANES, LANES)
    return jnp.transpose(value, (0, 1, 3, 2, 4)).reshape(-1, LANES)


def cell_rows(rows, count, points):
    value = rows.reshape(3, count // 8, points // LANES, 8, LANES)
    value = jnp.transpose(value, (0, 1, 3, 2, 4)).reshape(3, count, points)
    return jnp.transpose(value, (1, 0, 2))


def body(positions, forces, pair_cells, pair_count):
    n_space = lax.axis_size("space")
    n_pairs = lax.axis_size("pairs")
    cell_dev, _, points = positions.shape
    n_slots = pair_cells.shape[1]
    share = n_slots // (3 * n_pairs)
    tiles = points // LANES
    sizes = (n_space, n_pairs, share, cell_dev, tiles)
    rows_in = share * 6 * tiles
    rows_out = share * 3 * tiles
    pos = flat_rows(positions)
    frc = flat_rows(forces)
    vmem = pl.BlockSpec(memory_space=pltpu.VMEM)
    smem = pl.BlockSpec(memory_space=pltpu.SMEM)
    hbm = pl.BlockSpec(memory_space=pltpu.HBM)
    message = jax.ShapeDtypeStruct((3, rows_in + 8, LANES), f32)
    total = jax.ShapeDtypeStruct((3 * cell_dev * tiles, LANES), f32)

    def across(value, turn):
        return lax.ppermute(value, "pairs", [(j, j ^ turn) for j in range(n_pairs)])

    def beyond(value, kind):
        moves = [(i, (i + away_of(kind, i % 2)) % n_space) for i in range(n_space)]
        return lax.ppermute(value, "space", moves)

    packed = pl.pallas_call(
        functools.partial(pack_kernel, sizes),
        out_shape=[message] * n_pairs + [jax.ShapeDtypeStruct((n_slots + 1,), jnp.int32)],
        in_specs=[smem, smem, hbm, hbm],
        out_specs=[vmem] * n_pairs + [smem],
        scratch_shapes=[
            pltpu.SMEM((n_slots,), jnp.int32),
            pltpu.SMEM((3 * n_pairs,), jnp.int32),
            pltpu.VMEM(total.shape, f32),
            pltpu.VMEM(total.shape, f32),
            pltpu.SemaphoreType.DMA((2,)),
        ],
        compiler_params=pltpu.CompilerParams(vmem_limit_bytes=60 * 1024 * 1024),
        name="pack",
    )(pair_cells, pair_count, pos, frc)
    sent, table = packed[:n_pairs], packed[n_pairs]
    got = [sent[0]] + [across(sent[turn], turn) for turn in range(1, n_pairs)]

    def pairs(kind, arrived, before, own=False):
        n = len(arrived)
        blocks = 1 if kind == 0 else n_pairs
        part = kind if kind == 0 else 0
        label = pl.BlockSpec(
            (blocks, 8, LANES), lambda i: (part, rows_in // 8, 0), memory_space=pltpu.SMEM
        )
        data = pl.BlockSpec((blocks, rows_in + 8, LANES), lambda i: (part, 0, 0))
        work = 1 if own else 4
        return pl.pallas_call(
            functools.partial(pair_kernel, sizes, kind, n, len(before) == 1),
            out_shape=[total, jax.ShapeDtypeStruct((n * blocks * rows_out, LANES), f32)],
            grid=(1,),
            in_specs=[smem] + [label] * n + [data] * n + [vmem] * (2 + len(before)),
            out_specs=[vmem] * 2,
            scratch_shapes=[
                pltpu.VMEM((n * blocks * rows_in, LANES), f32),
                pltpu.SMEM((2, n * blocks * share + 1), jnp.int32),
            ],
            compiler_params=pltpu.CompilerParams(vmem_limit_bytes=48 * 1024 * 1024),
            cost_estimate=pl.CostEstimate(
                flops=work * 1_000_000_000, bytes_accessed=2_000_000, transcendentals=2_000_000
            ),
            name="pairs",
        )(table, *arrived, *arrived, pos, frc, *before)

    acc, reply_own = pairs(0, got[:1], [], True)
    out_1 = beyond(jnp.stack([value[1] for value in got]), 1)
    out_2 = beyond(jnp.stack([value[2] for value in got]), 2)
    acc, reply_0 = pairs(0, got[1:], [acc])
    acc, reply_1 = pairs(1, [out_1], [acc])
    back_1 = beyond(reply_1, 1)
    acc, reply_2 = pairs(2, [out_2], [acc])
    back_2 = beyond(reply_2, 2)
    back_0 = jnp.concatenate([reply_own, reply_0], axis=0)
    shape = (n_pairs, rows_out, LANES)
    back_0, back_1, back_2 = (value.reshape(shape) for value in (back_0, back_1, back_2))
    back = []
    for turn in range(n_pairs):
        value = jnp.stack([back_0[turn], back_1[turn], back_2[turn]])
        back.append(across(value, turn) if turn else value)
    velocity = pl.pallas_call(
        functools.partial(add_kernel, sizes),
        out_shape=total,
        in_specs=[smem] + [vmem] * (1 + n_pairs),
        out_specs=vmem,
        compiler_params=pltpu.CompilerParams(vmem_limit_bytes=48 * 1024 * 1024),
        name="add",
    )(table, acc, *back)
    return cell_rows(velocity, cell_dev, points)


def solution(mesh):
    placed = (
        P(("space", "pairs"), None, None),
        P(("space", "pairs"), None, None),
        P(None, ("space", "pairs")),
        P(("space", "pairs")),
    )
    return jax.shard_map(
        body,
        mesh=mesh,
        in_specs=placed,
        out_specs=P(("space", "pairs"), None, None),
        check_vma=False,
    )
```

```python
import functools
import math

import jax
import jax.numpy as jnp
from jax import lax
from jax.experimental import pallas as pl
from jax.experimental.pallas import tpu as pltpu
from jax.sharding import PartitionSpec as P

stokes_coef = 1.0 / (8.0 * math.pi)
eps_sq = 0.01
slab_width = 3.0
across_middle = 1.0
LANES = 128
FEATURES = 16

f32 = jnp.float32
bf16 = jnp.bfloat16


def split(value, terms):
    parts = []
    for _ in range(terms - 1):
        part = value.astype(bf16).astype(f32)
        parts.append(part)
        value = value - part
    parts.append(value)
    return parts


def features(x, f):
    norm = jnp.sum(x * x, axis=0, keepdims=True)
    along = jnp.sum(x * f, axis=0, keepdims=True)
    rows = [f] + [x[k : k + 1] * f for k in range(3)] + [norm * f + x * along]
    rows.append(jnp.zeros_like(norm))
    stacked = jnp.concatenate(rows, axis=0)
    return jnp.concatenate([part.astype(bf16) for part in split(stacked, 3)], axis=0)


def combine(sums, y):
    force = sums[0:3]
    moment = [sums[3 + 3 * k : 6 + 3 * k] for k in range(3)]
    second = sums[12:15]
    norm = jnp.sum(y * y, axis=0, keepdims=True)
    trace = moment[0][0:1] + moment[1][1:2] + moment[2][2:3]
    along = jnp.sum(y * force, axis=0, keepdims=True) - trace
    turned = jnp.concatenate(
        [jnp.sum(y * moment[k], axis=0, keepdims=True) for k in range(3)], axis=0
    )
    mixed = y[0:1] * moment[0] + y[1:2] * moment[1] + y[2:3] * moment[2]
    velocity = (norm + 2.0 * eps_sq) * force + second - 2.0 * mixed + y * along - turned
    return velocity * stokes_coef


def gram_factors(x, y):
    one = jnp.ones((1, x.shape[1]), f32)
    none = jnp.zeros((3, x.shape[1]), f32)
    norm_x = jnp.sum(x * x, axis=0, keepdims=True)
    norm_y = jnp.sum(y * y, axis=0, keepdims=True) + eps_sq
    left = split(jnp.concatenate([x, norm_x, one, none], axis=0), 3)
    right = split(jnp.concatenate([-2.0 * y, one, norm_y, none], axis=0), 3)
    order = ((0, 0), (0, 1), (1, 0), (0, 2), (1, 1), (2, 0))
    return (
        jnp.concatenate([left[p] for p, _ in order], axis=0).astype(bf16),
        jnp.concatenate([right[q] for _, q in order], axis=0).astype(bf16),
    )


def dot(left, right, left_dim, right_dim):
    return lax.dot_general(
        left, right, (((left_dim,), (right_dim,)), ((), ())), preferred_element_type=f32
    )


def fold(high, low):
    return (
        high[0:FEATURES]
        + high[FEATURES : 2 * FEATURES]
        + high[2 * FEATURES :]
        + low[0:FEATURES]
        + low[FEATURES:]
    )


def weights(factors, half):
    left, right = factors
    dist_sq = dot(left[:, half], right, 0, 0)
    inverse = lax.rsqrt(dist_sq)
    cubed = inverse * inverse * inverse
    high = cubed.astype(bf16)
    return high, (cubed - high.astype(f32)).astype(bf16)


def pair_velocities(cells):
    two = 2 * FEATURES
    points = cells[0][0].shape[1]
    halves = [slice(0, points // 2), slice(points // 2, points)]
    factors = [gram_factors(xa, xb) for xa, _, xb, _ in cells]
    feats = [(features(xa, fa), features(xb, fb)) for xa, fa, xb, fb in cells]
    sums_a = [[] for _ in cells]
    sums_b = [[] for _ in cells]
    for half in halves:
        for i, (feat_a, feat_b) in enumerate(feats):
            high, low = weights(factors[i], half)
            part = feat_a[:, half]
            sums_b[i].append(fold(dot(part, high, 1, 0), dot(part[:two], low, 1, 0)))
            sums_a[i].append(fold(dot(feat_b, high, 1, 1), dot(feat_b[:two], low, 1, 1)))
    return [
        (
            combine(jnp.concatenate(sums_a[i], axis=1), xa),
            combine(sums_b[i][0] + sums_b[i][1], xb),
        )
        for i, (xa, _, xb, _) in enumerate(cells)
    ]


def row_base(cell, tiles):
    return cell // 8 * (8 * tiles) + lax.rem(cell, 8)


def away_of(kind, odd):
    return (0, 1 - 2 * odd, 2 * odd - 1)[kind]


def pack_kernel(sizes, cells, count, pos_hbm, frc_hbm, *refs):
    n_space, n_pairs, share, cell_dev, tiles = sizes
    outs, table = refs[:n_pairs], refs[n_pairs]
    slots, used, pos, frc, sems = refs[n_pairs + 1 :]
    fetches = [
        pltpu.make_async_copy(pos_hbm, pos, sems.at[0]),
        pltpu.make_async_copy(frc_hbm, frc, sems.at[1]),
    ]
    for fetch in fetches:
        fetch.start()
    n_slots = cells.shape[1]
    owner = cells[0, 0] // cell_dev
    here = owner // n_pairs
    here_turn = lax.rem(owner, n_pairs)
    table[n_slots] = here
    for bucket in range(3 * n_pairs):
        used[bucket] = 0
    for s in range(n_slots):
        owner = cells[1, s] // cell_dev
        there = owner // n_pairs
        turn = lax.rem(owner, n_pairs) ^ here_turn
        kind = jnp.where(there == here, 0, jnp.where(there // 2 == here // 2, 1, 2))
        bucket = kind * n_pairs + turn
        rank = used[bucket]
        used[bucket] = rank + 1
        slots[bucket * share + rank] = s
    for fetch in fetches:
        fetch.wait()
    lane = lax.broadcasted_iota(jnp.int32, (1, LANES), 1)
    plane = cell_dev * tiles
    for m in range(3 * n_pairs):
        kind, turn = m // n_pairs, m % n_pairs
        out = outs[turn]
        label = jnp.full((1, LANES), -1.0, f32)
        for k in range(share):
            s = slots[m * share + k]
            a = lax.rem(cells[0, s], cell_dev)
            live = s < count[0]
            b = jnp.where(live, lax.rem(cells[1, s], cell_dev), -1)
            table[m * share + k] = jnp.where(live, a, -1)
            label = jnp.where(lane == k, b.astype(f32), label)
            base = row_base(a, tiles)
            for c in range(6):
                source = pos if c < 3 else frc
                for t in range(tiles):
                    row = (k * tiles + t) * 6 + c
                    out[kind, row : row + 1, :] = source[
                        pl.ds(base + (c % 3 * plane + t * 8), 1), :
                    ]
        last = share * 6 * tiles
        out[kind, last : last + 1, :] = label


def pair_kernel(sizes, kind, n, started, table, *refs):
    n_space, n_pairs, share, cell_dev, tiles = sizes
    labels, messages = refs[:n], refs[n : 2 * n]
    pos, frc = refs[2 * n : 2 * n + 2]
    acc, reply, inbox, todo = refs[-4:]
    here = table[3 * n_pairs * share]
    away = jnp.int32(away_of(kind, lax.rem(here, 2)))
    there = lax.rem(here + away + n_space, n_space)
    half = 0.5 * slab_width * away.astype(f32)
    middle_a = slab_width * (there.astype(f32) + 0.5) - half
    middle_b = slab_width * (here.astype(f32) + 0.5) + half
    rows_in = share * 6 * tiles
    plane = cell_dev * tiles
    if started:
        acc[...] = refs[2 * n + 2][...]
    else:
        acc[...] = jnp.zeros_like(acc)
    number = jnp.int32(0)
    first = 0
    for label, message in zip(labels, messages):
        for block in range(message.shape[0]):
            inbox[first * rows_in : (first + 1) * rows_in, :] = message[block, 0:rows_in, :]
            for k in range(share):
                b = label[block, 0, k].astype(jnp.int32)
                todo[0, number] = first * share + k
                todo[1, number] = b
                number = number + jnp.where(b >= 0, 1, 0)
            first += 1

    axis = lax.broadcasted_iota(jnp.int32, (3, 1), 0)
    shift_a = jnp.where(axis == 0, middle_a, across_middle)
    shift_b = jnp.where(axis == 0, middle_b, across_middle)

    def load(i):
        base = todo[0, i] * (6 * tiles)
        data = jnp.concatenate(
            [inbox[pl.ds(base + 6 * t, 6), :] for t in range(tiles)], axis=1
        )
        start = row_base(todo[1, i], tiles)
        xb, fb = (
            jnp.concatenate(
                [
                    jnp.concatenate(
                        [ref[pl.ds(start + (c * plane + t * 8), 1), :] for t in range(tiles)],
                        axis=1,
                    )
                    for c in range(3)
                ],
                axis=0,
            )
            for ref in (pos, frc)
        )
        return data[0:3] - shift_a, data[3:6], xb - shift_b, fb

    def store(i, vel_a, vel_b):
        base = todo[0, i] * (3 * tiles)
        start = row_base(todo[1, i], tiles)
        for t in range(tiles):
            part = slice(t * LANES, (t + 1) * LANES)
            for c in range(3):
                acc[pl.ds(start + (c * plane + t * 8), 1), :] += vel_b[c : c + 1, part]
            reply[pl.ds(base + 3 * t, 3), :] = vel_a[:, part]

    def several(numbers):
        results = pair_velocities([load(i) for i in numbers])
        for i, result in zip(numbers, results):
            store(i, *result)

    def two(i, _):
        several([2 * i, 2 * i + 1])
        return 0

    lax.fori_loop(0, number // 2, two, 0)

    @pl.when(lax.rem(number, 2) == 1)
    def _():
        several([number - 1])


def add_kernel(sizes, table, acc, *refs):
    n_space, n_pairs, share, cell_dev, tiles = sizes
    replies, out = refs[:-1], refs[-1]
    plane = cell_dev * tiles
    out[...] = acc[...]
    for m in range(3 * n_pairs):
        kind, turn = m // n_pairs, m % n_pairs
        for k in range(share):
            a = table[m * share + k]
            live = a >= 0
            base = row_base(jnp.maximum(a, 0), tiles)
            for t in range(tiles):
                for c in range(3):
                    row = (k * tiles + t) * 3 + c
                    term = jnp.where(live, replies[turn][kind, row : row + 1, :], 0.0)
                    out[pl.ds(base + (c * plane + t * 8), 1), :] += term


def flat_rows(cells):
    count, _, points = cells.shape
    value = jnp.transpose(cells, (1, 0, 2)).reshape(3, count // 8, 8, points // LANES, LANES)
    return jnp.transpose(value, (0, 1, 3, 2, 4)).reshape(-1, LANES)


def cell_rows(rows, count, points):
    value = rows.reshape(3, count // 8, points // LANES, 8, LANES)
    value = jnp.transpose(value, (0, 1, 3, 2, 4)).reshape(3, count, points)
    return jnp.transpose(value, (1, 0, 2))


def body(positions, forces, pair_cells, pair_count):
    n_space = lax.axis_size("space")
    n_pairs = lax.axis_size("pairs")
    cell_dev, _, points = positions.shape
    n_slots = pair_cells.shape[1]
    share = n_slots // (3 * n_pairs)
    tiles = points // LANES
    sizes = (n_space, n_pairs, share, cell_dev, tiles)
    rows_in = share * 6 * tiles
    rows_out = share * 3 * tiles
    pos = flat_rows(positions)
    frc = flat_rows(forces)
    vmem = pl.BlockSpec(memory_space=pltpu.VMEM)
    smem = pl.BlockSpec(memory_space=pltpu.SMEM)
    hbm = pl.BlockSpec(memory_space=pltpu.HBM)
    message = jax.ShapeDtypeStruct((3, rows_in + 8, LANES), f32)
    total = jax.ShapeDtypeStruct((3 * cell_dev * tiles, LANES), f32)

    def across(value, turn):
        return lax.ppermute(value, "pairs", [(j, j ^ turn) for j in range(n_pairs)])

    def beyond(value, kind):
        moves = [(i, (i + away_of(kind, i % 2)) % n_space) for i in range(n_space)]
        return lax.ppermute(value, "space", moves)

    packed = pl.pallas_call(
        functools.partial(pack_kernel, sizes),
        out_shape=[message] * n_pairs + [jax.ShapeDtypeStruct((n_slots + 1,), jnp.int32)],
        in_specs=[smem, smem, hbm, hbm],
        out_specs=[vmem] * n_pairs + [smem],
        scratch_shapes=[
            pltpu.SMEM((n_slots,), jnp.int32),
            pltpu.SMEM((3 * n_pairs,), jnp.int32),
            pltpu.VMEM(total.shape, f32),
            pltpu.VMEM(total.shape, f32),
            pltpu.SemaphoreType.DMA((2,)),
        ],
        compiler_params=pltpu.CompilerParams(vmem_limit_bytes=60 * 1024 * 1024),
        name="pack",
    )(pair_cells, pair_count, pos, frc)
    sent, table = packed[:n_pairs], packed[n_pairs]
    got = [sent[0]] + [across(sent[turn], turn) for turn in range(1, n_pairs)]

    def pairs(kind, arrived, before, own=False):
        n = len(arrived)
        blocks = 1 if kind == 0 else n_pairs
        part = kind if kind == 0 else 0
        label = pl.BlockSpec(
            (blocks, 8, LANES), lambda i: (part, rows_in // 8, 0), memory_space=pltpu.SMEM
        )
        data = pl.BlockSpec((blocks, rows_in + 8, LANES), lambda i: (part, 0, 0))
        work = 1 if own else 4
        return pl.pallas_call(
            functools.partial(pair_kernel, sizes, kind, n, len(before) == 1),
            out_shape=[total, jax.ShapeDtypeStruct((n * blocks * rows_out, LANES), f32)],
            grid=(1,),
            in_specs=[smem] + [label] * n + [data] * n + [vmem] * (2 + len(before)),
            out_specs=[vmem] * 2,
            scratch_shapes=[
                pltpu.VMEM((n * blocks * rows_in, LANES), f32),
                pltpu.SMEM((2, n * blocks * share + 1), jnp.int32),
            ],
            compiler_params=pltpu.CompilerParams(vmem_limit_bytes=48 * 1024 * 1024),
            cost_estimate=pl.CostEstimate(
                flops=work * 1_000_000_000, bytes_accessed=2_000_000, transcendentals=2_000_000
            ),
            name="pairs",
        )(table, *arrived, *arrived, pos, frc, *before)

    acc, reply_own = pairs(0, got[:1], [], True)
    out_1 = beyond(jnp.stack([value[1] for value in got]), 1)
    out_2 = beyond(jnp.stack([value[2] for value in got]), 2)
    acc, reply_0 = pairs(0, got[1:], [acc])
    acc, reply_1 = pairs(1, [out_1], [acc])
    back_1 = beyond(reply_1, 1)
    acc, reply_2 = pairs(2, [out_2], [acc])
    back_2 = beyond(reply_2, 2)
    back_0 = jnp.concatenate([reply_own, reply_0], axis=0)
    shape = (n_pairs, rows_out, LANES)
    back_0, back_1, back_2 = (value.reshape(shape) for value in (back_0, back_1, back_2))
    back = []
    for turn in range(n_pairs):
        value = jnp.stack([back_0[turn], back_1[turn], back_2[turn]])
        back.append(across(value, turn) if turn else value)
    velocity = pl.pallas_call(
        functools.partial(add_kernel, sizes),
        out_shape=total,
        in_specs=[smem] + [vmem] * (1 + n_pairs),
        out_specs=vmem,
        compiler_params=pltpu.CompilerParams(vmem_limit_bytes=48 * 1024 * 1024),
        name="add",
    )(table, acc, *back)
    return cell_rows(velocity, cell_dev, points)


def solution(mesh):
    placed = (
        P(("space", "pairs"), None, None),
        P(("space", "pairs"), None, None),
        P(None, ("space", "pairs")),
        P(("space", "pairs")),
    )
    return jax.shard_map(
        body,
        mesh=mesh,
        in_specs=placed,
        out_specs=P(("space", "pairs"), None, None),
        check_vma=False,
    )
```

```python
import functools
import math

import jax
import jax.numpy as jnp
from jax import lax
from jax.experimental import pallas as pl
from jax.experimental.pallas import tpu as pltpu
from jax.sharding import PartitionSpec as P

stokes_coef = 1.0 / (8.0 * math.pi)
eps_sq = 0.01
slab_width = 3.0
across_middle = 1.0
LANES = 128
FEATURES = 16

f32 = jnp.float32
bf16 = jnp.bfloat16


def split(value, terms):
    parts = []
    for _ in range(terms - 1):
        part = value.astype(bf16).astype(f32)
        parts.append(part)
        value = value - part
    parts.append(value)
    return parts


def features(x, f):
    norm = jnp.sum(x * x, axis=0, keepdims=True)
    along = jnp.sum(x * f, axis=0, keepdims=True)
    rows = [f] + [x[k : k + 1] * f for k in range(3)] + [norm * f + x * along]
    rows.append(jnp.zeros_like(norm))
    stacked = jnp.concatenate(rows, axis=0)
    return jnp.concatenate([part.astype(bf16) for part in split(stacked, 3)], axis=0)


def combine(sums, y):
    force = sums[0:3]
    moment = [sums[3 + 3 * k : 6 + 3 * k] for k in range(3)]
    second = sums[12:15]
    norm = jnp.sum(y * y, axis=0, keepdims=True)
    trace = moment[0][0:1] + moment[1][1:2] + moment[2][2:3]
    along = jnp.sum(y * force, axis=0, keepdims=True) - trace
    turned = jnp.concatenate(
        [jnp.sum(y * moment[k], axis=0, keepdims=True) for k in range(3)], axis=0
    )
    mixed = y[0:1] * moment[0] + y[1:2] * moment[1] + y[2:3] * moment[2]
    velocity = (norm + 2.0 * eps_sq) * force + second - 2.0 * mixed + y * along - turned
    return velocity * stokes_coef


def gram_factors(x, y):
    one = jnp.ones((1, x.shape[1]), f32)
    none = jnp.zeros((3, x.shape[1]), f32)
    norm_x = jnp.sum(x * x, axis=0, keepdims=True)
    norm_y = jnp.sum(y * y, axis=0, keepdims=True) + eps_sq
    left = split(jnp.concatenate([x, norm_x, one, none], axis=0), 3)
    right = split(jnp.concatenate([-2.0 * y, one, norm_y, none], axis=0), 3)
    order = ((0, 0), (0, 1), (1, 0), (0, 2), (1, 1), (2, 0))
    return (
        jnp.concatenate([left[p] for p, _ in order], axis=0).astype(bf16),
        jnp.concatenate([right[q] for _, q in order], axis=0).astype(bf16),
    )


def dot(left, right, left_dim, right_dim):
    return lax.dot_general(
        left, right, (((left_dim,), (right_dim,)), ((), ())), preferred_element_type=f32
    )


def fold(high, low):
    return (
        high[0:FEATURES]
        + high[FEATURES : 2 * FEATURES]
        + high[2 * FEATURES :]
        + low[0:FEATURES]
        + low[FEATURES:]
    )


def weights(factors):
    dist_sq = dot(*factors, 0, 0)
    inverse = lax.rsqrt(dist_sq)
    cubed = inverse * inverse * inverse
    high = cubed.astype(bf16)
    return high, (cubed - high.astype(f32)).astype(bf16)


def pair_velocities(cells):
    two = 2 * FEATURES
    factors = [gram_factors(xa, xb) for xa, _, xb, _ in cells]
    feats = [(features(xa, fa), features(xb, fb)) for xa, fa, xb, fb in cells]
    sums = []
    for factor, (feat_a, feat_b) in zip(factors, feats):
        high, low = weights(factor)
        sums_b = fold(dot(feat_a, high, 1, 0), dot(feat_a[:two], low, 1, 0))
        sums_a = fold(dot(feat_b, high, 1, 1), dot(feat_b[:two], low, 1, 1))
        sums.append((sums_a, sums_b))
    return [
        (combine(sums_a, xa), combine(sums_b, xb))
        for (sums_a, sums_b), (xa, _, xb, _) in zip(sums, cells)
    ]


def row_base(cell, tiles):
    return cell // 8 * (8 * tiles) + lax.rem(cell, 8)


def away_of(kind, odd):
    return (0, 1 - 2 * odd, 2 * odd - 1)[kind]


def pack_kernel(sizes, cells, count, pos_hbm, frc_hbm, *refs):
    n_space, n_pairs, share, cell_dev, tiles = sizes
    outs, table = refs[:n_pairs], refs[n_pairs]
    slots, used, pos, frc, sems = refs[n_pairs + 1 :]
    fetches = [
        pltpu.make_async_copy(pos_hbm, pos, sems.at[0]),
        pltpu.make_async_copy(frc_hbm, frc, sems.at[1]),
    ]
    for fetch in fetches:
        fetch.start()
    n_slots = cells.shape[1]
    owner = cells[0, 0] // cell_dev
    here = owner // n_pairs
    here_turn = lax.rem(owner, n_pairs)
    table[n_slots] = here
    for bucket in range(3 * n_pairs):
        used[bucket] = 0
    for s in range(n_slots):
        owner = cells[1, s] // cell_dev
        there = owner // n_pairs
        turn = lax.rem(owner, n_pairs) ^ here_turn
        kind = jnp.where(there == here, 0, jnp.where(there // 2 == here // 2, 1, 2))
        bucket = kind * n_pairs + turn
        rank = used[bucket]
        used[bucket] = rank + 1
        slots[bucket * share + rank] = s
    for fetch in fetches:
        fetch.wait()
    lane = lax.broadcasted_iota(jnp.int32, (1, LANES), 1)
    plane = cell_dev * tiles
    for m in range(3 * n_pairs):
        kind, turn = m // n_pairs, m % n_pairs
        out = outs[turn]
        label = jnp.full((1, LANES), -1.0, f32)
        for k in range(share):
            s = slots[m * share + k]
            a = lax.rem(cells[0, s], cell_dev)
            live = s < count[0]
            b = jnp.where(live, lax.rem(cells[1, s], cell_dev), -1)
            table[m * share + k] = jnp.where(live, a, -1)
            label = jnp.where(lane == k, b.astype(f32), label)
            base = row_base(a, tiles)
            for c in range(6):
                source = pos if c < 3 else frc
                for t in range(tiles):
                    row = (k * tiles + t) * 6 + c
                    out[kind, row : row + 1, :] = source[
                        pl.ds(base + (c % 3 * plane + t * 8), 1), :
                    ]
        last = share * 6 * tiles
        out[kind, last : last + 1, :] = label


def pair_kernel(sizes, kinds, started, table, *refs):
    n_space, n_pairs, share, cell_dev, tiles = sizes
    n = len(kinds)
    labels, messages = refs[:n], refs[n : 2 * n]
    pos, frc = refs[2 * n : 2 * n + 2]
    outs = refs[2 * n + 2 + started :]
    (acc, reply), (inbox, todo, middles) = outs[:2], outs[-3:]
    if not started:
        outs[2][...] = jnp.zeros_like(outs[2])
    here = table[3 * n_pairs * share]
    rows_in = share * 6 * tiles
    plane = cell_dev * tiles
    if started:
        acc[...] = refs[2 * n + 2][...]
    else:
        acc[...] = jnp.zeros_like(acc)
    number = jnp.int32(0)
    first = 0
    for kind, label, message in zip(kinds, labels, messages):
        away = jnp.int32(away_of(kind, lax.rem(here, 2)))
        there = lax.rem(here + away + n_space, n_space)
        half = 0.5 * slab_width * away.astype(f32)
        middle_a = slab_width * (there.astype(f32) + 0.5) - half
        middle_b = slab_width * (here.astype(f32) + 0.5) + half
        for block in range(message.shape[0]):
            inbox[first * rows_in : (first + 1) * rows_in, :] = message[block, 0:rows_in, :]
            for k in range(share):
                b = label[block, 0, k].astype(jnp.int32)
                todo[0, number] = first * share + k
                todo[1, number] = b
                middles[0, number] = middle_a
                middles[1, number] = middle_b
                number = number + jnp.where(b >= 0, 1, 0)
            first += 1

    axis = lax.broadcasted_iota(jnp.int32, (3, 1), 0)

    def load(i):
        base = todo[0, i] * (6 * tiles)
        data = jnp.concatenate(
            [inbox[pl.ds(base + 6 * t, 6), :] for t in range(tiles)], axis=1
        )
        start = row_base(todo[1, i], tiles)
        xb, fb = (
            jnp.concatenate(
                [
                    jnp.concatenate(
                        [ref[pl.ds(start + (c * plane + t * 8), 1), :] for t in range(tiles)],
                        axis=1,
                    )
                    for c in range(3)
                ],
                axis=0,
            )
            for ref in (pos, frc)
        )
        xa = data[0:3] - jnp.where(axis == 0, middles[0, i], across_middle)
        xb = xb - jnp.where(axis == 0, middles[1, i], across_middle)
        return xa, data[3:6], xb, fb

    def store(i, vel_a, vel_b):
        base = todo[0, i] * (3 * tiles)
        start = row_base(todo[1, i], tiles)
        for t in range(tiles):
            part = slice(t * LANES, (t + 1) * LANES)
            for c in range(3):
                acc[pl.ds(start + (c * plane + t * 8), 1), :] += vel_b[c : c + 1, part]
            reply[pl.ds(base + 3 * t, 3), :] = vel_a[:, part]

    def several(numbers):
        results = pair_velocities([load(i) for i in numbers])
        for i, result in zip(numbers, results):
            store(i, *result)

    def two(i, _):
        several([2 * i, 2 * i + 1])
        return 0

    lax.fori_loop(0, number // 2, two, 0)

    @pl.when(lax.rem(number, 2) == 1)
    def _():
        several([number - 1])


def add_kernel(sizes, table, acc, *refs):
    n_space, n_pairs, share, cell_dev, tiles = sizes
    replies, out = refs[:-1], refs[-1]
    plane = cell_dev * tiles
    out[...] = acc[...]
    for m in range(3 * n_pairs):
        kind, turn = m // n_pairs, m % n_pairs
        for k in range(share):
            a = table[m * share + k]
            live = a >= 0
            base = row_base(jnp.maximum(a, 0), tiles)
            for t in range(tiles):
                for c in range(3):
                    row = (k * tiles + t) * 3 + c
                    term = jnp.where(live, replies[turn][kind, row : row + 1, :], 0.0)
                    out[pl.ds(base + (c * plane + t * 8), 1), :] += term


def flat_rows(cells):
    count, _, points = cells.shape
    value = jnp.transpose(cells, (1, 0, 2)).reshape(3, count // 8, 8, points // LANES, LANES)
    return jnp.transpose(value, (0, 1, 3, 2, 4)).reshape(-1, LANES)


def cell_rows(rows, count, points):
    value = rows.reshape(3, count // 8, points // LANES, 8, LANES)
    value = jnp.transpose(value, (0, 1, 3, 2, 4)).reshape(3, count, points)
    return jnp.transpose(value, (1, 0, 2))


def body(positions, forces, pair_cells, pair_count):
    n_space = lax.axis_size("space")
    n_pairs = lax.axis_size("pairs")
    cell_dev, _, points = positions.shape
    n_slots = pair_cells.shape[1]
    share = n_slots // (3 * n_pairs)
    tiles = points // LANES
    sizes = (n_space, n_pairs, share, cell_dev, tiles)
    rows_in = share * 6 * tiles
    rows_out = share * 3 * tiles
    pos = flat_rows(positions)
    frc = flat_rows(forces)
    vmem = pl.BlockSpec(memory_space=pltpu.VMEM)
    smem = pl.BlockSpec(memory_space=pltpu.SMEM)
    hbm = pl.BlockSpec(memory_space=pltpu.HBM)
    message = jax.ShapeDtypeStruct((3, rows_in + 8, LANES), f32)
    total = jax.ShapeDtypeStruct((3 * cell_dev * tiles, LANES), f32)

    def across(value, turn):
        return lax.ppermute(value, "pairs", [(j, j ^ turn) for j in range(n_pairs)])

    def beyond(value, kind):
        moves = [(i, (i + away_of(kind, i % 2)) % n_space) for i in range(n_space)]
        return lax.ppermute(value, "space", moves)

    packed = pl.pallas_call(
        functools.partial(pack_kernel, sizes),
        out_shape=[message] * n_pairs + [jax.ShapeDtypeStruct((n_slots + 1,), jnp.int32)],
        in_specs=[smem, smem, hbm, hbm],
        out_specs=[vmem] * n_pairs + [smem],
        scratch_shapes=[
            pltpu.SMEM((n_slots,), jnp.int32),
            pltpu.SMEM((3 * n_pairs,), jnp.int32),
            pltpu.VMEM(total.shape, f32),
            pltpu.VMEM(total.shape, f32),
            pltpu.SemaphoreType.DMA((2,)),
        ],
        compiler_params=pltpu.CompilerParams(vmem_limit_bytes=60 * 1024 * 1024),
        name="pack",
    )(pair_cells, pair_count, pos, frc)
    sent, table = packed[:n_pairs], packed[n_pairs]
    got = [sent[0]] + [across(sent[turn], turn) for turn in range(1, n_pairs)]

    def pairs(arrived, before):
        kinds, values, labels, data = [], [], [], []
        for kind, value, whole in arrived:
            blocks = value.shape[0] if whole else 1
            part = 0 if whole else kind
            kinds += [kind]
            values += [value]
            labels.append(
                pl.BlockSpec(
                    (blocks, 8, LANES),
                    functools.partial(lambda part, i: (part, rows_in // 8, 0), part),
                    memory_space=pltpu.SMEM,
                )
            )
            data.append(
                pl.BlockSpec(
                    (blocks, rows_in + 8, LANES),
                    functools.partial(lambda part, i: (part, 0, 0), part),
                )
            )
        total_blocks = sum(spec.block_shape[0] for spec in data)
        return pl.pallas_call(
            functools.partial(pair_kernel, sizes, kinds, len(before) == 1),
            out_shape=[total, jax.ShapeDtypeStruct((total_blocks * rows_out, LANES), f32)]
            + [jax.ShapeDtypeStruct((1, LANES), f32)] * (not before),
            grid=(1,),
            in_specs=[smem] + labels + data + [vmem] * (2 + len(before)),
            out_specs=[vmem] * (2 + (not before)),
            scratch_shapes=[
                pltpu.VMEM((total_blocks * rows_in, LANES), f32),
                pltpu.SMEM((2, total_blocks * share + 1), jnp.int32),
                pltpu.SMEM((2, total_blocks * share + 1), f32),
            ],
            compiler_params=pltpu.CompilerParams(vmem_limit_bytes=48 * 1024 * 1024),
            cost_estimate=pl.CostEstimate(
                flops=total_blocks * 1_000_000_000, bytes_accessed=2_000_000, transcendentals=2_000_000
            ),
            name="pairs",
        )(table, *values, *values, pos, frc, *before)

    near, far = range(2), range(2, n_pairs)
    acc, reply_0n, nothing = pairs([(0, got[turn], False) for turn in near], [])
    ready = got[:2] + [value + nothing[None] for value in got[2:]]
    out = {
        (kind, group): beyond(jnp.stack([ready[turn][kind] for turn in group]), kind)
        for group in (near, far)
        for kind in (1, 2)
    }
    acc, reply_1n = pairs([(1, out[1, near], True)], [acc])
    acc, reply_m = pairs([(0, got[turn], False) for turn in far] + [(2, out[2, near], True)], [acc])
    acc, reply_f = pairs([(1, out[1, far], True), (2, out[2, far], True)], [acc])
    reply_0n, reply_1n, reply_m, reply_f = (
        value.reshape(-1, rows_out, LANES) for value in (reply_0n, reply_1n, reply_m, reply_f)
    )
    cut = n_pairs - 2
    back_0 = jnp.concatenate([reply_0n, reply_m[:cut]])
    back_1 = beyond(jnp.concatenate([reply_1n, reply_f[:cut]]), 1)
    back_2 = beyond(jnp.concatenate([reply_m[cut:], reply_f[cut:]]), 2)
    back = []
    for turn in range(n_pairs):
        value = jnp.stack([back_0[turn], back_1[turn], back_2[turn]])
        back.append(across(value, turn) if turn else value)
    velocity = pl.pallas_call(
        functools.partial(add_kernel, sizes),
        out_shape=total,
        in_specs=[smem] + [vmem] * (1 + n_pairs),
        out_specs=vmem,
        compiler_params=pltpu.CompilerParams(vmem_limit_bytes=48 * 1024 * 1024),
        name="add",
    )(table, acc, *back)
    return cell_rows(velocity, cell_dev, points)


def solution(mesh):
    placed = (
        P(("space", "pairs"), None, None),
        P(("space", "pairs"), None, None),
        P(None, ("space", "pairs")),
        P(("space", "pairs")),
    )
    return jax.shard_map(
        body,
        mesh=mesh,
        in_specs=placed,
        out_specs=P(("space", "pairs"), None, None),
        check_vma=False,
    )
```

```python
import functools
import math

import jax
import jax.numpy as jnp
from jax import lax
from jax.experimental import pallas as pl
from jax.experimental.pallas import tpu as pltpu
from jax.sharding import PartitionSpec as P

stokes_coef = 1.0 / (8.0 * math.pi)
eps_sq = 0.01
slab_width = 3.0
across_middle = 1.0
LANES = 128
FEATURES = 16

f32 = jnp.float32
bf16 = jnp.bfloat16


def split(value, terms):
    parts = []
    for _ in range(terms - 1):
        part = value.astype(bf16).astype(f32)
        parts.append(part)
        value = value - part
    parts.append(value)
    return parts


def features(x, f):
    norm = jnp.sum(x * x, axis=0, keepdims=True)
    along = jnp.sum(x * f, axis=0, keepdims=True)
    rows = [f] + [x[k : k + 1] * f for k in range(3)] + [norm * f + x * along]
    rows.append(jnp.zeros_like(norm))
    stacked = jnp.concatenate(rows, axis=0)
    return jnp.concatenate([part.astype(bf16) for part in split(stacked, 3)], axis=0)


def combine(sums, y):
    force = sums[0:3]
    moment = [sums[3 + 3 * k : 6 + 3 * k] for k in range(3)]
    second = sums[12:15]
    norm = jnp.sum(y * y, axis=0, keepdims=True)
    trace = moment[0][0:1] + moment[1][1:2] + moment[2][2:3]
    along = jnp.sum(y * force, axis=0, keepdims=True) - trace
    turned = jnp.concatenate(
        [jnp.sum(y * moment[k], axis=0, keepdims=True) for k in range(3)], axis=0
    )
    mixed = y[0:1] * moment[0] + y[1:2] * moment[1] + y[2:3] * moment[2]
    velocity = (norm + 2.0 * eps_sq) * force + second - 2.0 * mixed + y * along - turned
    return velocity * stokes_coef


def gram_factors(x, y):
    one = jnp.ones((1, x.shape[1]), f32)
    none = jnp.zeros((3, x.shape[1]), f32)
    norm_x = jnp.sum(x * x, axis=0, keepdims=True)
    norm_y = jnp.sum(y * y, axis=0, keepdims=True) + eps_sq
    left = split(jnp.concatenate([x, norm_x, one, none], axis=0), 3)
    right = split(jnp.concatenate([-2.0 * y, one, norm_y, none], axis=0), 3)
    order = ((0, 0), (0, 1), (1, 0), (0, 2), (1, 1), (2, 0))
    return (
        jnp.concatenate([left[p] for p, _ in order], axis=0).astype(bf16),
        jnp.concatenate([right[q] for _, q in order], axis=0).astype(bf16),
    )


def dot(left, right, left_dim, right_dim):
    return lax.dot_general(
        left, right, (((left_dim,), (right_dim,)), ((), ())), preferred_element_type=f32
    )


def fold(sums):
    return sums[0:FEATURES] + sums[FEATURES : 2 * FEATURES] + sums[2 * FEATURES :]


def weights(dist_sq):
    inverse = lax.rsqrt(dist_sq)
    cubed = inverse * inverse * inverse
    high = cubed.astype(bf16)
    low = (cubed - high.astype(f32)).astype(bf16)
    return high, low


def pair_velocities(cells):
    grams = [dot(*gram_factors(xa, xb), 0, 0) for xa, _, xb, _ in cells]
    feats = [(features(xa, fa), features(xb, fb)) for xa, fa, xb, fb in cells]
    sums = []
    for gram, (feat_a, feat_b) in zip(grams, feats):
        high, low = weights(gram)
        sums_b = fold(
            dot(
                jnp.concatenate([feat_a, feat_a], axis=1),
                jnp.concatenate([high, low], axis=0),
                1,
                0,
            )
        )
        sums_a = fold(
            dot(
                jnp.concatenate([feat_b, feat_b], axis=1),
                jnp.concatenate([high, low], axis=1),
                1,
                1,
            )
        )
        sums.append((sums_a, sums_b))
    return [
        (combine(sums_a, xa), combine(sums_b, xb))
        for (sums_a, sums_b), (xa, _, xb, _) in zip(sums, cells)
    ]


def row_base(cell, tiles):
    return cell // 8 * (8 * tiles) + lax.rem(cell, 8)


def away_of(kind, odd):
    return (0, 1 - 2 * odd, 2 * odd - 1)[kind]


def pack_kernel(sizes, cells, count, pos_hbm, frc_hbm, *refs):
    n_space, n_pairs, share, cell_dev, tiles = sizes
    outs, table = refs[:n_pairs], refs[n_pairs]
    slots, used, pos, frc, sems = refs[n_pairs + 1 :]
    fetches = [
        pltpu.make_async_copy(pos_hbm, pos, sems.at[0]),
        pltpu.make_async_copy(frc_hbm, frc, sems.at[1]),
    ]
    for fetch in fetches:
        fetch.start()
    n_slots = cells.shape[1]
    owner = cells[0, 0] // cell_dev
    here = owner // n_pairs
    here_turn = lax.rem(owner, n_pairs)
    table[n_slots] = here
    for bucket in range(3 * n_pairs):
        used[bucket] = 0
    for s in range(n_slots):
        owner = cells[1, s] // cell_dev
        there = owner // n_pairs
        turn = lax.rem(owner, n_pairs) ^ here_turn
        kind = jnp.where(there == here, 0, jnp.where(there // 2 == here // 2, 1, 2))
        bucket = kind * n_pairs + turn
        rank = used[bucket]
        used[bucket] = rank + 1
        slots[bucket * share + rank] = s
    for fetch in fetches:
        fetch.wait()
    lane = lax.broadcasted_iota(jnp.int32, (1, LANES), 1)
    plane = cell_dev * tiles
    for m in range(3 * n_pairs):
        kind, turn = m // n_pairs, m % n_pairs
        out = outs[turn]
        label = jnp.full((1, LANES), -1.0, f32)
        for k in range(share):
            s = slots[m * share + k]
            a = lax.rem(cells[0, s], cell_dev)
            live = s < count[0]
            b = jnp.where(live, lax.rem(cells[1, s], cell_dev), -1)
            table[m * share + k] = jnp.where(live, a, -1)
            label = jnp.where(lane == k, b.astype(f32), label)
            base = row_base(a, tiles)
            for c in range(6):
                source = pos if c < 3 else frc
                row = (k * 6 + c) * tiles
                out[kind, row : row + tiles, :] = source[
                    pl.ds(base + c % 3 * plane, tiles, stride=8), :
                ]
        last = share * 6 * tiles
        out[kind, last : last + 1, :] = label


def pair_kernel(sizes, kinds, started, table, *refs):
    n_space, n_pairs, share, cell_dev, tiles = sizes
    n = len(kinds)
    messages, (pos, frc) = refs[:n], refs[n : n + 2]
    outs = refs[n + 2 + started :]
    (acc, reply), (inbox, todo, middles, labels, sems) = outs[:2], outs[-5:]
    rows_in = share * 6 * tiles
    plane = cell_dev * tiles
    fetches = []
    first = 0
    for message in messages:
        blocks = message.shape[0]
        fetch = pltpu.make_async_copy(
            message.at[:, pl.ds(rows_in, 8), :],
            labels.at[pl.ds(first, blocks)],
            sems.at[len(fetches)],
        )
        fetch.start()
        fetches.append(fetch)
        for block in range(blocks):
            inbox[first * rows_in : (first + 1) * rows_in, :] = message[block, 0:rows_in, :]
            first += 1
    if not started:
        acc[...] = jnp.zeros_like(acc)
        outs[2][...] = jnp.zeros_like(outs[2])
    for fetch in fetches:
        fetch.wait()
    here = table[3 * n_pairs * share]
    number = jnp.int32(0)
    first = 0
    for kind, message in zip(kinds, messages):
        away = jnp.int32(away_of(kind, lax.rem(here, 2)))
        there = lax.rem(here + away + n_space, n_space)
        half = 0.5 * slab_width * away.astype(f32)
        middle_a = slab_width * (there.astype(f32) + 0.5) - half
        middle_b = slab_width * (here.astype(f32) + 0.5) + half
        for _ in range(message.shape[0]):
            for k in range(share):
                b = labels[first, 0, k].astype(jnp.int32)
                todo[0, number] = first * share + k
                todo[1, number] = b
                middles[0, number] = middle_a
                middles[1, number] = middle_b
                number = number + jnp.where(b >= 0, 1, 0)
            first += 1

    axis = lax.broadcasted_iota(jnp.int32, (3, 1), 0)

    def load(i):
        base = todo[0, i] * (6 * tiles)
        data = jnp.concatenate(
            [inbox[pl.ds(base + t, 6, stride=tiles), :] for t in range(tiles)], axis=1
        )
        start = row_base(todo[1, i], tiles)
        xb, fb = (
            jnp.concatenate(
                [ref[pl.ds(start + 8 * t, 3, stride=plane), :] for t in range(tiles)], axis=1
            )
            for ref in (pos, frc)
        )
        xa = data[0:3] - jnp.where(axis == 0, middles[0, i], across_middle)
        xb = xb - jnp.where(axis == 0, middles[1, i], across_middle)
        return xa, data[3:6], xb, fb

    def store(i, vel_a, vel_b):
        base = todo[0, i] * (3 * tiles)
        start = row_base(todo[1, i], tiles)
        for t in range(tiles):
            part = slice(t * LANES, (t + 1) * LANES)
            acc[pl.ds(start + 8 * t, 3, stride=plane), :] += vel_b[:, part]
            reply[pl.ds(base + 3 * t, 3), :] = vel_a[:, part]

    def several(numbers):
        results = pair_velocities([load(i) for i in numbers])
        for i, result in zip(numbers, results):
            store(i, *result)

    def two(i, _):
        several([2 * i, 2 * i + 1])
        return 0

    lax.fori_loop(0, number // 2, two, 0)

    @pl.when(lax.rem(number, 2) == 1)
    def _():
        several([number - 1])


def add_kernel(sizes, table, acc, *refs):
    n_space, n_pairs, share, cell_dev, tiles = sizes
    replies, out = refs[:-1], refs[-1]
    plane = cell_dev * tiles
    out[...] = acc[...]
    for m in range(3 * n_pairs):
        kind, turn = m // n_pairs, m % n_pairs
        for k in range(share):
            a = table[m * share + k]
            live = a >= 0
            base = row_base(jnp.maximum(a, 0), tiles)
            for t in range(tiles):
                row = (k * tiles + t) * 3
                term = jnp.where(live, replies[turn][kind, row : row + 3, :], 0.0)
                out[pl.ds(base + 8 * t, 3, stride=plane), :] += term


def flat_rows(cells):
    count, _, points = cells.shape
    value = jnp.transpose(cells, (1, 0, 2)).reshape(3, count // 8, 8, points // LANES, LANES)
    return jnp.transpose(value, (0, 1, 3, 2, 4)).reshape(-1, LANES)


def cell_rows(rows, count, points):
    value = rows.reshape(3, count // 8, points // LANES, 8, LANES)
    value = jnp.transpose(value, (0, 1, 3, 2, 4)).reshape(3, count, points)
    return jnp.transpose(value, (1, 0, 2))


def body(positions, forces, pair_cells, pair_count):
    n_space = lax.axis_size("space")
    n_pairs = lax.axis_size("pairs")
    cell_dev, _, points = positions.shape
    n_slots = pair_cells.shape[1]
    share = n_slots // (3 * n_pairs)
    tiles = points // LANES
    sizes = (n_space, n_pairs, share, cell_dev, tiles)
    rows_in = share * 6 * tiles
    rows_out = share * 3 * tiles
    pos = flat_rows(positions)
    frc = flat_rows(forces)
    vmem = pl.BlockSpec(memory_space=pltpu.VMEM)
    smem = pl.BlockSpec(memory_space=pltpu.SMEM)
    hbm = pl.BlockSpec(memory_space=pltpu.HBM)
    message = jax.ShapeDtypeStruct((3, rows_in + 8, LANES), f32)
    total = jax.ShapeDtypeStruct((3 * cell_dev * tiles, LANES), f32)

    def across(value, turn):
        return lax.ppermute(value, "pairs", [(j, j ^ turn) for j in range(n_pairs)])

    def beyond(value, kind):
        moves = [(i, (i + away_of(kind, i % 2)) % n_space) for i in range(n_space)]
        return lax.ppermute(value, "space", moves)

    packed = pl.pallas_call(
        functools.partial(pack_kernel, sizes),
        out_shape=[message] * n_pairs + [jax.ShapeDtypeStruct((n_slots + 1,), jnp.int32)],
        in_specs=[smem, smem, hbm, hbm],
        out_specs=[vmem] * n_pairs + [smem],
        scratch_shapes=[
            pltpu.SMEM((n_slots,), jnp.int32),
            pltpu.SMEM((3 * n_pairs,), jnp.int32),
            pltpu.VMEM(total.shape, f32),
            pltpu.VMEM(total.shape, f32),
            pltpu.SemaphoreType.DMA((2,)),
        ],
        compiler_params=pltpu.CompilerParams(vmem_limit_bytes=60 * 1024 * 1024),
        name="pack",
    )(pair_cells, pair_count, pos, frc)
    sent, table = packed[:n_pairs], packed[n_pairs]
    got = [sent[0]] + [across(sent[turn], turn) for turn in range(1, n_pairs)]

    def pairs(arrived, before):
        kinds = [kind for kind, _ in arrived]
        values = [value for _, value in arrived]
        n = len(values)
        blocks = sum(value.shape[0] for value in values)
        return pl.pallas_call(
            functools.partial(pair_kernel, sizes, kinds, len(before)),
            out_shape=[total, jax.ShapeDtypeStruct((blocks * rows_out, LANES), f32)]
            + [jax.ShapeDtypeStruct((1, LANES), f32)] * (not before),
            in_specs=[smem] + [vmem] * (n + 2 + len(before)),
            out_specs=[vmem] * (2 + (not before)),
            scratch_shapes=[
                pltpu.VMEM((blocks * rows_in, LANES), f32),
                pltpu.SMEM((2, blocks * share + 1), jnp.int32),
                pltpu.SMEM((2, blocks * share + 1), f32),
                pltpu.SMEM((blocks, 8, LANES), f32),
                pltpu.SemaphoreType.DMA((n,)),
            ],
            input_output_aliases={n + 3: 0} if before else {},
            compiler_params=pltpu.CompilerParams(vmem_limit_bytes=48 * 1024 * 1024),
            cost_estimate=pl.CostEstimate(
                flops=blocks * 1_000_000_000, bytes_accessed=2_000_000, transcendentals=2_000_000
            ),
            name="pairs",
        )(table, *values, pos, frc, *before)

    near, far = range(2), range(2, n_pairs)
    own = [sent[0][kind : kind + 1] for kind in range(3)]
    core = [got[1][kind : kind + 1] for kind in range(3)]
    out_1n = beyond(jnp.concatenate([own[1], core[1]]), 1)
    acc, reply_0n, nothing = pairs([(0, own[0]), (0, core[0])], [])
    rest = [got[turn] + nothing[None] for turn in far]
    out_1f = beyond(jnp.stack([value[1] for value in rest]), 1)
    out_2 = beyond(jnp.concatenate([own[2], core[2]] + [value[2:] for value in rest]), 2)
    acc, reply_m = pairs([(1, out_1n)] + [(0, got[turn][0:1]) for turn in far], [acc])
    acc, reply_f = pairs([(1, out_1f), (2, out_2)], [acc])
    reply_0n, reply_m, reply_f = (
        value.reshape(-1, rows_out, LANES) for value in (reply_0n, reply_m, reply_f)
    )
    cut = n_pairs - 2
    back_0 = jnp.concatenate([reply_0n, reply_m[2:]])
    back_1 = beyond(jnp.concatenate([reply_m[:2], reply_f[:cut]]), 1)
    back_2 = beyond(reply_f[cut:], 2)
    back = []
    for turn in range(n_pairs):
        value = jnp.stack([back_0[turn], back_1[turn], back_2[turn]])
        back.append(across(value, turn) if turn else value)
    velocity = pl.pallas_call(
        functools.partial(add_kernel, sizes),
        out_shape=total,
        in_specs=[smem] + [vmem] * (1 + n_pairs),
        out_specs=vmem,
        compiler_params=pltpu.CompilerParams(vmem_limit_bytes=48 * 1024 * 1024),
        name="add",
    )(table, acc, *back)
    return cell_rows(velocity, cell_dev, points)


def solution(mesh):
    placed = (
        P(("space", "pairs"), None, None),
        P(("space", "pairs"), None, None),
        P(None, ("space", "pairs")),
        P(("space", "pairs")),
    )
    return jax.shard_map(
        body,
        mesh=mesh,
        in_specs=placed,
        out_specs=P(("space", "pairs"), None, None),
        check_vma=False,
    )
```

```python
import functools
import math

import jax
import jax.numpy as jnp
from jax import lax
from jax.experimental import pallas as pl
from jax.experimental.pallas import tpu as pltpu
from jax.sharding import PartitionSpec as P

stokes_coef = 1.0 / (8.0 * math.pi)
eps_sq = 0.01
slab_width = 3.0
across_middle = 1.0
LANES = 128
FEATURES = 16

f32 = jnp.float32
bf16 = jnp.bfloat16


def split(value, terms):
    parts = []
    for _ in range(terms - 1):
        part = value.astype(bf16).astype(f32)
        parts.append(part)
        value = value - part
    parts.append(value)
    return parts


def features(x, f):
    norm = jnp.sum(x * x, axis=0, keepdims=True)
    along = jnp.sum(x * f, axis=0, keepdims=True)
    rows = [f] + [x[k : k + 1] * f for k in range(3)] + [norm * f + x * along]
    rows.append(jnp.zeros_like(norm))
    stacked = jnp.concatenate(rows, axis=0)
    return jnp.concatenate([part.astype(bf16) for part in split(stacked, 3)], axis=0)


def combine(sums, y):
    force = sums[0:3]
    moment = [sums[3 + 3 * k : 6 + 3 * k] for k in range(3)]
    second = sums[12:15]
    norm = jnp.sum(y * y, axis=0, keepdims=True)
    trace = moment[0][0:1] + moment[1][1:2] + moment[2][2:3]
    along = jnp.sum(y * force, axis=0, keepdims=True) - trace
    turned = jnp.concatenate(
        [jnp.sum(y * moment[k], axis=0, keepdims=True) for k in range(3)], axis=0
    )
    mixed = y[0:1] * moment[0] + y[1:2] * moment[1] + y[2:3] * moment[2]
    velocity = (norm + 2.0 * eps_sq) * force + second - 2.0 * mixed + y * along - turned
    return velocity * stokes_coef


def gram_factors(x, y):
    one = jnp.ones((1, x.shape[1]), f32)
    none = jnp.zeros((3, x.shape[1]), f32)
    norm_x = jnp.sum(x * x, axis=0, keepdims=True)
    norm_y = jnp.sum(y * y, axis=0, keepdims=True) + eps_sq
    left = split(jnp.concatenate([x, norm_x, one, none], axis=0), 3)
    right = split(jnp.concatenate([-2.0 * y, one, norm_y, none], axis=0), 3)
    order = ((0, 0), (0, 1), (1, 0), (0, 2), (1, 1), (2, 0))
    return (
        jnp.concatenate([left[p] for p, _ in order], axis=0).astype(bf16),
        jnp.concatenate([right[q] for _, q in order], axis=0).astype(bf16),
    )


def dot(left, right, left_dim, right_dim):
    return lax.dot_general(
        left, right, (((left_dim,), (right_dim,)), ((), ())), preferred_element_type=f32
    )


def fold(sums):
    return sums[0:FEATURES] + sums[FEATURES : 2 * FEATURES] + sums[2 * FEATURES :]


def weights(dist_sq):
    inverse = lax.rsqrt(dist_sq)
    cubed = inverse * inverse * inverse
    high = cubed.astype(bf16)
    low = (cubed - high.astype(f32)).astype(bf16)
    return high, low


def pair_velocities(cells):
    grams = [dot(*gram_factors(xa, xb), 0, 0) for xa, _, xb, _ in cells]
    feats = [(features(xa, fa), features(xb, fb)) for xa, fa, xb, fb in cells]
    results = []
    waiting = []

    def finish():
        sums_a, sums_b, xa, xb = waiting.pop(0)
        results.append((combine(fold(sums_a), xa), combine(fold(sums_b), xb)))

    for gram, (feat_a, feat_b), (xa, _, xb, _) in zip(grams, feats, cells):
        high, low = weights(gram)
        rows = jnp.concatenate([high, low], axis=0)
        columns = jnp.concatenate([high, low], axis=1)
        sums_b = dot(jnp.concatenate([feat_a, feat_a], axis=1), rows, 1, 0)
        sums_a = dot(jnp.concatenate([feat_b, feat_b], axis=1), columns, 1, 1)
        waiting.append((sums_a, sums_b, xa, xb))
        if len(waiting) > 1:
            finish()
    finish()
    return results


def row_base(cell, tiles):
    return cell // 8 * (8 * tiles) + lax.rem(cell, 8)


def away_of(kind, odd):
    return (0, 1 - 2 * odd, 2 * odd - 1)[kind]


def pack_kernel(sizes, cells, count, pos_hbm, frc_hbm, *refs):
    n_space, n_pairs, share, cell_dev, tiles = sizes
    outs, table = refs[:n_pairs], refs[n_pairs]
    slots, used, pos, frc, sems = refs[n_pairs + 1 :]
    fetches = [
        pltpu.make_async_copy(pos_hbm, pos, sems.at[0]),
        pltpu.make_async_copy(frc_hbm, frc, sems.at[1]),
    ]
    for fetch in fetches:
        fetch.start()
    n_slots = cells.shape[1]
    owner = cells[0, 0] // cell_dev
    here = owner // n_pairs
    here_turn = lax.rem(owner, n_pairs)
    for bucket in range(3 * n_pairs):
        used[bucket] = 0
    for s in range(n_slots):
        owner = cells[1, s] // cell_dev
        there = owner // n_pairs
        turn = lax.rem(owner, n_pairs) ^ here_turn
        kind = jnp.where(there == here, 0, jnp.where(there // 2 == here // 2, 1, 2))
        bucket = kind * n_pairs + turn
        rank = used[bucket]
        used[bucket] = rank + 1
        slots[bucket * share + rank] = s
    for fetch in fetches:
        fetch.wait()
    lane = lax.broadcasted_iota(jnp.int32, (1, LANES), 1)
    plane = cell_dev * tiles
    for m in range(3 * n_pairs):
        kind, turn = m // n_pairs, m % n_pairs
        out = outs[turn]
        label = jnp.full((1, LANES), -1.0, f32)
        for k in range(share):
            s = slots[m * share + k]
            a = lax.rem(cells[0, s], cell_dev)
            live = s < count[0]
            b = jnp.where(live, lax.rem(cells[1, s], cell_dev), -1)
            table[m * share + k] = jnp.where(live, a, -1)
            label = jnp.where(lane == k, b.astype(f32), label)
            base = row_base(a, tiles)
            for c in range(6):
                source = pos if c < 3 else frc
                row = (k * 6 + c) * tiles
                out[kind, row : row + tiles, :] = source[
                    pl.ds(base + c % 3 * plane, tiles, stride=8), :
                ]
        last = share * 6 * tiles
        out[kind, last : last + 1, :] = label


def pair_kernel(sizes, kinds, started, *refs):
    n_space, n_pairs, share, cell_dev, tiles = sizes
    n = len(kinds)
    messages, (pos, frc) = refs[:n], refs[n : n + 2]
    outs = refs[n + 2 + started :]
    (acc, reply), (inbox, todo, middles) = outs[:2], outs[-3:]
    rows_in = share * 6 * tiles
    plane = cell_dev * tiles
    if not started:
        acc[...] = jnp.zeros_like(acc)
        outs[2][...] = jnp.zeros_like(outs[2])
    here = lax.axis_index("space")
    number = jnp.int32(0)
    first = 0
    for kind, message in zip(kinds, messages):
        away = jnp.int32(away_of(kind, lax.rem(here, 2)))
        there = lax.rem(here + away + n_space, n_space)
        half = 0.5 * slab_width * away.astype(f32)
        middle_a = slab_width * (there.astype(f32) + 0.5) - half
        middle_b = slab_width * (here.astype(f32) + 0.5) + half
        for block in range(message.shape[0]):
            inbox[first * rows_in : (first + 1) * rows_in, :] = message[block, 0:rows_in, :]
            label = message[block, rows_in : rows_in + 1, :].astype(jnp.int32)
            for k in range(share):
                b = label[0, k]
                todo[0, number] = first * share + k
                todo[1, number] = b
                middles[0, number] = middle_a
                middles[1, number] = middle_b
                number = number + jnp.where(b >= 0, 1, 0)
            first += 1

    axis = lax.broadcasted_iota(jnp.int32, (3, 1), 0)

    def load(i):
        base = todo[0, i] * (6 * tiles)
        data = jnp.concatenate(
            [inbox[pl.ds(base + t, 6, stride=tiles), :] for t in range(tiles)], axis=1
        )
        start = row_base(todo[1, i], tiles)
        xb, fb = (
            jnp.concatenate(
                [ref[pl.ds(start + 8 * t, 3, stride=plane), :] for t in range(tiles)], axis=1
            )
            for ref in (pos, frc)
        )
        xa = data[0:3] - jnp.where(axis == 0, middles[0, i], across_middle)
        xb = xb - jnp.where(axis == 0, middles[1, i], across_middle)
        return xa, data[3:6], xb, fb

    def store(i, vel_a, vel_b):
        base = todo[0, i] * (3 * tiles)
        start = row_base(todo[1, i], tiles)
        parts = [slice(t * LANES, (t + 1) * LANES) for t in range(tiles)]
        places = [pl.ds(start + 8 * t, 3, stride=plane) for t in range(tiles)]
        totals = [acc[place, :] + vel_b[:, part] for place, part in zip(places, parts)]
        for t in range(tiles):
            acc[places[t], :] = totals[t]
            reply[pl.ds(base + t, 3, stride=tiles), :] = vel_a[:, parts[t]]

    def several(numbers):
        results = pair_velocities([load(i) for i in numbers])
        for i, result in zip(numbers, results):
            store(i, *result)

    def four(i, _):
        several([4 * i + j for j in range(4)])
        return 0

    lax.fori_loop(0, number // 4, four, 0)
    left = lax.rem(number, 4)

    @pl.when(left >= 2)
    def _():
        several([number - left, number - left + 1])

    @pl.when(lax.rem(left, 2) == 1)
    def _():
        several([number - 1])


def add_kernel(sizes, table, acc, *refs):
    n_space, n_pairs, share, cell_dev, tiles = sizes
    replies, out = refs[:-1], refs[-1]
    plane = cell_dev * tiles
    out[...] = acc[...]
    for m in range(3 * n_pairs):
        kind, turn = m // n_pairs, m % n_pairs
        for k in range(share):
            a = table[m * share + k]
            live = a >= 0
            base = row_base(jnp.maximum(a, 0), tiles)
            places = [pl.ds(base + c * plane, tiles, stride=8) for c in range(3)]
            totals = []
            for c in range(3):
                row = (k * 3 + c) * tiles
                term = jnp.where(live, replies[turn][kind, row : row + tiles, :], 0.0)
                totals.append(out[places[c], :] + term)
            for c in range(3):
                out[places[c], :] = totals[c]


def flat_rows(cells):
    count, _, points = cells.shape
    value = jnp.transpose(cells, (1, 0, 2)).reshape(3, count // 8, 8, points // LANES, LANES)
    return jnp.transpose(value, (0, 1, 3, 2, 4)).reshape(-1, LANES)


def cell_rows(rows, count, points):
    value = rows.reshape(3, count // 8, points // LANES, 8, LANES)
    value = jnp.transpose(value, (0, 1, 3, 2, 4)).reshape(3, count, points)
    return jnp.transpose(value, (1, 0, 2))


def body(positions, forces, pair_cells, pair_count):
    n_space = lax.axis_size("space")
    n_pairs = lax.axis_size("pairs")
    cell_dev, _, points = positions.shape
    n_slots = pair_cells.shape[1]
    share = n_slots // (3 * n_pairs)
    tiles = points // LANES
    sizes = (n_space, n_pairs, share, cell_dev, tiles)
    rows_in = share * 6 * tiles
    rows_out = share * 3 * tiles
    pos = flat_rows(positions)
    frc = flat_rows(forces)
    vmem = pl.BlockSpec(memory_space=pltpu.VMEM)
    smem = pl.BlockSpec(memory_space=pltpu.SMEM)
    hbm = pl.BlockSpec(memory_space=pltpu.HBM)
    message = jax.ShapeDtypeStruct((3, rows_in + 8, LANES), f32)
    total = jax.ShapeDtypeStruct((3 * cell_dev * tiles, LANES), f32)

    def across(value, turn):
        return lax.ppermute(value, "pairs", [(j, j ^ turn) for j in range(n_pairs)])

    def beyond(value, kind):
        moves = [(i, (i + away_of(kind, i % 2)) % n_space) for i in range(n_space)]
        return lax.ppermute(value, "space", moves)

    packed = pl.pallas_call(
        functools.partial(pack_kernel, sizes),
        out_shape=[message] * n_pairs + [jax.ShapeDtypeStruct((n_slots,), jnp.int32)],
        in_specs=[smem, smem, hbm, hbm],
        out_specs=[vmem] * n_pairs + [smem],
        scratch_shapes=[
            pltpu.SMEM((n_slots,), jnp.int32),
            pltpu.SMEM((3 * n_pairs,), jnp.int32),
            pltpu.VMEM(total.shape, f32),
            pltpu.VMEM(total.shape, f32),
            pltpu.SemaphoreType.DMA((2,)),
        ],
        compiler_params=pltpu.CompilerParams(vmem_limit_bytes=60 * 1024 * 1024),
        name="pack",
    )(pair_cells, pair_count, pos, frc)
    sent, table = packed[:n_pairs], packed[n_pairs]
    got = [sent[0]] + [across(sent[turn], turn) for turn in range(1, n_pairs)]

    def pairs(arrived, before):
        kinds = [kind for kind, _ in arrived]
        values = [value for _, value in arrived]
        n = len(values)
        blocks = sum(value.shape[0] for value in values)
        return pl.pallas_call(
            functools.partial(pair_kernel, sizes, kinds, len(before)),
            out_shape=[total, jax.ShapeDtypeStruct((blocks * rows_out, LANES), f32)]
            + [jax.ShapeDtypeStruct((1, LANES), f32)] * (not before),
            in_specs=[vmem] * (n + 2 + len(before)),
            out_specs=[vmem] * (2 + (not before)),
            scratch_shapes=[
                pltpu.VMEM((blocks * rows_in, LANES), f32),
                pltpu.SMEM((2, blocks * share + 1), jnp.int32),
                pltpu.SMEM((2, blocks * share + 1), f32),
            ],
            input_output_aliases={n + 2: 0} if before else {},
            compiler_params=pltpu.CompilerParams(vmem_limit_bytes=48 * 1024 * 1024),
            cost_estimate=pl.CostEstimate(
                flops=blocks * 1_000_000_000, bytes_accessed=2_000_000, transcendentals=2_000_000
            ),
            name="pairs",
        )(*values, pos, frc, *before)

    near, far = range(2), range(2, n_pairs)
    own = [sent[0][kind : kind + 1] for kind in range(3)]
    core = [got[1][kind : kind + 1] for kind in range(3)]
    out_1n = beyond(jnp.concatenate([own[1], core[1]]), 1)
    acc, reply_0n, nothing = pairs([(0, own[0]), (0, core[0])], [])
    rest = [got[turn] + nothing[None] for turn in far]
    out_1f = beyond(jnp.stack([value[1] for value in rest]), 1)
    out_2 = beyond(jnp.concatenate([own[2], core[2]] + [value[2:] for value in rest]), 2)
    acc, reply_m = pairs([(1, out_1n)] + [(0, got[turn][0:1]) for turn in far], [acc])
    acc, reply_f = pairs([(1, out_1f), (2, out_2)], [acc])
    reply_0n, reply_m, reply_f = (
        value.reshape(-1, rows_out, LANES) for value in (reply_0n, reply_m, reply_f)
    )
    cut = n_pairs - 2
    back_0 = jnp.concatenate([reply_0n, reply_m[2:]])
    back_1 = beyond(jnp.concatenate([reply_m[:2], reply_f[:cut]]), 1)
    back_2 = beyond(reply_f[cut:], 2)
    back = []
    for turn in range(n_pairs):
        value = jnp.stack([back_0[turn], back_1[turn], back_2[turn]])
        back.append(across(value, turn) if turn else value)
    velocity = pl.pallas_call(
        functools.partial(add_kernel, sizes),
        out_shape=total,
        in_specs=[smem] + [vmem] * (1 + n_pairs),
        out_specs=vmem,
        compiler_params=pltpu.CompilerParams(vmem_limit_bytes=48 * 1024 * 1024),
        name="add",
    )(table, acc, *back)
    return cell_rows(velocity, cell_dev, points)


def solution(mesh):
    placed = (
        P(("space", "pairs"), None, None),
        P(("space", "pairs"), None, None),
        P(None, ("space", "pairs")),
        P(("space", "pairs")),
    )
    return jax.shard_map(
        body,
        mesh=mesh,
        in_specs=placed,
        out_specs=P(("space", "pairs"), None, None),
        check_vma=False,
    )
```

```python
import functools
import math

import jax
import jax.numpy as jnp
from jax import lax
from jax.experimental import pallas as pl
from jax.experimental.pallas import tpu as pltpu
from jax.sharding import PartitionSpec as P

stokes_coef = 1.0 / (8.0 * math.pi)
eps_sq = 0.01
slab_width = 3.0
across_middle = 1.0
LANES = 128
FEATURES = 16

f32 = jnp.float32
bf16 = jnp.bfloat16


def split(value, terms):
    parts = []
    for _ in range(terms - 1):
        part = value.astype(bf16).astype(f32)
        parts.append(part)
        value = value - part
    parts.append(value)
    return parts


def features(x, f):
    norm = jnp.sum(x * x, axis=0, keepdims=True)
    along = jnp.sum(x * f, axis=0, keepdims=True)
    rows = [f] + [x[k : k + 1] * f for k in range(3)] + [norm * f + x * along]
    rows.append(jnp.zeros_like(norm))
    stacked = jnp.concatenate(rows, axis=0)
    return jnp.concatenate([part.astype(bf16) for part in split(stacked, 3)], axis=0)


def combine(sums, y):
    force = sums[0:3]
    moment = [sums[3 + 3 * k : 6 + 3 * k] for k in range(3)]
    second = sums[12:15]
    norm = jnp.sum(y * y, axis=0, keepdims=True)
    trace = moment[0][0:1] + moment[1][1:2] + moment[2][2:3]
    along = jnp.sum(y * force, axis=0, keepdims=True) - trace
    turned = jnp.concatenate(
        [jnp.sum(y * moment[k], axis=0, keepdims=True) for k in range(3)], axis=0
    )
    mixed = y[0:1] * moment[0] + y[1:2] * moment[1] + y[2:3] * moment[2]
    velocity = (norm + 2.0 * eps_sq) * force + second - 2.0 * mixed + y * along - turned
    return velocity * stokes_coef


def gram_factors(x, y):
    one = jnp.ones((1, x.shape[1]), f32)
    none = jnp.zeros((3, x.shape[1]), f32)
    norm_x = jnp.sum(x * x, axis=0, keepdims=True)
    norm_y = jnp.sum(y * y, axis=0, keepdims=True) + eps_sq
    left = split(jnp.concatenate([x, norm_x, one, none], axis=0), 3)
    right = split(jnp.concatenate([-2.0 * y, one, norm_y, none], axis=0), 3)
    order = ((0, 0), (0, 1), (1, 0), (0, 2), (1, 1), (2, 0))
    return (
        jnp.concatenate([left[p] for p, _ in order], axis=0).astype(bf16),
        jnp.concatenate([right[q] for _, q in order], axis=0).astype(bf16),
    )


def dot(left, right, left_dim, right_dim):
    return lax.dot_general(
        left, right, (((left_dim,), (right_dim,)), ((), ())), preferred_element_type=f32
    )


def fold(sums):
    return sums[0:FEATURES] + sums[FEATURES : 2 * FEATURES] + sums[2 * FEATURES :]


def weights(dist_sq):
    inverse = lax.rsqrt(dist_sq)
    cubed = inverse * inverse * inverse
    high = cubed.astype(bf16)
    low = (cubed - high.astype(f32)).astype(bf16)
    return high, low


def pair_velocities(cells):
    grams = [dot(*gram_factors(xa, xb), 0, 0) for xa, _, xb, _ in cells]
    feats = [(features(xa, fa), features(xb, fb)) for xa, fa, xb, fb in cells]
    results = []
    waiting = []

    def finish():
        sums_a, sums_b, xa, xb = waiting.pop(0)
        results.append((combine(fold(sums_a), xa), combine(fold(sums_b), xb)))

    for gram, (feat_a, feat_b), (xa, _, xb, _) in zip(grams, feats, cells):
        high, low = weights(gram)
        rows = jnp.concatenate([high, low], axis=0)
        columns = jnp.concatenate([high, low], axis=1)
        sums_b = dot(jnp.concatenate([feat_a, feat_a], axis=1), rows, 1, 0)
        sums_a = dot(jnp.concatenate([feat_b, feat_b], axis=1), columns, 1, 1)
        waiting.append((sums_a, sums_b, xa, xb))
        if len(waiting) > 1:
            finish()
    finish()
    return results


def row_base(cell, tiles):
    return cell // 8 * (8 * tiles) + lax.rem(cell, 8)


def away_of(kind, odd):
    return (0, 1 - 2 * odd, 2 * odd - 1)[kind]


def pack_kernel(sizes, cells, count, pos_hbm, frc_hbm, *refs):
    n_space, n_pairs, share, cell_dev, tiles = sizes
    targets, table = refs[:n_pairs], refs[n_pairs]
    slots, used, pos, frc, built, sems, out_sems = refs[n_pairs + 1 :]
    fetches = [
        pltpu.make_async_copy(pos_hbm, pos, sems.at[0]),
        pltpu.make_async_copy(frc_hbm, frc, sems.at[1]),
    ]
    for fetch in fetches:
        fetch.start()
    n_slots = cells.shape[1]
    owner = cells[0, 0] // cell_dev
    here = owner // n_pairs
    here_turn = lax.rem(owner, n_pairs)
    for bucket in range(3 * n_pairs):
        used[bucket] = 0
    for s in range(n_slots):
        owner = cells[1, s] // cell_dev
        there = owner // n_pairs
        turn = lax.rem(owner, n_pairs) ^ here_turn
        kind = jnp.where(there == here, 0, jnp.where(there // 2 == here // 2, 1, 2))
        bucket = kind * n_pairs + turn
        rank = used[bucket]
        used[bucket] = rank + 1
        slots[bucket * share + rank] = s
    for fetch in fetches:
        fetch.wait()
    lane = lax.broadcasted_iota(jnp.int32, (1, LANES), 1)
    plane = cell_dev * tiles
    sends = []
    for turn, kind in [(turn, kind) for turn in reversed(range(n_pairs)) for kind in range(3)]:
        m = kind * n_pairs + turn
        out = built.at[turn]
        label = jnp.full((1, LANES), -1.0, f32)
        for k in range(share):
            s = slots[m * share + k]
            a = lax.rem(cells[0, s], cell_dev)
            live = s < count[0]
            b = jnp.where(live, lax.rem(cells[1, s], cell_dev), -1)
            table[m * share + k] = jnp.where(live, a, -1)
            label = jnp.where(lane == k, b.astype(f32), label)
            base = row_base(a, tiles)
            for c in range(6):
                source = pos if c < 3 else frc
                row = (k * 6 + c) * tiles
                out[kind, row : row + tiles, :] = source[
                    pl.ds(base + c % 3 * plane, tiles, stride=8), :
                ]
        last = share * 6 * tiles
        out[kind, last : last + 1, :] = label
        if kind == 2:
            send = pltpu.make_async_copy(out, targets[turn], out_sems.at[turn])
            send.start()
            sends.append(send)
    for send in sends:
        send.wait()


def pair_kernel(sizes, kinds, started, extra, *refs):
    n_space, n_pairs, share, cell_dev, tiles = sizes
    n = len(kinds)
    refs = refs[extra:]
    messages, (pos, frc) = refs[:n], refs[n : n + 2]
    outs = refs[n + 2 + started :]
    (acc, reply), (inbox, todo, middles) = outs[:2], outs[-3:]
    rows_in = share * 6 * tiles
    plane = cell_dev * tiles
    if not started:
        acc[...] = jnp.zeros_like(acc)
        outs[2][...] = jnp.zeros_like(outs[2])
    here = lax.axis_index("space")
    number = jnp.int32(0)
    first = 0
    for kind, message in zip(kinds, messages):
        away = jnp.int32(away_of(kind, lax.rem(here, 2)))
        there = lax.rem(here + away + n_space, n_space)
        half = 0.5 * slab_width * away.astype(f32)
        middle_a = slab_width * (there.astype(f32) + 0.5) - half
        middle_b = slab_width * (here.astype(f32) + 0.5) + half
        for block in range(message.shape[0]):
            inbox[first * rows_in : (first + 1) * rows_in, :] = message[block, 0:rows_in, :]
            label = message[block, rows_in : rows_in + 1, :].astype(jnp.int32)
            for k in range(share):
                b = label[0, k]
                todo[0, number] = first * share + k
                todo[1, number] = b
                middles[0, number] = middle_a
                middles[1, number] = middle_b
                number = number + jnp.where(b >= 0, 1, 0)
            first += 1

    axis = lax.broadcasted_iota(jnp.int32, (3, 1), 0)

    def load(i):
        base = todo[0, i] * (6 * tiles)
        data = jnp.concatenate(
            [inbox[pl.ds(base + t, 6, stride=tiles), :] for t in range(tiles)], axis=1
        )
        start = row_base(todo[1, i], tiles)
        xb, fb = (
            jnp.concatenate(
                [ref[pl.ds(start + 8 * t, 3, stride=plane), :] for t in range(tiles)], axis=1
            )
            for ref in (pos, frc)
        )
        xa = data[0:3] - jnp.where(axis == 0, middles[0, i], across_middle)
        xb = xb - jnp.where(axis == 0, middles[1, i], across_middle)
        return xa, data[3:6], xb, fb

    def store(i, vel_a, vel_b):
        base = todo[0, i] * (3 * tiles)
        start = row_base(todo[1, i], tiles)
        parts = [slice(t * LANES, (t + 1) * LANES) for t in range(tiles)]
        places = [pl.ds(start + 8 * t, 3, stride=plane) for t in range(tiles)]
        totals = [acc[place, :] + vel_b[:, part] for place, part in zip(places, parts)]
        for t in range(tiles):
            acc[places[t], :] = totals[t]
            reply[pl.ds(base + t, 3, stride=tiles), :] = vel_a[:, parts[t]]

    def several(numbers):
        results = pair_velocities([load(i) for i in numbers])
        for i, result in zip(numbers, results):
            store(i, *result)

    def four(i, _):
        several([4 * i + j for j in range(4)])
        return 0

    lax.fori_loop(0, number // 4, four, 0)
    left = lax.rem(number, 4)

    @pl.when(left >= 2)
    def _():
        several([number - left, number - left + 1])

    @pl.when(lax.rem(left, 2) == 1)
    def _():
        several([number - 1])


def add_kernel(sizes, table, acc, *refs):
    n_space, n_pairs, share, cell_dev, tiles = sizes
    replies, (out, *others) = refs[:n_pairs], refs[n_pairs:]
    plane = cell_dev * tiles
    out[...] = acc[...]
    for other in others:
        other[...] = jnp.zeros_like(other)
    chains = [out, *others]
    for turn in range(n_pairs):
        for k in range(share):
            steps = []
            for kind, chain in enumerate(chains):
                a = table[(kind * n_pairs + turn) * share + k]
                live = a >= 0
                base = row_base(jnp.maximum(a, 0), tiles)
                for c in range(3):
                    place = pl.ds(base + c * plane, tiles, stride=8)
                    row = (k * 3 + c) * tiles
                    term = jnp.where(live, replies[turn][kind, row : row + tiles, :], 0.0)
                    steps.append((chain, place, chain[place, :] + term))
            for chain, place, value in steps:
                chain[place, :] = value
    out[...] += others[0][...] + others[1][...]


def flat_rows(cells):
    count, _, points = cells.shape
    value = jnp.transpose(cells, (1, 0, 2)).reshape(3, count // 8, 8, points // LANES, LANES)
    return jnp.transpose(value, (0, 1, 3, 2, 4)).reshape(-1, LANES)


def cell_rows(rows, count, points):
    value = rows.reshape(3, count // 8, points // LANES, 8, LANES)
    value = jnp.transpose(value, (0, 1, 3, 2, 4)).reshape(3, count, points)
    return jnp.transpose(value, (1, 0, 2))


def body(positions, forces, pair_cells, pair_count):
    n_space = lax.axis_size("space")
    n_pairs = lax.axis_size("pairs")
    cell_dev, _, points = positions.shape
    n_slots = pair_cells.shape[1]
    share = n_slots // (3 * n_pairs)
    tiles = points // LANES
    sizes = (n_space, n_pairs, share, cell_dev, tiles)
    rows_in = share * 6 * tiles
    rows_out = share * 3 * tiles
    pos = flat_rows(positions)
    frc = flat_rows(forces)
    vmem = pl.BlockSpec(memory_space=pltpu.VMEM)
    smem = pl.BlockSpec(memory_space=pltpu.SMEM)
    hbm = pl.BlockSpec(memory_space=pltpu.HBM)
    message = jax.ShapeDtypeStruct((3, rows_in + 8, LANES), f32)
    total = jax.ShapeDtypeStruct((3 * cell_dev * tiles, LANES), f32)

    def across(value, turn):
        return lax.ppermute(value, "pairs", [(j, j ^ turn) for j in range(n_pairs)])

    def beyond(value, kind):
        moves = [(i, (i + away_of(kind, i % 2)) % n_space) for i in range(n_space)]
        return lax.ppermute(value, "space", moves)

    packed = pl.pallas_call(
        functools.partial(pack_kernel, sizes),
        out_shape=[message] * n_pairs + [jax.ShapeDtypeStruct((n_slots,), jnp.int32)],
        in_specs=[smem, smem, hbm, hbm],
        out_specs=[hbm] * n_pairs + [smem],
        scratch_shapes=[
            pltpu.SMEM((n_slots,), jnp.int32),
            pltpu.SMEM((3 * n_pairs,), jnp.int32),
            pltpu.VMEM(total.shape, f32),
            pltpu.VMEM(total.shape, f32),
            pltpu.VMEM((n_pairs,) + message.shape, f32),
            pltpu.SemaphoreType.DMA((2,)),
            pltpu.SemaphoreType.DMA((n_pairs,)),
        ],
        compiler_params=pltpu.CompilerParams(vmem_limit_bytes=60 * 1024 * 1024),
        name="pack",
    )(pair_cells, pair_count, pos, frc)
    sent, table = packed[:n_pairs], packed[n_pairs]
    got = [sent[0]] + [across(sent[turn], turn) for turn in range(1, n_pairs)]

    def pairs(arrived, before, extra=()):
        kinds = [kind for kind, _ in arrived]
        values = [value for _, value in arrived]
        n = len(values)
        blocks = sum(value.shape[0] for value in values)
        return pl.pallas_call(
            functools.partial(pair_kernel, sizes, kinds, len(before), len(extra)),
            out_shape=[total, jax.ShapeDtypeStruct((blocks * rows_out, LANES), f32)]
            + [jax.ShapeDtypeStruct((1, LANES), f32)] * (not before),
            in_specs=[spec for spec, _ in extra] + [vmem] * (n + 2 + len(before)),
            out_specs=[vmem] * (2 + (not before)),
            scratch_shapes=[
                pltpu.VMEM((blocks * rows_in, LANES), f32),
                pltpu.SMEM((2, blocks * share + 1), jnp.int32),
                pltpu.SMEM((2, blocks * share + 1), f32),
            ],
            input_output_aliases={len(extra) + n + 2: 0} if before else {},
            compiler_params=pltpu.CompilerParams(vmem_limit_bytes=48 * 1024 * 1024),
            cost_estimate=pl.CostEstimate(
                flops=blocks * 1_000_000_000, bytes_accessed=2_000_000, transcendentals=2_000_000
            ),
            name="pairs",
        )(*[value for _, value in extra], *values, pos, frc, *before)

    near, far = range(2), range(2, n_pairs)
    own = [sent[0][kind : kind + 1] for kind in range(3)]
    core = [got[1][kind : kind + 1] for kind in range(3)]
    out_1n = beyond(jnp.concatenate([own[1], core[1]]), 1)
    acc, reply_0n, nothing = pairs([(0, own[0]), (0, core[0])], [])
    rest = [got[turn] + nothing[None] for turn in far]
    out_2 = beyond(jnp.concatenate([own[2], core[2]] + [value[2:] for value in rest]), 2)
    out_1f = beyond(jnp.stack([value[1] for value in rest]), 1)
    half = (n_pairs - 2) // 2
    early, late = far[:half], far[half:]
    acc, reply_m = pairs(
        [(1, out_1n)] + [(0, got[turn][0:1]) for turn in early], [acc], [(smem, table)]
    )
    acc, reply_2 = pairs([(2, out_2)], [acc])
    back_2 = beyond(reply_2, 2)
    acc, reply_l = pairs(
        [(0, got[turn][0:1]) for turn in late] + [(1, out_1f[:half])], [acc]
    )
    acc, reply_f = pairs([(1, out_1f[half:])], [acc], [(hbm, back_2)])
    reply_0n, reply_m, reply_l, reply_f, back_2 = (
        value.reshape(-1, rows_out, LANES)
        for value in (reply_0n, reply_m, reply_l, reply_f, back_2)
    )
    back_0 = jnp.concatenate([reply_0n, reply_m[2:], reply_l[:half]])
    back_1n = beyond(reply_m[:2], 1)
    back_1f = beyond(jnp.concatenate([reply_l[half:], reply_f]), 1)
    back_1 = jnp.concatenate([back_1n, back_1f])
    back = []
    for turn in range(n_pairs):
        value = jnp.stack([back_0[turn], back_1[turn], back_2[turn]])
        back.append(across(value, turn) if turn else value)
    velocity = pl.pallas_call(
        functools.partial(add_kernel, sizes),
        out_shape=total,
        in_specs=[smem] + [vmem] * (1 + n_pairs),
        out_specs=vmem,
        scratch_shapes=[pltpu.VMEM(total.shape, f32)] * 2,
        compiler_params=pltpu.CompilerParams(vmem_limit_bytes=48 * 1024 * 1024),
        name="add",
    )(table, acc, *back)
    return cell_rows(velocity, cell_dev, points)


def solution(mesh):
    placed = (
        P(("space", "pairs"), None, None),
        P(("space", "pairs"), None, None),
        P(None, ("space", "pairs")),
        P(("space", "pairs")),
    )
    return jax.shard_map(
        body,
        mesh=mesh,
        in_specs=placed,
        out_specs=P(("space", "pairs"), None, None),
        check_vma=False,
    )
```

```python
import functools
import math

import jax
import jax.numpy as jnp
from jax import lax
from jax.experimental import pallas as pl
from jax.experimental.pallas import tpu as pltpu
from jax.sharding import PartitionSpec as P

stokes_coef = 1.0 / (8.0 * math.pi)
eps_sq = 0.01
slab_width = 3.0
across_middle = 1.0
LANES = 128
FEATURES = 16

f32 = jnp.float32
bf16 = jnp.bfloat16


def split(value, terms):
    parts = []
    for _ in range(terms - 1):
        part = value.astype(bf16).astype(f32)
        parts.append(part)
        value = value - part
    parts.append(value)
    return parts


def features(x, f):
    norm = jnp.sum(x * x, axis=0, keepdims=True)
    along = jnp.sum(x * f, axis=0, keepdims=True)
    rows = [f] + [x[k : k + 1] * f for k in range(3)] + [norm * f + x * along]
    rows.append(jnp.zeros_like(norm))
    stacked = jnp.concatenate(rows, axis=0)
    return jnp.concatenate([part.astype(bf16) for part in split(stacked, 3)], axis=0)


def combine(sums, y):
    force = sums[0:3]
    moment = [sums[3 + 3 * k : 6 + 3 * k] for k in range(3)]
    second = sums[12:15]
    norm = jnp.sum(y * y, axis=0, keepdims=True)
    trace = moment[0][0:1] + moment[1][1:2] + moment[2][2:3]
    along = jnp.sum(y * force, axis=0, keepdims=True) - trace
    turned = jnp.concatenate(
        [jnp.sum(y * moment[k], axis=0, keepdims=True) for k in range(3)], axis=0
    )
    mixed = y[0:1] * moment[0] + y[1:2] * moment[1] + y[2:3] * moment[2]
    velocity = (norm + 2.0 * eps_sq) * force + second - 2.0 * mixed + y * along - turned
    return velocity * stokes_coef


def gram_factors(x, y):
    one = jnp.ones((1, x.shape[1]), f32)
    none = jnp.zeros((3, x.shape[1]), f32)
    norm_x = jnp.sum(x * x, axis=0, keepdims=True)
    norm_y = jnp.sum(y * y, axis=0, keepdims=True) + eps_sq
    left = split(jnp.concatenate([x, norm_x, one, none], axis=0), 3)
    right = split(jnp.concatenate([-2.0 * y, one, norm_y, none], axis=0), 3)
    order = ((0, 0), (0, 1), (1, 0), (0, 2), (1, 1), (2, 0))
    return (
        jnp.concatenate([left[p] for p, _ in order], axis=0).astype(bf16),
        jnp.concatenate([right[q] for _, q in order], axis=0).astype(bf16),
    )


def dot(left, right, left_dim, right_dim):
    return lax.dot_general(
        left, right, (((left_dim,), (right_dim,)), ((), ())), preferred_element_type=f32
    )


def fold(sums):
    return sums[0:FEATURES] + sums[FEATURES : 2 * FEATURES] + sums[2 * FEATURES :]


def weights(dist_sq):
    inverse = lax.rsqrt(dist_sq)
    cubed = inverse * inverse * inverse
    high = cubed.astype(bf16)
    low = (cubed - high.astype(f32)).astype(bf16)
    return high, low


def pair_velocities(cells):
    grams = [dot(*gram_factors(xa, xb), 0, 0) for xa, _, xb, _ in cells]
    feats = [(features(xa, fa), features(xb, fb)) for xa, fa, xb, fb in cells]
    results = []
    waiting = []

    def finish():
        sums_a, sums_b, xa, xb = waiting.pop(0)
        results.append((combine(fold(sums_a), xa), combine(fold(sums_b), xb)))

    for gram, (feat_a, feat_b), (xa, _, xb, _) in zip(grams, feats, cells):
        high, low = weights(gram)
        rows = jnp.concatenate([high, low], axis=0)
        columns = jnp.concatenate([high, low], axis=1)
        sums_b = dot(jnp.concatenate([feat_a, feat_a], axis=1), rows, 1, 0)
        sums_a = dot(jnp.concatenate([feat_b, feat_b], axis=1), columns, 1, 1)
        waiting.append((sums_a, sums_b, xa, xb))
        if len(waiting) > 1:
            finish()
    finish()
    return results


def row_base(cell, tiles):
    return cell // 8 * (8 * tiles) + lax.rem(cell, 8)


def away_of(kind, odd):
    return (0, 1 - 2 * odd, 2 * odd - 1)[kind]


def pack_kernel(sizes, cells, count, pos_hbm, frc_hbm, *refs):
    n_space, n_pairs, share, cell_dev, tiles = sizes
    outs, (first, second, table) = refs[:n_pairs], refs[n_pairs : n_pairs + 3]
    slots, used, pos, frc, sems = refs[n_pairs + 3 :]
    fetches = [
        pltpu.make_async_copy(pos_hbm, pos, sems.at[0]),
        pltpu.make_async_copy(frc_hbm, frc, sems.at[1]),
    ]
    for fetch in fetches:
        fetch.start()
    n_slots = cells.shape[1]
    owner = cells[0, 0] // cell_dev
    here = owner // n_pairs
    here_turn = lax.rem(owner, n_pairs)
    for bucket in range(3 * n_pairs):
        used[bucket] = 0
    for s in range(n_slots):
        owner = cells[1, s] // cell_dev
        there = owner // n_pairs
        turn = lax.rem(owner, n_pairs) ^ here_turn
        kind = jnp.where(there == here, 0, jnp.where(there // 2 == here // 2, 1, 2))
        bucket = kind * n_pairs + turn
        rank = used[bucket]
        used[bucket] = rank + 1
        slots[bucket * share + rank] = s
    for fetch in fetches:
        fetch.wait()
    lane = lax.broadcasted_iota(jnp.int32, (1, LANES), 1)
    plane = cell_dev * tiles
    for m in range(3 * n_pairs):
        kind, turn = m // n_pairs, m % n_pairs
        out = (outs[turn].at[0], first.at[turn], second.at[turn])[kind]
        label = jnp.full((1, LANES), -1.0, f32)
        for k in range(share):
            s = slots[m * share + k]
            a = lax.rem(cells[0, s], cell_dev)
            live = s < count[0]
            b = jnp.where(live, lax.rem(cells[1, s], cell_dev), -1)
            table[m * share + k] = jnp.where(live, a, -1)
            label = jnp.where(lane == k, b.astype(f32), label)
            base = row_base(a, tiles)
            for c in range(6):
                source = pos if c < 3 else frc
                row = (k * 6 + c) * tiles
                out[row : row + tiles, :] = source[
                    pl.ds(base + c % 3 * plane, tiles, stride=8), :
                ]
        last = share * 6 * tiles
        out[last : last + 1, :] = label


def pair_kernel(sizes, kinds, started, extra, *refs):
    n_space, n_pairs, share, cell_dev, tiles = sizes
    n = len(kinds)
    refs = refs[extra:]
    messages, (pos, frc) = refs[:n], refs[n : n + 2]
    outs = refs[n + 2 + started :]
    (acc, reply), (inbox, todo, middles) = outs[:2], outs[-3:]
    rows_in = share * 6 * tiles
    plane = cell_dev * tiles
    if not started:
        acc[...] = jnp.zeros_like(acc)
    outs[2][...] = jnp.zeros_like(outs[2])
    here = lax.axis_index("space")
    number = jnp.int32(0)
    first = 0
    for several_kinds, message in zip(kinds, messages):
        for block, kind in enumerate(several_kinds):
            away = jnp.int32(away_of(kind, lax.rem(here, 2)))
            there = lax.rem(here + away + n_space, n_space)
            half = 0.5 * slab_width * away.astype(f32)
            middle_a = slab_width * (there.astype(f32) + 0.5) - half
            middle_b = slab_width * (here.astype(f32) + 0.5) + half
            inbox[first * rows_in : (first + 1) * rows_in, :] = message[block, 0:rows_in, :]
            label = message[block, rows_in : rows_in + 1, :].astype(jnp.int32)
            for k in range(share):
                b = label[0, k]
                todo[0, number] = first * share + k
                todo[1, number] = b
                middles[0, number] = middle_a
                middles[1, number] = middle_b
                number = number + jnp.where(b >= 0, 1, 0)
            first += 1

    axis = lax.broadcasted_iota(jnp.int32, (3, 1), 0)

    def load(i):
        base = todo[0, i] * (6 * tiles)
        data = jnp.concatenate(
            [inbox[pl.ds(base + t, 6, stride=tiles), :] for t in range(tiles)], axis=1
        )
        start = row_base(todo[1, i], tiles)
        xb, fb = (
            jnp.concatenate(
                [ref[pl.ds(start + 8 * t, 3, stride=plane), :] for t in range(tiles)], axis=1
            )
            for ref in (pos, frc)
        )
        xa = data[0:3] - jnp.where(axis == 0, middles[0, i], across_middle)
        xb = xb - jnp.where(axis == 0, middles[1, i], across_middle)
        return xa, data[3:6], xb, fb

    def store(i, vel_a, vel_b):
        base = todo[0, i] * (3 * tiles)
        start = row_base(todo[1, i], tiles)
        parts = [slice(t * LANES, (t + 1) * LANES) for t in range(tiles)]
        places = [pl.ds(start + 8 * t, 3, stride=plane) for t in range(tiles)]
        totals = [acc[place, :] + vel_b[:, part] for place, part in zip(places, parts)]
        for t in range(tiles):
            acc[places[t], :] = totals[t]
            reply[pl.ds(base + t, 3, stride=tiles), :] = vel_a[:, parts[t]]

    def several(numbers):
        results = pair_velocities([load(i) for i in numbers])
        for i, result in zip(numbers, results):
            store(i, *result)

    def four(i, _):
        several([4 * i + j for j in range(4)])
        return 0

    lax.fori_loop(0, number // 4, four, 0)
    left = lax.rem(number, 4)

    @pl.when(left >= 2)
    def _():
        several([number - left, number - left + 1])

    @pl.when(lax.rem(left, 2) == 1)
    def _():
        several([number - 1])


def add_kernel(sizes, table, acc, *refs):
    n_space, n_pairs, share, cell_dev, tiles = sizes
    replies, out = refs[:-1], refs[-1]
    plane = cell_dev * tiles
    out[...] = acc[...]
    for m in range(3 * n_pairs):
        kind, turn = m // n_pairs, m % n_pairs
        for k in range(share):
            a = table[m * share + k]
            live = a >= 0
            base = row_base(jnp.maximum(a, 0), tiles)
            places = [pl.ds(base + c * plane, tiles, stride=8) for c in range(3)]
            totals = []
            for c in range(3):
                row = (k * 3 + c) * tiles
                term = jnp.where(live, replies[turn][kind, row : row + tiles, :], 0.0)
                totals.append(out[places[c], :] + term)
            for c in range(3):
                out[places[c], :] = totals[c]


def flat_rows(cells):
    count, _, points = cells.shape
    value = jnp.transpose(cells, (1, 0, 2)).reshape(3, count // 8, 8, points // LANES, LANES)
    return jnp.transpose(value, (0, 1, 3, 2, 4)).reshape(-1, LANES)


def cell_rows(rows, count, points):
    value = rows.reshape(3, count // 8, points // LANES, 8, LANES)
    value = jnp.transpose(value, (0, 1, 3, 2, 4)).reshape(3, count, points)
    return jnp.transpose(value, (1, 0, 2))


def body(positions, forces, pair_cells, pair_count):
    n_space = lax.axis_size("space")
    n_pairs = lax.axis_size("pairs")
    cell_dev, _, points = positions.shape
    n_slots = pair_cells.shape[1]
    share = n_slots // (3 * n_pairs)
    tiles = points // LANES
    sizes = (n_space, n_pairs, share, cell_dev, tiles)
    rows_in = share * 6 * tiles
    rows_out = share * 3 * tiles
    pos = flat_rows(positions)
    frc = flat_rows(forces)
    vmem = pl.BlockSpec(memory_space=pltpu.VMEM)
    smem = pl.BlockSpec(memory_space=pltpu.SMEM)
    hbm = pl.BlockSpec(memory_space=pltpu.HBM)
    message = jax.ShapeDtypeStruct((1, rows_in + 8, LANES), f32)
    messages = jax.ShapeDtypeStruct((n_pairs, rows_in + 8, LANES), f32)
    total = jax.ShapeDtypeStruct((3 * cell_dev * tiles, LANES), f32)

    def across(value, turn):
        return lax.ppermute(value, "pairs", [(j, j ^ turn) for j in range(n_pairs)])

    def beyond(value, kind):
        moves = [(i, (i + away_of(kind, i % 2)) % n_space) for i in range(n_space)]
        return lax.ppermute(value, "space", moves)

    packed = pl.pallas_call(
        functools.partial(pack_kernel, sizes),
        out_shape=[message] * n_pairs
        + [messages] * 2
        + [jax.ShapeDtypeStruct((n_slots,), jnp.int32)],
        in_specs=[smem, smem, hbm, hbm],
        out_specs=[vmem] * (n_pairs + 2) + [smem],
        scratch_shapes=[
            pltpu.SMEM((n_slots,), jnp.int32),
            pltpu.SMEM((3 * n_pairs,), jnp.int32),
            pltpu.VMEM(total.shape, f32),
            pltpu.VMEM(total.shape, f32),
            pltpu.SemaphoreType.DMA((2,)),
        ],
        compiler_params=pltpu.CompilerParams(vmem_limit_bytes=60 * 1024 * 1024),
        name="pack",
    )(pair_cells, pair_count, pos, frc)
    sent, (first, second, table) = packed[:n_pairs], packed[n_pairs:]
    first, second = beyond(first, 1), beyond(second, 2)
    own = [sent[0]] + [across(sent[turn], turn) for turn in range(1, n_pairs)]

    def pairs(arrived, before, extra=()):
        kinds = [kinds for kinds, _ in arrived]
        values = [value for _, value in arrived]
        n = len(values)
        blocks = sum(value.shape[0] for value in values)
        return pl.pallas_call(
            functools.partial(pair_kernel, sizes, kinds, len(before), len(extra)),
            out_shape=[total, jax.ShapeDtypeStruct((blocks * rows_out, LANES), f32)]
            + [jax.ShapeDtypeStruct((1, LANES), f32)],
            in_specs=[smem] * len(extra) + [vmem] * (n + 2 + len(before)),
            out_specs=[vmem] * 3,
            scratch_shapes=[
                pltpu.VMEM((blocks * rows_in, LANES), f32),
                pltpu.SMEM((2, blocks * share + 1), jnp.int32),
                pltpu.SMEM((2, blocks * share + 1), f32),
            ],
            input_output_aliases={len(extra) + n + 2: 0} if before else {},
            compiler_params=pltpu.CompilerParams(vmem_limit_bytes=48 * 1024 * 1024),
            cost_estimate=pl.CostEstimate(
                flops=blocks * 1_000_000_000, bytes_accessed=2_000_000, transcendentals=2_000_000
            ),
            name="pairs",
        )(*extra, *values, pos, frc, *before)

    near, far = range(2), range(2, n_pairs)
    acc, reply_0n, nothing = pairs([((0,), own[turn]) for turn in near], [])
    acc, reply_0f, nothing = pairs([((0,), own[turn]) for turn in far], [acc], [table])
    first, second = first + nothing[None], second + nothing[None]
    got = [
        across(jnp.stack([first[turn], second[turn]]), turn) for turn in range(1, n_pairs)
    ]
    acc, reply_n, _ = pairs([((1,), first[:1]), ((2,), second[:1])], [acc])
    acc, reply_f, _ = pairs([((1, 2), value) for value in got], [acc])
    reply_0n, reply_0f, reply_n, reply_f = (
        value.reshape(-1, rows_out, LANES) for value in (reply_0n, reply_0f, reply_n, reply_f)
    )
    back_0 = jnp.concatenate([reply_0n, reply_0f])
    back_1 = beyond(jnp.concatenate([reply_n[0:1], reply_f[0::2]]), 1)
    back_2 = beyond(jnp.concatenate([reply_n[1:2], reply_f[1::2]]), 2)
    back = []
    for turn in range(n_pairs):
        value = jnp.stack([back_0[turn], back_1[turn], back_2[turn]])
        back.append(across(value, turn) if turn else value)
    velocity = pl.pallas_call(
        functools.partial(add_kernel, sizes),
        out_shape=total,
        in_specs=[smem] + [vmem] * (1 + n_pairs),
        out_specs=vmem,
        compiler_params=pltpu.CompilerParams(vmem_limit_bytes=48 * 1024 * 1024),
        name="add",
    )(table, acc, *back)
    return cell_rows(velocity, cell_dev, points)


def solution(mesh):
    placed = (
        P(("space", "pairs"), None, None),
        P(("space", "pairs"), None, None),
        P(None, ("space", "pairs")),
        P(("space", "pairs")),
    )
    return jax.shard_map(
        body,
        mesh=mesh,
        in_specs=placed,
        out_specs=P(("space", "pairs"), None, None),
        check_vma=False,
    )
```

```python
import functools
import math

import jax
import jax.numpy as jnp
from jax import lax
from jax.experimental import pallas as pl
from jax.experimental.pallas import tpu as pltpu
from jax.sharding import PartitionSpec as P

stokes_coef = 1.0 / (8.0 * math.pi)
eps_sq = 0.01
slab_width = 3.0
across_middle = 1.0
LANES = 128
FEATURES = 16

f32 = jnp.float32
bf16 = jnp.bfloat16


def split(value, terms):
    parts = []
    for _ in range(terms - 1):
        part = value.astype(bf16).astype(f32)
        parts.append(part)
        value = value - part
    parts.append(value)
    return parts


def features(x, f):
    norm = jnp.sum(x * x, axis=0, keepdims=True)
    along = jnp.sum(x * f, axis=0, keepdims=True)
    rows = [f] + [x[k : k + 1] * f for k in range(3)] + [norm * f + x * along]
    rows.append(jnp.zeros_like(norm))
    stacked = jnp.concatenate(rows, axis=0)
    return jnp.concatenate([part.astype(bf16) for part in split(stacked, 3)], axis=0)


def combine(sums, y):
    force = sums[0:3]
    moment = [sums[3 + 3 * k : 6 + 3 * k] for k in range(3)]
    second = sums[12:15]
    norm = jnp.sum(y * y, axis=0, keepdims=True)
    trace = moment[0][0:1] + moment[1][1:2] + moment[2][2:3]
    along = jnp.sum(y * force, axis=0, keepdims=True) - trace
    turned = jnp.concatenate(
        [jnp.sum(y * moment[k], axis=0, keepdims=True) for k in range(3)], axis=0
    )
    mixed = y[0:1] * moment[0] + y[1:2] * moment[1] + y[2:3] * moment[2]
    velocity = (norm + 2.0 * eps_sq) * force + second - 2.0 * mixed + y * along - turned
    return velocity * stokes_coef


def distances(x, y):
    columns = jnp.transpose(x)
    total = eps_sq
    for c in range(3):
        delta = columns[:, c : c + 1] - y[c : c + 1]
        total = delta * delta + total
    return total


def dot(left, right, left_dim, right_dim):
    return lax.dot_general(
        left, right, (((left_dim,), (right_dim,)), ((), ())), preferred_element_type=f32
    )


def fold(sums):
    return sums[0:FEATURES] + sums[FEATURES : 2 * FEATURES] + sums[2 * FEATURES :]


def weights(dist_sq):
    inverse = lax.rsqrt(dist_sq)
    cubed = inverse * inverse * inverse
    high = cubed.astype(bf16)
    low = (cubed - high.astype(f32)).astype(bf16)
    return high, low


def pair_velocities(cells):
    squares = [distances(xa, xb) for xa, _, xb, _ in cells]
    feats = [(features(xa, fa), features(xb, fb)) for xa, fa, xb, fb in cells]
    results = []
    waiting = []

    def finish():
        sums_a, sums_b, xa, xb = waiting.pop(0)
        results.append((combine(fold(sums_a), xa), combine(fold(sums_b), xb)))

    for square, (feat_a, feat_b), (xa, _, xb, _) in zip(squares, feats, cells):
        high, low = weights(square)
        rows = jnp.concatenate([high, low], axis=0)
        columns = jnp.concatenate([high, low], axis=1)
        sums_b = dot(jnp.concatenate([feat_a, feat_a], axis=1), rows, 1, 0)
        sums_a = dot(jnp.concatenate([feat_b, feat_b], axis=1), columns, 1, 1)
        waiting.append((sums_a, sums_b, xa, xb))
        if len(waiting) > 1:
            finish()
    finish()
    return results


def row_base(cell, tiles):
    return cell // 8 * (8 * tiles) + lax.rem(cell, 8)


def away_of(kind, odd):
    return (0, 1 - 2 * odd, 2 * odd - 1)[kind]


def pack_kernel(sizes, cells, count, pos_hbm, frc_hbm, *refs):
    n_space, n_pairs, share, cell_dev, tiles = sizes
    outs, table = refs[:n_pairs], refs[n_pairs]
    slots, used, pos, frc, sems = refs[n_pairs + 1 :]
    fetches = [
        pltpu.make_async_copy(pos_hbm, pos, sems.at[0]),
        pltpu.make_async_copy(frc_hbm, frc, sems.at[1]),
    ]
    for fetch in fetches:
        fetch.start()
    n_slots = cells.shape[1]
    owner = cells[0, 0] // cell_dev
    here = owner // n_pairs
    here_turn = lax.rem(owner, n_pairs)
    for bucket in range(3 * n_pairs):
        used[bucket] = 0
    for s in range(n_slots):
        owner = cells[1, s] // cell_dev
        there = owner // n_pairs
        turn = lax.rem(owner, n_pairs) ^ here_turn
        kind = jnp.where(there == here, 0, jnp.where(there // 2 == here // 2, 1, 2))
        bucket = kind * n_pairs + turn
        rank = used[bucket]
        used[bucket] = rank + 1
        slots[bucket * share + rank] = s
    for fetch in fetches:
        fetch.wait()
    lane = lax.broadcasted_iota(jnp.int32, (1, LANES), 1)
    plane = cell_dev * tiles
    for m in range(3 * n_pairs):
        kind, turn = m // n_pairs, m % n_pairs
        out = outs[turn]
        label = jnp.full((1, LANES), -1.0, f32)
        for k in range(share):
            s = slots[m * share + k]
            a = lax.rem(cells[0, s], cell_dev)
            live = s < count[0]
            b = jnp.where(live, lax.rem(cells[1, s], cell_dev), -1)
            table[m * share + k] = jnp.where(live, a, -1)
            label = jnp.where(lane == k, b.astype(f32), label)
            base = row_base(a, tiles)
            for c in range(6):
                source = pos if c < 3 else frc
                row = (k * 6 + c) * tiles
                out[kind, row : row + tiles, :] = source[
                    pl.ds(base + c % 3 * plane, tiles, stride=8), :
                ]
        last = share * 6 * tiles
        out[kind, last : last + 1, :] = label


def pair_kernel(sizes, kinds, started, extra, *refs):
    n_space, n_pairs, share, cell_dev, tiles = sizes
    n = len(kinds)
    refs = refs[extra:]
    messages, (pos, frc) = refs[:n], refs[n : n + 2]
    outs = refs[n + 2 + started :]
    (acc, reply), (inbox, todo, middles) = outs[:2], outs[-3:]
    rows_in = share * 6 * tiles
    plane = cell_dev * tiles
    if not started:
        acc[...] = jnp.zeros_like(acc)
        outs[2][...] = jnp.zeros_like(outs[2])
    here = lax.axis_index("space")
    number = jnp.int32(0)
    first = 0
    for kind, message in zip(kinds, messages):
        away = jnp.int32(away_of(kind, lax.rem(here, 2)))
        there = lax.rem(here + away + n_space, n_space)
        half = 0.5 * slab_width * away.astype(f32)
        middle_a = slab_width * (there.astype(f32) + 0.5) - half
        middle_b = slab_width * (here.astype(f32) + 0.5) + half
        for block in range(message.shape[0]):
            inbox[first * rows_in : (first + 1) * rows_in, :] = message[block, 0:rows_in, :]
            label = message[block, rows_in : rows_in + 1, :].astype(jnp.int32)
            for k in range(share):
                b = label[0, k]
                todo[0, number] = first * share + k
                todo[1, number] = b
                middles[0, number] = middle_a
                middles[1, number] = middle_b
                number = number + jnp.where(b >= 0, 1, 0)
            first += 1

    axis = lax.broadcasted_iota(jnp.int32, (3, 1), 0)

    def load(i):
        base = todo[0, i] * (6 * tiles)
        data = jnp.concatenate(
            [inbox[pl.ds(base + t, 6, stride=tiles), :] for t in range(tiles)], axis=1
        )
        start = row_base(todo[1, i], tiles)
        xb, fb = (
            jnp.concatenate(
                [ref[pl.ds(start + 8 * t, 3, stride=plane), :] for t in range(tiles)], axis=1
            )
            for ref in (pos, frc)
        )
        xa = data[0:3] - jnp.where(axis == 0, middles[0, i], across_middle)
        xb = xb - jnp.where(axis == 0, middles[1, i], across_middle)
        return xa, data[3:6], xb, fb

    def store(i, vel_a, vel_b):
        base = todo[0, i] * (3 * tiles)
        start = row_base(todo[1, i], tiles)
        parts = [slice(t * LANES, (t + 1) * LANES) for t in range(tiles)]
        places = [pl.ds(start + 8 * t, 3, stride=plane) for t in range(tiles)]
        totals = [acc[place, :] + vel_b[:, part] for place, part in zip(places, parts)]
        for t in range(tiles):
            acc[places[t], :] = totals[t]
            reply[pl.ds(base + t, 3, stride=tiles), :] = vel_a[:, parts[t]]

    def several(numbers):
        results = pair_velocities([load(i) for i in numbers])
        for i, result in zip(numbers, results):
            store(i, *result)

    def four(i, _):
        several([4 * i + j for j in range(4)])
        return 0

    lax.fori_loop(0, number // 4, four, 0)
    left = lax.rem(number, 4)

    @pl.when(left >= 2)
    def _():
        several([number - left, number - left + 1])

    @pl.when(lax.rem(left, 2) == 1)
    def _():
        several([number - 1])


def add_kernel(sizes, table, acc, *refs):
    n_space, n_pairs, share, cell_dev, tiles = sizes
    replies, out = refs[:-1], refs[-1]
    plane = cell_dev * tiles
    out[...] = acc[...]
    for m in range(3 * n_pairs):
        kind, turn = m // n_pairs, m % n_pairs
        for k in range(share):
            a = table[m * share + k]
            live = a >= 0
            base = row_base(jnp.maximum(a, 0), tiles)
            places = [pl.ds(base + c * plane, tiles, stride=8) for c in range(3)]
            totals = []
            for c in range(3):
                row = (k * 3 + c) * tiles
                term = jnp.where(live, replies[turn][kind, row : row + tiles, :], 0.0)
                totals.append(out[places[c], :] + term)
            for c in range(3):
                out[places[c], :] = totals[c]


def flat_rows(cells):
    count, _, points = cells.shape
    value = jnp.transpose(cells, (1, 0, 2)).reshape(3, count // 8, 8, points // LANES, LANES)
    return jnp.transpose(value, (0, 1, 3, 2, 4)).reshape(-1, LANES)


def cell_rows(rows, count, points):
    value = rows.reshape(3, count // 8, points // LANES, 8, LANES)
    value = jnp.transpose(value, (0, 1, 3, 2, 4)).reshape(3, count, points)
    return jnp.transpose(value, (1, 0, 2))


def body(positions, forces, pair_cells, pair_count):
    n_space = lax.axis_size("space")
    n_pairs = lax.axis_size("pairs")
    cell_dev, _, points = positions.shape
    n_slots = pair_cells.shape[1]
    share = n_slots // (3 * n_pairs)
    tiles = points // LANES
    sizes = (n_space, n_pairs, share, cell_dev, tiles)
    rows_in = share * 6 * tiles
    rows_out = share * 3 * tiles
    pos = flat_rows(positions)
    frc = flat_rows(forces)
    vmem = pl.BlockSpec(memory_space=pltpu.VMEM)
    smem = pl.BlockSpec(memory_space=pltpu.SMEM)
    hbm = pl.BlockSpec(memory_space=pltpu.HBM)
    message = jax.ShapeDtypeStruct((3, rows_in + 8, LANES), f32)
    total = jax.ShapeDtypeStruct((3 * cell_dev * tiles, LANES), f32)

    def across(value, turn):
        return lax.ppermute(value, "pairs", [(j, j ^ turn) for j in range(n_pairs)])

    def beyond(value, kind):
        moves = [(i, (i + away_of(kind, i % 2)) % n_space) for i in range(n_space)]
        return lax.ppermute(value, "space", moves)

    packed = pl.pallas_call(
        functools.partial(pack_kernel, sizes),
        out_shape=[message] * n_pairs + [jax.ShapeDtypeStruct((n_slots,), jnp.int32)],
        in_specs=[smem, smem, hbm, hbm],
        out_specs=[vmem] * n_pairs + [smem],
        scratch_shapes=[
            pltpu.SMEM((n_slots,), jnp.int32),
            pltpu.SMEM((3 * n_pairs,), jnp.int32),
            pltpu.VMEM(total.shape, f32),
            pltpu.VMEM(total.shape, f32),
            pltpu.SemaphoreType.DMA((2,)),
        ],
        compiler_params=pltpu.CompilerParams(vmem_limit_bytes=60 * 1024 * 1024),
        name="pack",
    )(pair_cells, pair_count, pos, frc)
    sent, table = packed[:n_pairs], packed[n_pairs]
    got = [sent[0]] + [across(sent[turn], turn) for turn in range(1, n_pairs)]

    def pairs(arrived, before, extra=()):
        kinds = [kind for kind, _ in arrived]
        values = [value for _, value in arrived]
        n = len(values)
        blocks = sum(value.shape[0] for value in values)
        return pl.pallas_call(
            functools.partial(pair_kernel, sizes, kinds, len(before), len(extra)),
            out_shape=[total, jax.ShapeDtypeStruct((blocks * rows_out, LANES), f32)]
            + [jax.ShapeDtypeStruct((1, LANES), f32)] * (not before),
            in_specs=[smem] * len(extra) + [vmem] * (n + 2 + len(before)),
            out_specs=[vmem] * (2 + (not before)),
            scratch_shapes=[
                pltpu.VMEM((blocks * rows_in, LANES), f32),
                pltpu.SMEM((2, blocks * share + 1), jnp.int32),
                pltpu.SMEM((2, blocks * share + 1), f32),
            ],
            input_output_aliases={len(extra) + n + 2: 0} if before else {},
            compiler_params=pltpu.CompilerParams(vmem_limit_bytes=48 * 1024 * 1024),
            cost_estimate=pl.CostEstimate(
                flops=blocks * 1_000_000_000, bytes_accessed=2_000_000, transcendentals=2_000_000
            ),
            name="pairs",
        )(*extra, *values, pos, frc, *before)

    near, far = range(2), range(2, n_pairs)
    own = [sent[0][kind : kind + 1] for kind in range(3)]
    core = [got[1][kind : kind + 1] for kind in range(3)]
    out_1n = beyond(jnp.concatenate([own[1], core[1]]), 1)
    acc, reply_0n, nothing = pairs([(0, own[0]), (0, core[0])], [])
    rest = [got[turn] + nothing[None] for turn in far]
    out_1f = beyond(jnp.stack([value[1] for value in rest]), 1)
    out_2 = beyond(jnp.concatenate([own[2], core[2]] + [value[2:] for value in rest]), 2)
    acc, reply_m = pairs(
        [(1, out_1n)] + [(0, got[turn][0:1]) for turn in far], [acc], [table]
    )
    acc, reply_f = pairs([(1, out_1f), (2, out_2)], [acc])
    reply_0n, reply_m, reply_f = (
        value.reshape(-1, rows_out, LANES) for value in (reply_0n, reply_m, reply_f)
    )
    cut = n_pairs - 2
    back_0 = jnp.concatenate([reply_0n, reply_m[2:]])
    back_1 = beyond(jnp.concatenate([reply_m[:2], reply_f[:cut]]), 1)
    back_2 = beyond(reply_f[cut:], 2)
    back = []
    for turn in range(n_pairs):
        value = jnp.stack([back_0[turn], back_1[turn], back_2[turn]])
        back.append(across(value, turn) if turn else value)
    velocity = pl.pallas_call(
        functools.partial(add_kernel, sizes),
        out_shape=total,
        in_specs=[smem] + [vmem] * (1 + n_pairs),
        out_specs=vmem,
        compiler_params=pltpu.CompilerParams(vmem_limit_bytes=48 * 1024 * 1024),
        name="add",
    )(table, acc, *back)
    return cell_rows(velocity, cell_dev, points)


def solution(mesh):
    placed = (
        P(("space", "pairs"), None, None),
        P(("space", "pairs"), None, None),
        P(None, ("space", "pairs")),
        P(("space", "pairs")),
    )
    return jax.shard_map(
        body,
        mesh=mesh,
        in_specs=placed,
        out_specs=P(("space", "pairs"), None, None),
        check_vma=False,
    )
```

```python
import functools
import math

import jax
import jax.numpy as jnp
from jax import lax
from jax.experimental import pallas as pl
from jax.experimental.pallas import tpu as pltpu
from jax.sharding import PartitionSpec as P

stokes_coef = 1.0 / (8.0 * math.pi)
eps_sq = 0.01
slab_width = 3.0
across_middle = 1.0
LANES = 128
FEATURES = 16
ROWS = 32

f32 = jnp.float32
bf16 = jnp.bfloat16


def split(value, terms):
    parts = []
    for _ in range(terms - 1):
        part = value.astype(bf16).astype(f32)
        parts.append(part)
        value = value - part
    parts.append(value)
    return parts


def features(x, f):
    norm = jnp.sum(x * x, axis=0, keepdims=True)
    along = jnp.sum(x * f, axis=0, keepdims=True)
    rows = [f] + [x[k : k + 1] * f for k in range(3)] + [norm * f + x * along]
    rows.append(jnp.zeros_like(norm))
    stacked = jnp.concatenate(rows, axis=0)
    return jnp.concatenate([part.astype(bf16) for part in split(stacked, 3)], axis=0)


def combine(sums, y):
    force = sums[0:3]
    moment = [sums[3 + 3 * k : 6 + 3 * k] for k in range(3)]
    second = sums[12:15]
    norm = jnp.sum(y * y, axis=0, keepdims=True)
    trace = moment[0][0:1] + moment[1][1:2] + moment[2][2:3]
    along = jnp.sum(y * force, axis=0, keepdims=True) - trace
    turned = jnp.concatenate(
        [jnp.sum(y * moment[k], axis=0, keepdims=True) for k in range(3)], axis=0
    )
    mixed = y[0:1] * moment[0] + y[1:2] * moment[1] + y[2:3] * moment[2]
    velocity = (norm + 2.0 * eps_sq) * force + second - 2.0 * mixed + y * along - turned
    return velocity * stokes_coef


def gram_factors(x, y):
    one = jnp.ones((1, x.shape[1]), f32)
    none = jnp.zeros((3, x.shape[1]), f32)
    norm_x = jnp.sum(x * x, axis=0, keepdims=True)
    norm_y = jnp.sum(y * y, axis=0, keepdims=True) + eps_sq
    left = split(jnp.concatenate([x, norm_x, one, none], axis=0), 3)
    right = split(jnp.concatenate([-2.0 * y, one, norm_y, none], axis=0), 3)
    order = ((0, 0), (0, 1), (1, 0), (0, 2), (1, 1), (2, 0))
    return (
        jnp.concatenate([left[p] for p, _ in order], axis=0).astype(bf16),
        jnp.concatenate([right[q] for _, q in order], axis=0).astype(bf16),
    )


def dot(left, right, left_dim, right_dim):
    return lax.dot_general(
        left, right, (((left_dim,), (right_dim,)), ((), ())), preferred_element_type=f32
    )


def fold(sums):
    return sums[0:FEATURES] + sums[FEATURES : 2 * FEATURES] + sums[2 * FEATURES :]


def weights(dist_sq, out):
    for start in range(0, dist_sq.shape[0], ROWS):
        rows = slice(start, start + ROWS)
        inverse = lax.rsqrt(dist_sq[rows])
        cubed = inverse * inverse * inverse
        high = cubed.astype(bf16)
        out[0, rows, :] = high
        out[1, rows, :] = (cubed - high.astype(f32)).astype(bf16)


def pair_velocities(cells, kept):
    grams = [dot(*gram_factors(xa, xb), 0, 0) for xa, _, xb, _ in cells]
    feats = [(features(xa, fa), features(xb, fb)) for xa, fa, xb, fb in cells]
    results = []
    waiting = []

    def finish():
        sums_a, sums_b, xa, xb = waiting.pop(0)
        results.append((combine(fold(sums_a), xa), combine(fold(sums_b), xb)))

    for i, (gram, (feat_a, feat_b), (xa, _, xb, _)) in enumerate(zip(grams, feats, cells)):
        weights(gram, kept.at[i])
        rows = jnp.concatenate([kept[i, 0], kept[i, 1]], axis=0)
        columns = jnp.concatenate([kept[i, 0], kept[i, 1]], axis=1)
        sums_b = dot(jnp.concatenate([feat_a, feat_a], axis=1), rows, 1, 0)
        sums_a = dot(jnp.concatenate([feat_b, feat_b], axis=1), columns, 1, 1)
        waiting.append((sums_a, sums_b, xa, xb))
        if len(waiting) > 1:
            finish()
    finish()
    return results


def row_base(cell, tiles):
    return cell // 8 * (8 * tiles) + lax.rem(cell, 8)


def away_of(kind, odd):
    return (0, 1 - 2 * odd, 2 * odd - 1)[kind]


def pack_kernel(sizes, cells, count, pos_hbm, frc_hbm, *refs):
    n_space, n_pairs, share, cell_dev, tiles = sizes
    outs, table = refs[:n_pairs], refs[n_pairs]
    slots, used, pos, frc, sems = refs[n_pairs + 1 :]
    fetches = [
        pltpu.make_async_copy(pos_hbm, pos, sems.at[0]),
        pltpu.make_async_copy(frc_hbm, frc, sems.at[1]),
    ]
    for fetch in fetches:
        fetch.start()
    n_slots = cells.shape[1]
    owner = cells[0, 0] // cell_dev
    here = owner // n_pairs
    here_turn = lax.rem(owner, n_pairs)
    for bucket in range(3 * n_pairs):
        used[bucket] = 0
    for s in range(n_slots):
        owner = cells[1, s] // cell_dev
        there = owner // n_pairs
        turn = lax.rem(owner, n_pairs) ^ here_turn
        kind = jnp.where(there == here, 0, jnp.where(there // 2 == here // 2, 1, 2))
        bucket = kind * n_pairs + turn
        rank = used[bucket]
        used[bucket] = rank + 1
        slots[bucket * share + rank] = s
    for fetch in fetches:
        fetch.wait()
    lane = lax.broadcasted_iota(jnp.int32, (1, LANES), 1)
    plane = cell_dev * tiles
    for m in range(3 * n_pairs):
        kind, turn = m // n_pairs, m % n_pairs
        out = outs[turn]
        label = jnp.full((1, LANES), -1.0, f32)
        for k in range(share):
            s = slots[m * share + k]
            a = lax.rem(cells[0, s], cell_dev)
            live = s < count[0]
            b = jnp.where(live, lax.rem(cells[1, s], cell_dev), -1)
            table[m * share + k] = jnp.where(live, a, -1)
            label = jnp.where(lane == k, b.astype(f32), label)
            base = row_base(a, tiles)
            for c in range(6):
                source = pos if c < 3 else frc
                row = (k * 6 + c) * tiles
                out[kind, row : row + tiles, :] = source[
                    pl.ds(base + c % 3 * plane, tiles, stride=8), :
                ]
        last = share * 6 * tiles
        out[kind, last : last + 1, :] = label


def pair_kernel(sizes, kinds, started, extra, *refs):
    n_space, n_pairs, share, cell_dev, tiles = sizes
    n = len(kinds)
    refs = refs[extra:]
    messages, (pos, frc) = refs[:n], refs[n : n + 2]
    outs = refs[n + 2 + started :]
    (acc, reply), (inbox, kept, todo, middles) = outs[:2], outs[-4:]
    rows_in = share * 6 * tiles
    plane = cell_dev * tiles
    if not started:
        acc[...] = jnp.zeros_like(acc)
        outs[2][...] = jnp.zeros_like(outs[2])
    here = lax.axis_index("space")
    number = jnp.int32(0)
    first = 0
    for kind, message in zip(kinds, messages):
        away = jnp.int32(away_of(kind, lax.rem(here, 2)))
        there = lax.rem(here + away + n_space, n_space)
        half = 0.5 * slab_width * away.astype(f32)
        middle_a = slab_width * (there.astype(f32) + 0.5) - half
        middle_b = slab_width * (here.astype(f32) + 0.5) + half
        for block in range(message.shape[0]):
            inbox[first * rows_in : (first + 1) * rows_in, :] = message[block, 0:rows_in, :]
            label = message[block, rows_in : rows_in + 1, :].astype(jnp.int32)
            for k in range(share):
                b = label[0, k]
                todo[0, number] = first * share + k
                todo[1, number] = b
                middles[0, number] = middle_a
                middles[1, number] = middle_b
                number = number + jnp.where(b >= 0, 1, 0)
            first += 1

    axis = lax.broadcasted_iota(jnp.int32, (3, 1), 0)

    def load(i):
        base = todo[0, i] * (6 * tiles)
        data = jnp.concatenate(
            [inbox[pl.ds(base + t, 6, stride=tiles), :] for t in range(tiles)], axis=1
        )
        start = row_base(todo[1, i], tiles)
        xb, fb = (
            jnp.concatenate(
                [ref[pl.ds(start + 8 * t, 3, stride=plane), :] for t in range(tiles)], axis=1
            )
            for ref in (pos, frc)
        )
        xa = data[0:3] - jnp.where(axis == 0, middles[0, i], across_middle)
        xb = xb - jnp.where(axis == 0, middles[1, i], across_middle)
        return xa, data[3:6], xb, fb

    def store(i, vel_a, vel_b):
        base = todo[0, i] * (3 * tiles)
        start = row_base(todo[1, i], tiles)
        parts = [slice(t * LANES, (t + 1) * LANES) for t in range(tiles)]
        places = [pl.ds(start + 8 * t, 3, stride=plane) for t in range(tiles)]
        totals = [acc[place, :] + vel_b[:, part] for place, part in zip(places, parts)]
        for t in range(tiles):
            acc[places[t], :] = totals[t]
            reply[pl.ds(base + t, 3, stride=tiles), :] = vel_a[:, parts[t]]

    def several(numbers):
        results = pair_velocities([load(i) for i in numbers], kept)
        for i, result in zip(numbers, results):
            store(i, *result)

    def four(i, _):
        several([4 * i + j for j in range(4)])
        return 0

    lax.fori_loop(0, number // 4, four, 0)
    left = lax.rem(number, 4)

    @pl.when(left >= 2)
    def _():
        several([number - left, number - left + 1])

    @pl.when(lax.rem(left, 2) == 1)
    def _():
        several([number - 1])


def add_kernel(sizes, table, acc, *refs):
    n_space, n_pairs, share, cell_dev, tiles = sizes
    replies, out = refs[:-1], refs[-1]
    plane = cell_dev * tiles
    out[...] = acc[...]
    for m in range(3 * n_pairs):
        kind, turn = m // n_pairs, m % n_pairs
        for k in range(share):
            a = table[m * share + k]
            live = a >= 0
            base = row_base(jnp.maximum(a, 0), tiles)
            places = [pl.ds(base + c * plane, tiles, stride=8) for c in range(3)]
            totals = []
            for c in range(3):
                row = (k * 3 + c) * tiles
                term = jnp.where(live, replies[turn][kind, row : row + tiles, :], 0.0)
                totals.append(out[places[c], :] + term)
            for c in range(3):
                out[places[c], :] = totals[c]


def flat_rows(cells):
    count, _, points = cells.shape
    value = jnp.transpose(cells, (1, 0, 2)).reshape(3, count // 8, 8, points // LANES, LANES)
    return jnp.transpose(value, (0, 1, 3, 2, 4)).reshape(-1, LANES)


def cell_rows(rows, count, points):
    value = rows.reshape(3, count // 8, points // LANES, 8, LANES)
    value = jnp.transpose(value, (0, 1, 3, 2, 4)).reshape(3, count, points)
    return jnp.transpose(value, (1, 0, 2))


def body(positions, forces, pair_cells, pair_count):
    n_space = lax.axis_size("space")
    n_pairs = lax.axis_size("pairs")
    cell_dev, _, points = positions.shape
    n_slots = pair_cells.shape[1]
    share = n_slots // (3 * n_pairs)
    tiles = points // LANES
    sizes = (n_space, n_pairs, share, cell_dev, tiles)
    rows_in = share * 6 * tiles
    rows_out = share * 3 * tiles
    pos = flat_rows(positions)
    frc = flat_rows(forces)
    vmem = pl.BlockSpec(memory_space=pltpu.VMEM)
    smem = pl.BlockSpec(memory_space=pltpu.SMEM)
    hbm = pl.BlockSpec(memory_space=pltpu.HBM)
    message = jax.ShapeDtypeStruct((3, rows_in + 8, LANES), f32)
    total = jax.ShapeDtypeStruct((3 * cell_dev * tiles, LANES), f32)

    def across(value, turn):
        return lax.ppermute(value, "pairs", [(j, j ^ turn) for j in range(n_pairs)])

    def beyond(value, kind):
        moves = [(i, (i + away_of(kind, i % 2)) % n_space) for i in range(n_space)]
        return lax.ppermute(value, "space", moves)

    packed = pl.pallas_call(
        functools.partial(pack_kernel, sizes),
        out_shape=[message] * n_pairs + [jax.ShapeDtypeStruct((n_slots,), jnp.int32)],
        in_specs=[smem, smem, hbm, hbm],
        out_specs=[vmem] * n_pairs + [smem],
        scratch_shapes=[
            pltpu.SMEM((n_slots,), jnp.int32),
            pltpu.SMEM((3 * n_pairs,), jnp.int32),
            pltpu.VMEM(total.shape, f32),
            pltpu.VMEM(total.shape, f32),
            pltpu.SemaphoreType.DMA((2,)),
        ],
        compiler_params=pltpu.CompilerParams(vmem_limit_bytes=60 * 1024 * 1024),
        name="pack",
    )(pair_cells, pair_count, pos, frc)
    sent, table = packed[:n_pairs], packed[n_pairs]
    got = [sent[0]] + [across(sent[turn], turn) for turn in range(1, n_pairs)]

    def pairs(arrived, before, extra=()):
        kinds = [kind for kind, _ in arrived]
        values = [value for _, value in arrived]
        n = len(values)
        blocks = sum(value.shape[0] for value in values)
        return pl.pallas_call(
            functools.partial(pair_kernel, sizes, kinds, len(before), len(extra)),
            out_shape=[total, jax.ShapeDtypeStruct((blocks * rows_out, LANES), f32)]
            + [jax.ShapeDtypeStruct((1, LANES), f32)] * (not before),
            in_specs=[smem] * len(extra) + [vmem] * (n + 2 + len(before)),
            out_specs=[vmem] * (2 + (not before)),
            scratch_shapes=[
                pltpu.VMEM((blocks * rows_in, LANES), f32),
                pltpu.VMEM((4, 2, points, points), bf16),
                pltpu.SMEM((2, blocks * share + 1), jnp.int32),
                pltpu.SMEM((2, blocks * share + 1), f32),
            ],
            input_output_aliases={len(extra) + n + 2: 0} if before else {},
            compiler_params=pltpu.CompilerParams(vmem_limit_bytes=48 * 1024 * 1024),
            cost_estimate=pl.CostEstimate(
                flops=blocks * 1_000_000_000, bytes_accessed=2_000_000, transcendentals=2_000_000
            ),
            name="pairs",
        )(*extra, *values, pos, frc, *before)

    near, far = range(2), range(2, n_pairs)
    own = [sent[0][kind : kind + 1] for kind in range(3)]
    core = [got[1][kind : kind + 1] for kind in range(3)]
    out_1n = beyond(jnp.concatenate([own[1], core[1]]), 1)
    acc, reply_0n, nothing = pairs([(0, own[0]), (0, core[0])], [])
    rest = [got[turn] + nothing[None] for turn in far]
    out_1f = beyond(jnp.stack([value[1] for value in rest]), 1)
    out_2 = beyond(jnp.concatenate([own[2], core[2]] + [value[2:] for value in rest]), 2)
    acc, reply_m = pairs(
        [(1, out_1n)] + [(0, got[turn][0:1]) for turn in far], [acc], [table]
    )
    acc, reply_f = pairs([(1, out_1f), (2, out_2)], [acc])
    reply_0n, reply_m, reply_f = (
        value.reshape(-1, rows_out, LANES) for value in (reply_0n, reply_m, reply_f)
    )
    cut = n_pairs - 2
    back_0 = jnp.concatenate([reply_0n, reply_m[2:]])
    back_1 = beyond(jnp.concatenate([reply_m[:2], reply_f[:cut]]), 1)
    back_2 = beyond(reply_f[cut:], 2)
    back = []
    for turn in range(n_pairs):
        value = jnp.stack([back_0[turn], back_1[turn], back_2[turn]])
        back.append(across(value, turn) if turn else value)
    velocity = pl.pallas_call(
        functools.partial(add_kernel, sizes),
        out_shape=total,
        in_specs=[smem] + [vmem] * (1 + n_pairs),
        out_specs=vmem,
        compiler_params=pltpu.CompilerParams(vmem_limit_bytes=48 * 1024 * 1024),
        name="add",
    )(table, acc, *back)
    return cell_rows(velocity, cell_dev, points)


def solution(mesh):
    placed = (
        P(("space", "pairs"), None, None),
        P(("space", "pairs"), None, None),
        P(None, ("space", "pairs")),
        P(("space", "pairs")),
    )
    return jax.shard_map(
        body,
        mesh=mesh,
        in_specs=placed,
        out_specs=P(("space", "pairs"), None, None),
        check_vma=False,
    )
```

```python
import functools
import math

import jax
import jax.numpy as jnp
from jax import lax
from jax.experimental import pallas as pl
from jax.experimental.pallas import tpu as pltpu
from jax.sharding import PartitionSpec as P

stokes_coef = 1.0 / (8.0 * math.pi)
eps_sq = 0.01
slab_width = 3.0
across_middle = 1.0
LANES = 128
FEATURES = 16

f32 = jnp.float32
bf16 = jnp.bfloat16


def split(value, terms):
    parts = []
    for _ in range(terms - 1):
        part = value.astype(bf16).astype(f32)
        parts.append(part)
        value = value - part
    parts.append(value)
    return parts


def features(x, f):
    norm = jnp.sum(x * x, axis=0, keepdims=True)
    along = jnp.sum(x * f, axis=0, keepdims=True)
    rows = [f] + [x[k : k + 1] * f for k in range(3)] + [norm * f + x * along]
    rows.append(jnp.zeros_like(norm))
    stacked = jnp.concatenate(rows, axis=0)
    return jnp.concatenate([part.astype(bf16) for part in split(stacked, 3)], axis=0)


def combine(sums, y):
    force = sums[0:3]
    moment = [sums[3 + 3 * k : 6 + 3 * k] for k in range(3)]
    second = sums[12:15]
    norm = jnp.sum(y * y, axis=0, keepdims=True)
    trace = moment[0][0:1] + moment[1][1:2] + moment[2][2:3]
    along = jnp.sum(y * force, axis=0, keepdims=True) - trace
    turned = jnp.concatenate(
        [jnp.sum(y * moment[k], axis=0, keepdims=True) for k in range(3)], axis=0
    )
    mixed = y[0:1] * moment[0] + y[1:2] * moment[1] + y[2:3] * moment[2]
    velocity = (norm + 2.0 * eps_sq) * force + second - 2.0 * mixed + y * along - turned
    return velocity * stokes_coef


def gram_factors(x, y):
    one = jnp.ones((1, x.shape[1]), f32)
    none = jnp.zeros((3, x.shape[1]), f32)
    norm_x = jnp.sum(x * x, axis=0, keepdims=True)
    norm_y = jnp.sum(y * y, axis=0, keepdims=True) + eps_sq
    left = split(jnp.concatenate([x, norm_x, one, none], axis=0), 3)
    right = split(jnp.concatenate([-2.0 * y, one, norm_y, none], axis=0), 3)
    order = ((0, 0), (0, 1), (1, 0), (0, 2), (1, 1), (2, 0))
    return (
        jnp.concatenate([left[p] for p, _ in order], axis=0).astype(bf16),
        jnp.concatenate([right[q] for _, q in order], axis=0).astype(bf16),
    )


def dot(left, right, left_dim, right_dim):
    return lax.dot_general(
        left, right, (((left_dim,), (right_dim,)), ((), ())), preferred_element_type=f32
    )


def fold(sums):
    return sums[0:FEATURES] + sums[FEATURES : 2 * FEATURES] + sums[2 * FEATURES :]


def weights(dist_sq):
    inverse = lax.rsqrt(dist_sq)
    cubed = inverse * inverse * inverse
    high = cubed.astype(bf16)
    low = (cubed - high.astype(f32)).astype(bf16)
    return high, low


def pair_velocities(cells):
    grams = [dot(*gram_factors(xa, xb), 0, 0) for xa, _, xb, _ in cells]
    feats = [(features(xa, fa), features(xb, fb)) for xa, fa, xb, fb in cells]
    results = []
    waiting = []

    def finish():
        sums_a, sums_b, xa, xb = waiting.pop(0)
        results.append((combine(fold(sums_a), xa), combine(fold(sums_b), xb)))

    for gram, (feat_a, feat_b), (xa, _, xb, _) in zip(grams, feats, cells):
        high, low = weights(gram)
        rows = jnp.concatenate([high, low], axis=0)
        columns = jnp.concatenate([high, low], axis=1)
        sums_b = dot(jnp.concatenate([feat_a, feat_a], axis=1), rows, 1, 0)
        sums_a = dot(jnp.concatenate([feat_b, feat_b], axis=1), columns, 1, 1)
        waiting.append((sums_a, sums_b, xa, xb))
        if len(waiting) > 1:
            finish()
    finish()
    return results


def row_base(cell, tiles):
    return cell // 8 * (8 * tiles) + lax.rem(cell, 8)


def away_of(kind, odd):
    return (0, 1 - 2 * odd, 2 * odd - 1)[kind]


def pack_kernel(sizes, cells, count, pos_hbm, frc_hbm, *refs):
    n_space, n_pairs, share, cell_dev, tiles = sizes
    outs = refs[:n_pairs]
    slots, used, pos, frc, sems = refs[n_pairs:]
    fetches = [
        pltpu.make_async_copy(pos_hbm, pos, sems.at[0]),
        pltpu.make_async_copy(frc_hbm, frc, sems.at[1]),
    ]
    for fetch in fetches:
        fetch.start()
    n_slots = cells.shape[1]
    owner = cells[0, 0] // cell_dev
    here = owner // n_pairs
    here_turn = lax.rem(owner, n_pairs)
    for bucket in range(3 * n_pairs):
        used[bucket] = 0
    for s in range(n_slots):
        owner = cells[1, s] // cell_dev
        there = owner // n_pairs
        turn = lax.rem(owner, n_pairs) ^ here_turn
        kind = jnp.where(there == here, 0, jnp.where(there // 2 == here // 2, 1, 2))
        bucket = kind * n_pairs + turn
        rank = used[bucket]
        used[bucket] = rank + 1
        slots[bucket * share + rank] = s
    for fetch in fetches:
        fetch.wait()
    lane = lax.broadcasted_iota(jnp.int32, (1, LANES), 1)
    plane = cell_dev * tiles
    last = share * 6 * tiles
    table = jnp.full((1, LANES), -1.0, f32)
    for m in range(3 * n_pairs):
        kind, turn = m // n_pairs, m % n_pairs
        out = outs[turn]
        label = jnp.full((1, LANES), -1.0, f32)
        for k in range(share):
            s = slots[m * share + k]
            a = lax.rem(cells[0, s], cell_dev)
            live = s < count[0]
            b = jnp.where(live, lax.rem(cells[1, s], cell_dev), -1)
            table = jnp.where(lane == m * share + k, jnp.where(live, a, -1).astype(f32), table)
            label = jnp.where(lane == k, b.astype(f32), label)
            base = row_base(a, tiles)
            for c in range(6):
                source = pos if c < 3 else frc
                row = (k * 6 + c) * tiles
                out[kind, row : row + tiles, :] = source[
                    pl.ds(base + c % 3 * plane, tiles, stride=8), :
                ]
        out[kind, last : last + 1, :] = label
    outs[0][0, last + 1 : last + 2, :] = table


def pair_kernel(sizes, kinds, started, marked, *refs):
    n_space, n_pairs, share, cell_dev, tiles = sizes
    n = len(kinds)
    messages, (pos, frc) = refs[:n], refs[n : n + 2]
    outs = refs[n + 2 + started :]
    (acc, reply), (inbox, todo, middles) = outs[:2], outs[-3:]
    rows_in = share * 6 * tiles
    plane = cell_dev * tiles
    if not started:
        acc[...] = jnp.zeros_like(acc)
    if marked:
        outs[2][...] = jnp.zeros_like(outs[2])
    here = lax.axis_index("space")
    number = jnp.int32(0)
    first = 0
    for kind, message in zip(kinds, messages):
        away = jnp.int32(away_of(kind, lax.rem(here, 2)))
        there = lax.rem(here + away + n_space, n_space)
        half = 0.5 * slab_width * away.astype(f32)
        middle_a = slab_width * (there.astype(f32) + 0.5) - half
        middle_b = slab_width * (here.astype(f32) + 0.5) + half
        for block in range(message.shape[0]):
            inbox[first * rows_in : (first + 1) * rows_in, :] = message[block, 0:rows_in, :]
            label = message[block, rows_in : rows_in + 1, :].astype(jnp.int32)
            for k in range(share):
                b = label[0, k]
                todo[0, number] = first * share + k
                todo[1, number] = b
                middles[0, number] = middle_a
                middles[1, number] = middle_b
                number = number + jnp.where(b >= 0, 1, 0)
            first += 1

    axis = lax.broadcasted_iota(jnp.int32, (3, 1), 0)

    def load(i):
        base = todo[0, i] * (6 * tiles)
        data = jnp.concatenate(
            [inbox[pl.ds(base + t, 6, stride=tiles), :] for t in range(tiles)], axis=1
        )
        start = row_base(todo[1, i], tiles)
        xb, fb = (
            jnp.concatenate(
                [ref[pl.ds(start + 8 * t, 3, stride=plane), :] for t in range(tiles)], axis=1
            )
            for ref in (pos, frc)
        )
        xa = data[0:3] - jnp.where(axis == 0, middles[0, i], across_middle)
        xb = xb - jnp.where(axis == 0, middles[1, i], across_middle)
        return xa, data[3:6], xb, fb

    def store(i, vel_a, vel_b):
        base = todo[0, i] * (3 * tiles)
        start = row_base(todo[1, i], tiles)
        parts = [slice(t * LANES, (t + 1) * LANES) for t in range(tiles)]
        places = [pl.ds(start + 8 * t, 3, stride=plane) for t in range(tiles)]
        totals = [acc[place, :] + vel_b[:, part] for place, part in zip(places, parts)]
        for t in range(tiles):
            acc[places[t], :] = totals[t]
            reply[pl.ds(base + t, 3, stride=tiles), :] = vel_a[:, parts[t]]

    def several(numbers):
        results = pair_velocities([load(i) for i in numbers])
        for i, result in zip(numbers, results):
            store(i, *result)

    def four(i, _):
        several([4 * i + j for j in range(4)])
        return 0

    lax.fori_loop(0, number // 4, four, 0)
    left = lax.rem(number, 4)

    @pl.when(left >= 2)
    def _():
        several([number - left, number - left + 1])

    @pl.when(lax.rem(left, 2) == 1)
    def _():
        several([number - 1])


def add_kernel(sizes, where, acc, mine, *refs):
    n_space, n_pairs, share, cell_dev, tiles = sizes
    replies, out = refs[:-1], refs[-1]
    plane = cell_dev * tiles
    last = share * 6 * tiles
    table = mine[0, last + 1 : last + 2, :].astype(jnp.int32)
    out[...] = acc[...]
    for m, (operand, block) in enumerate(where):
        for k in range(share):
            a = table[0, m * share + k]
            live = a >= 0
            base = row_base(jnp.maximum(a, 0), tiles)
            places = [pl.ds(base + c * plane, tiles, stride=8) for c in range(3)]
            totals = []
            for c in range(3):
                row = (k * 3 + c) * tiles
                term = jnp.where(live, replies[operand][block, row : row + tiles, :], 0.0)
                totals.append(out[places[c], :] + term)
            for c in range(3):
                out[places[c], :] = totals[c]


def flat_rows(cells):
    count, _, points = cells.shape
    value = jnp.transpose(cells, (1, 0, 2)).reshape(3, count // 8, 8, points // LANES, LANES)
    return jnp.transpose(value, (0, 1, 3, 2, 4)).reshape(-1, LANES)


def cell_rows(rows, count, points):
    value = rows.reshape(3, count // 8, points // LANES, 8, LANES)
    value = jnp.transpose(value, (0, 1, 3, 2, 4)).reshape(3, count, points)
    return jnp.transpose(value, (1, 0, 2))


def body(positions, forces, pair_cells, pair_count):
    n_space = lax.axis_size("space")
    n_pairs = lax.axis_size("pairs")
    cell_dev, _, points = positions.shape
    n_slots = pair_cells.shape[1]
    share = n_slots // (3 * n_pairs)
    tiles = points // LANES
    sizes = (n_space, n_pairs, share, cell_dev, tiles)
    rows_in = share * 6 * tiles
    rows_out = share * 3 * tiles
    pos = flat_rows(positions)
    frc = flat_rows(forces)
    vmem = pl.BlockSpec(memory_space=pltpu.VMEM)
    smem = pl.BlockSpec(memory_space=pltpu.SMEM)
    hbm = pl.BlockSpec(memory_space=pltpu.HBM)
    message = jax.ShapeDtypeStruct((3, rows_in + 8, LANES), f32)
    total = jax.ShapeDtypeStruct((3 * cell_dev * tiles, LANES), f32)

    def across(value, turn):
        return lax.ppermute(value, "pairs", [(j, j ^ turn) for j in range(n_pairs)])

    def beyond(value, kind):
        moves = [(i, (i + away_of(kind, i % 2)) % n_space) for i in range(n_space)]
        return lax.ppermute(value, "space", moves)

    sent = pl.pallas_call(
        functools.partial(pack_kernel, sizes),
        out_shape=[message] * n_pairs,
        in_specs=[smem, smem, hbm, hbm],
        out_specs=[vmem] * n_pairs,
        scratch_shapes=[
            pltpu.SMEM((n_slots,), jnp.int32),
            pltpu.SMEM((3 * n_pairs,), jnp.int32),
            pltpu.VMEM(total.shape, f32),
            pltpu.VMEM(total.shape, f32),
            pltpu.SemaphoreType.DMA((2,)),
        ],
        compiler_params=pltpu.CompilerParams(vmem_limit_bytes=60 * 1024 * 1024),
        name="pack",
    )(pair_cells, pair_count, pos, frc)
    got = [sent[0]] + [across(sent[turn], turn) for turn in range(1, n_pairs)]

    def pairs(arrived, before, marked=False):
        kinds = [kind for kind, _ in arrived]
        values = [value for _, value in arrived]
        n = len(values)
        blocks = sum(value.shape[0] for value in values)
        return pl.pallas_call(
            functools.partial(pair_kernel, sizes, kinds, len(before), marked),
            out_shape=[total, jax.ShapeDtypeStruct((blocks * rows_out, LANES), f32)]
            + [jax.ShapeDtypeStruct((1, LANES), f32)] * marked,
            in_specs=[vmem] * (n + 2 + len(before)),
            out_specs=[vmem] * (2 + marked),
            scratch_shapes=[
                pltpu.VMEM((blocks * rows_in, LANES), f32),
                pltpu.SMEM((2, blocks * share + 1), jnp.int32),
                pltpu.SMEM((2, blocks * share + 1), f32),
            ],
            input_output_aliases={n + 2: 0} if before else {},
            compiler_params=pltpu.CompilerParams(vmem_limit_bytes=48 * 1024 * 1024),
            cost_estimate=pl.CostEstimate(
                flops=blocks * 1_000_000_000, bytes_accessed=2_000_000, transcendentals=2_000_000
            ),
            name="pairs",
        )(*values, pos, frc, *before)

    near, far = range(2), range(2, n_pairs)
    own = [sent[0][kind : kind + 1] for kind in range(3)]
    core = [got[1][kind : kind + 1] for kind in range(3)]
    out_1n = beyond(jnp.concatenate([own[1], core[1]]), 1)
    acc, reply_0n, nothing = pairs([(0, own[0]), (0, core[0])], [], True)
    rest = [got[turn] + nothing[None] for turn in far]
    out_1f = beyond(jnp.stack([value[1] for value in rest]), 1)
    out_2 = beyond(jnp.concatenate([own[2], core[2]] + [value[2:] for value in rest]), 2)
    acc, reply_m = pairs([(1, out_1n)] + [(0, got[turn][0:1]) for turn in far], [acc])
    acc, reply_f, later = pairs([(1, out_1f), (2, out_2)], [acc], True)
    reply_0n, reply_m, reply_f = (
        value.reshape(-1, rows_out, LANES) for value in (reply_0n, reply_m, reply_f)
    )
    cut = n_pairs - 2
    back_1n = beyond(reply_m[:2] + later[None], 1)
    back_2n = beyond(reply_f[cut : cut + 2], 2)
    home = [
        across(jnp.stack([reply_m[turn], reply_f[turn - 2], reply_f[cut + turn]]), turn)
        for turn in far
    ]
    back_1f = beyond(jnp.stack([value[1] for value in home]), 1)
    back_2f = beyond(jnp.stack([value[2] for value in home]), 2)
    core = across(jnp.stack([reply_0n[1], back_1n[1], back_2n[1]]), 1)
    mine = jnp.stack([reply_0n[0], back_1n[0], back_2n[0]])
    replies = [mine, core, back_1f, back_2f] + home
    where = [(0, 0), (1, 0)] + [(2 + turn, 0) for turn in far]
    where += [(0, 1), (1, 1)] + [(2, turn - 2) for turn in far]
    where += [(0, 2), (1, 2)] + [(3, turn - 2) for turn in far]
    velocity = pl.pallas_call(
        functools.partial(add_kernel, sizes, where),
        out_shape=total,
        in_specs=[vmem] * (2 + len(replies)),
        out_specs=vmem,
        compiler_params=pltpu.CompilerParams(vmem_limit_bytes=48 * 1024 * 1024),
        name="add",
    )(acc, own[0], *replies)
    return cell_rows(velocity, cell_dev, points)


def solution(mesh):
    placed = (
        P(("space", "pairs"), None, None),
        P(("space", "pairs"), None, None),
        P(None, ("space", "pairs")),
        P(("space", "pairs")),
    )
    return jax.shard_map(
        body,
        mesh=mesh,
        in_specs=placed,
        out_specs=P(("space", "pairs"), None, None),
        check_vma=False,
    )
```

```python
import functools
import math

import jax
import jax.numpy as jnp
from jax import lax
from jax.experimental import pallas as pl
from jax.experimental.pallas import tpu as pltpu
from jax.sharding import PartitionSpec as P

stokes_coef = 1.0 / (8.0 * math.pi)
eps_sq = 0.01
slab_width = 3.0
across_middle = 1.0
LANES = 128
FEATURES = 16

f32 = jnp.float32
bf16 = jnp.bfloat16


def split(value, terms):
    parts = []
    for _ in range(terms - 1):
        part = value.astype(bf16).astype(f32)
        parts.append(part)
        value = value - part
    parts.append(value)
    return parts


def features(x, f):
    norm = jnp.sum(x * x, axis=0, keepdims=True)
    along = jnp.sum(x * f, axis=0, keepdims=True)
    rows = [f] + [x[k : k + 1] * f for k in range(3)] + [norm * f + x * along]
    rows.append(jnp.zeros_like(norm))
    stacked = jnp.concatenate(rows, axis=0)
    return jnp.concatenate([part.astype(bf16) for part in split(stacked, 3)], axis=0)


def combine(sums, y):
    force = sums[0:3]
    moment = [sums[3 + 3 * k : 6 + 3 * k] for k in range(3)]
    second = sums[12:15]
    norm = jnp.sum(y * y, axis=0, keepdims=True)
    trace = moment[0][0:1] + moment[1][1:2] + moment[2][2:3]
    along = jnp.sum(y * force, axis=0, keepdims=True) - trace
    turned = jnp.concatenate(
        [jnp.sum(y * moment[k], axis=0, keepdims=True) for k in range(3)], axis=0
    )
    mixed = y[0:1] * moment[0] + y[1:2] * moment[1] + y[2:3] * moment[2]
    velocity = (norm + 2.0 * eps_sq) * force + second - 2.0 * mixed + y * along - turned
    return velocity * stokes_coef


def gram_factors(x, y):
    one = jnp.ones((1, x.shape[1]), f32)
    none = jnp.zeros((3, x.shape[1]), f32)
    norm_x = jnp.sum(x * x, axis=0, keepdims=True)
    norm_y = jnp.sum(y * y, axis=0, keepdims=True) + eps_sq
    left = split(jnp.concatenate([x, norm_x, one, none], axis=0), 3)
    right = split(jnp.concatenate([-2.0 * y, one, norm_y, none], axis=0), 3)
    order = ((0, 0), (0, 1), (1, 0), (0, 2), (1, 1), (2, 0))
    return (
        jnp.concatenate([left[p] for p, _ in order], axis=0).astype(bf16),
        jnp.concatenate([right[q] for _, q in order], axis=0).astype(bf16),
    )


def dot(left, right, left_dim, right_dim):
    return lax.dot_general(
        left, right, (((left_dim,), (right_dim,)), ((), ())), preferred_element_type=f32
    )


def fold(sums):
    return sums[0:FEATURES] + sums[FEATURES : 2 * FEATURES] + sums[2 * FEATURES :]


def weights(dist_sq):
    inverse = lax.rsqrt(dist_sq)
    cubed = inverse * inverse * inverse
    high = cubed.astype(bf16)
    low = (cubed - high.astype(f32)).astype(bf16)
    return high, low


def pair_velocities(cells):
    grams = [dot(*gram_factors(xa, xb), 0, 0) for xa, _, xb, _ in cells]
    feats = [(features(xa, fa), features(xb, fb)) for xa, fa, xb, fb in cells]
    results = []
    waiting = []

    def finish():
        sums_a, sums_b, xa, xb = waiting.pop(0)
        results.append((combine(fold(sums_a), xa), combine(fold(sums_b), xb)))

    for gram, (feat_a, feat_b), (xa, _, xb, _) in zip(grams, feats, cells):
        high, low = weights(gram)
        rows = jnp.concatenate([high, low], axis=0)
        columns = jnp.concatenate([high, low], axis=1)
        sums_b = dot(jnp.concatenate([feat_a, feat_a], axis=1), rows, 1, 0)
        sums_a = dot(jnp.concatenate([feat_b, feat_b], axis=1), columns, 1, 1)
        waiting.append((sums_a, sums_b, xa, xb))
        if len(waiting) > 1:
            finish()
    finish()
    return results


def row_base(cell, tiles):
    return cell // 8 * (8 * tiles) + lax.rem(cell, 8)


def away_of(kind, odd):
    return (0, 1 - 2 * odd, 2 * odd - 1)[kind]


def pack_kernel(sizes, cells, count, pos_hbm, frc_hbm, *refs):
    n_space, n_pairs, share, cell_dev, tiles = sizes
    outs = refs[:n_pairs]
    slots, used, pos, frc, sems = refs[n_pairs:]
    fetches = [
        pltpu.make_async_copy(pos_hbm, pos, sems.at[0]),
        pltpu.make_async_copy(frc_hbm, frc, sems.at[1]),
    ]
    for fetch in fetches:
        fetch.start()
    n_slots = cells.shape[1]
    owner = cells[0, 0] // cell_dev
    here = owner // n_pairs
    here_turn = lax.rem(owner, n_pairs)
    for bucket in range(3 * n_pairs):
        used[bucket] = 0
    for s in range(n_slots):
        owner = cells[1, s] // cell_dev
        there = owner // n_pairs
        turn = lax.rem(owner, n_pairs) ^ here_turn
        kind = jnp.where(there == here, 0, jnp.where(there // 2 == here // 2, 1, 2))
        bucket = kind * n_pairs + turn
        rank = used[bucket]
        used[bucket] = rank + 1
        slots[bucket * share + rank] = s
    for fetch in fetches:
        fetch.wait()
    lane = lax.broadcasted_iota(jnp.int32, (1, LANES), 1)
    plane = cell_dev * tiles
    last = share * 6 * tiles
    table = jnp.full((1, LANES), -1.0, f32)
    for m in range(3 * n_pairs):
        kind, turn = m // n_pairs, m % n_pairs
        out = outs[turn]
        label = jnp.full((1, LANES), -1.0, f32)
        for k in range(share):
            s = slots[m * share + k]
            a = lax.rem(cells[0, s], cell_dev)
            live = s < count[0]
            b = jnp.where(live, lax.rem(cells[1, s], cell_dev), -1)
            table = jnp.where(lane == m * share + k, jnp.where(live, a, -1).astype(f32), table)
            label = jnp.where(lane == k, b.astype(f32), label)
            base = row_base(a, tiles)
            for c in range(6):
                source = pos if c < 3 else frc
                row = (k * 6 + c) * tiles
                out[kind, row : row + tiles, :] = source[
                    pl.ds(base + c % 3 * plane, tiles, stride=8), :
                ]
        out[kind, last : last + 1, :] = label
    outs[0][0, last + 1 : last + 2, :] = table


def pair_kernel(sizes, kinds, started, marked, *refs):
    n_space, n_pairs, share, cell_dev, tiles = sizes
    n = len(kinds)
    messages, (pos, frc) = refs[:n], refs[n : n + 2]
    outs = refs[n + 2 + started :]
    (acc, reply), (inbox, todo, middles) = outs[:2], outs[-3:]
    rows_in = share * 6 * tiles
    plane = cell_dev * tiles
    if not started:
        acc[...] = jnp.zeros_like(acc)
    if marked:
        outs[2][...] = jnp.zeros_like(outs[2])
    here = lax.axis_index("space")
    number = jnp.int32(0)
    first = 0
    for kind, message in zip(kinds, messages):
        away = jnp.int32(away_of(kind, lax.rem(here, 2)))
        there = lax.rem(here + away + n_space, n_space)
        half = 0.5 * slab_width * away.astype(f32)
        middle_a = slab_width * (there.astype(f32) + 0.5) - half
        middle_b = slab_width * (here.astype(f32) + 0.5) + half
        for block in range(message.shape[0]):
            inbox[first * rows_in : (first + 1) * rows_in, :] = message[block, 0:rows_in, :]
            label = message[block, rows_in : rows_in + 1, :].astype(jnp.int32)
            for k in range(share):
                b = label[0, k]
                todo[0, number] = first * share + k
                todo[1, number] = b
                middles[0, number] = middle_a
                middles[1, number] = middle_b
                number = number + jnp.where(b >= 0, 1, 0)
            first += 1

    axis = lax.broadcasted_iota(jnp.int32, (3, 1), 0)

    def load(i):
        base = todo[0, i] * (6 * tiles)
        data = jnp.concatenate(
            [inbox[pl.ds(base + t, 6, stride=tiles), :] for t in range(tiles)], axis=1
        )
        start = row_base(todo[1, i], tiles)
        xb, fb = (
            jnp.concatenate(
                [ref[pl.ds(start + 8 * t, 3, stride=plane), :] for t in range(tiles)], axis=1
            )
            for ref in (pos, frc)
        )
        xa = data[0:3] - jnp.where(axis == 0, middles[0, i], across_middle)
        xb = xb - jnp.where(axis == 0, middles[1, i], across_middle)
        return xa, data[3:6], xb, fb

    def store(i, vel_a, vel_b):
        base = todo[0, i] * (3 * tiles)
        start = row_base(todo[1, i], tiles)
        parts = [slice(t * LANES, (t + 1) * LANES) for t in range(tiles)]
        places = [pl.ds(start + 8 * t, 3, stride=plane) for t in range(tiles)]
        totals = [acc[place, :] + vel_b[:, part] for place, part in zip(places, parts)]
        for t in range(tiles):
            acc[places[t], :] = totals[t]
            reply[pl.ds(base + t, 3, stride=tiles), :] = vel_a[:, parts[t]]

    def several(numbers):
        results = pair_velocities([load(i) for i in numbers])
        for i, result in zip(numbers, results):
            store(i, *result)

    def four(i, _):
        several([4 * i + j for j in range(4)])
        return 0

    lax.fori_loop(0, number // 4, four, 0)
    left = lax.rem(number, 4)

    @pl.when(left >= 2)
    def _():
        several([number - left, number - left + 1])

    @pl.when(lax.rem(left, 2) == 1)
    def _():
        several([number - 1])


def add_kernel(sizes, where, acc, mine, *refs):
    n_space, n_pairs, share, cell_dev, tiles = sizes
    replies, out = refs[:-1], refs[-1]
    plane = cell_dev * tiles
    last = share * 6 * tiles
    table = mine[0, last + 1 : last + 2, :].astype(jnp.int32)
    out[...] = acc[...]
    for m, (operand, block) in enumerate(where):
        for k in range(share):
            a = table[0, m * share + k]
            live = a >= 0
            base = row_base(jnp.maximum(a, 0), tiles)
            places = [pl.ds(base + c * plane, tiles, stride=8) for c in range(3)]
            totals = []
            for c in range(3):
                row = (k * 3 + c) * tiles
                term = jnp.where(live, replies[operand][block, row : row + tiles, :], 0.0)
                totals.append(out[places[c], :] + term)
            for c in range(3):
                out[places[c], :] = totals[c]


def flat_rows(cells):
    count, _, points = cells.shape
    value = jnp.transpose(cells, (1, 0, 2)).reshape(3, count // 8, 8, points // LANES, LANES)
    return jnp.transpose(value, (0, 1, 3, 2, 4)).reshape(-1, LANES)


def cell_rows(rows, count, points):
    value = rows.reshape(3, count // 8, points // LANES, 8, LANES)
    value = jnp.transpose(value, (0, 1, 3, 2, 4)).reshape(3, count, points)
    return jnp.transpose(value, (1, 0, 2))


def body(positions, forces, pair_cells, pair_count):
    n_space = lax.axis_size("space")
    n_pairs = lax.axis_size("pairs")
    cell_dev, _, points = positions.shape
    n_slots = pair_cells.shape[1]
    share = n_slots // (3 * n_pairs)
    tiles = points // LANES
    sizes = (n_space, n_pairs, share, cell_dev, tiles)
    rows_in = share * 6 * tiles
    rows_out = share * 3 * tiles
    pos = flat_rows(positions)
    frc = flat_rows(forces)
    vmem = pl.BlockSpec(memory_space=pltpu.VMEM)
    smem = pl.BlockSpec(memory_space=pltpu.SMEM)
    hbm = pl.BlockSpec(memory_space=pltpu.HBM)
    message = jax.ShapeDtypeStruct((3, rows_in + 8, LANES), f32)
    total = jax.ShapeDtypeStruct((3 * cell_dev * tiles, LANES), f32)

    def across(value, turn):
        groups = [[j, j ^ turn] for j in range(n_pairs) if j < j ^ turn]
        both = lax.all_gather(value, "pairs", axis_index_groups=groups)
        mine = lax.axis_index("pairs")
        return lax.dynamic_index_in_dim(both, jnp.where(mine < mine ^ turn, 1, 0), 0, False)

    def beyond(value, kind):
        first = kind - 1
        groups = [[i, (i + 1) % n_space] for i in range(first, n_space, 2)]
        both = lax.all_gather(value, "space", axis_index_groups=groups)
        mine = lax.axis_index("space")
        return lax.dynamic_index_in_dim(both, (mine + first + 1) % 2, 0, False)

    sent = pl.pallas_call(
        functools.partial(pack_kernel, sizes),
        out_shape=[message] * n_pairs,
        in_specs=[smem, smem, hbm, hbm],
        out_specs=[vmem] * n_pairs,
        scratch_shapes=[
            pltpu.SMEM((n_slots,), jnp.int32),
            pltpu.SMEM((3 * n_pairs,), jnp.int32),
            pltpu.VMEM(total.shape, f32),
            pltpu.VMEM(total.shape, f32),
            pltpu.SemaphoreType.DMA((2,)),
        ],
        compiler_params=pltpu.CompilerParams(vmem_limit_bytes=60 * 1024 * 1024),
        name="pack",
    )(pair_cells, pair_count, pos, frc)
    got = [sent[0]] + [across(sent[turn], turn) for turn in range(1, n_pairs)]

    def pairs(arrived, before, marked=False):
        kinds = [kind for kind, _ in arrived]
        values = [value for _, value in arrived]
        n = len(values)
        blocks = sum(value.shape[0] for value in values)
        return pl.pallas_call(
            functools.partial(pair_kernel, sizes, kinds, len(before), marked),
            out_shape=[total, jax.ShapeDtypeStruct((blocks * rows_out, LANES), f32)]
            + [jax.ShapeDtypeStruct((1, LANES), f32)] * marked,
            in_specs=[vmem] * (n + 2 + len(before)),
            out_specs=[vmem] * (2 + marked),
            scratch_shapes=[
                pltpu.VMEM((blocks * rows_in, LANES), f32),
                pltpu.SMEM((2, blocks * share + 1), jnp.int32),
                pltpu.SMEM((2, blocks * share + 1), f32),
            ],
            input_output_aliases={n + 2: 0} if before else {},
            compiler_params=pltpu.CompilerParams(vmem_limit_bytes=48 * 1024 * 1024),
            cost_estimate=pl.CostEstimate(
                flops=blocks * 1_000_000_000, bytes_accessed=2_000_000, transcendentals=2_000_000
            ),
            name="pairs",
        )(*values, pos, frc, *before)

    near, far = range(2), range(2, n_pairs)
    own = [sent[0][kind : kind + 1] for kind in range(3)]
    core = [got[1][kind : kind + 1] for kind in range(3)]
    out_1n = beyond(jnp.concatenate([own[1], core[1]]), 1)
    acc, reply_0n, nothing = pairs([(0, own[0]), (0, core[0])], [], True)
    rest = [got[turn] + nothing[None] for turn in far]
    out_1f = beyond(jnp.stack([value[1] for value in rest]), 1)
    out_2 = beyond(jnp.concatenate([own[2], core[2]] + [value[2:] for value in rest]), 2)
    acc, reply_m = pairs([(1, out_1n)] + [(0, got[turn][0:1]) for turn in far], [acc])
    acc, reply_f, later = pairs([(1, out_1f), (2, out_2)], [acc], True)
    reply_0n, reply_m, reply_f = (
        value.reshape(-1, rows_out, LANES) for value in (reply_0n, reply_m, reply_f)
    )
    cut = n_pairs - 2
    back_1n = beyond(reply_m[:2] + later[None], 1)
    back_2n = beyond(reply_f[cut : cut + 2], 2)
    home = [
        across(jnp.stack([reply_m[turn], reply_f[turn - 2], reply_f[cut + turn]]), turn)
        for turn in far
    ]
    back_1f = beyond(jnp.stack([value[1] for value in home]), 1)
    back_2f = beyond(jnp.stack([value[2] for value in home]), 2)
    core = across(jnp.stack([reply_0n[1], back_1n[1], back_2n[1]]), 1)
    mine = jnp.stack([reply_0n[0], back_1n[0], back_2n[0]])
    replies = [mine, core, back_1f, back_2f] + home
    where = [(0, 0), (1, 0)] + [(2 + turn, 0) for turn in far]
    where += [(0, 1), (1, 1)] + [(2, turn - 2) for turn in far]
    where += [(0, 2), (1, 2)] + [(3, turn - 2) for turn in far]
    velocity = pl.pallas_call(
        functools.partial(add_kernel, sizes, where),
        out_shape=total,
        in_specs=[vmem] * (2 + len(replies)),
        out_specs=vmem,
        compiler_params=pltpu.CompilerParams(vmem_limit_bytes=48 * 1024 * 1024),
        name="add",
    )(acc, own[0], *replies)
    return cell_rows(velocity, cell_dev, points)


def solution(mesh):
    placed = (
        P(("space", "pairs"), None, None),
        P(("space", "pairs"), None, None),
        P(None, ("space", "pairs")),
        P(("space", "pairs")),
    )
    return jax.shard_map(
        body,
        mesh=mesh,
        in_specs=placed,
        out_specs=P(("space", "pairs"), None, None),
        check_vma=False,
    )
```

```python
import functools
import math

import jax
import jax.numpy as jnp
from jax import lax
from jax.experimental import pallas as pl
from jax.experimental.pallas import tpu as pltpu
from jax.sharding import PartitionSpec as P

stokes_coef = 1.0 / (8.0 * math.pi)
eps_sq = 0.01
slab_width = 3.0
across_middle = 1.0
LANES = 128
FEATURES = 16
GRAM = 8

f32 = jnp.float32
bf16 = jnp.bfloat16


def split(value, terms):
    parts = []
    for _ in range(terms - 1):
        part = value.astype(bf16).astype(f32)
        parts.append(part)
        value = value - part
    parts.append(value)
    return parts


def matrix(ref, cell, height, tiles):
    first = cell * tiles
    return jnp.concatenate(
        [ref[(first + t) * height : (first + t + 1) * height, :] for t in range(tiles)], axis=1
    )


def lay_out(x, f, first, feat, gram):
    rows = x[0].shape[0]
    norm = x[0] * x[0] + x[1] * x[1] + x[2] * x[2]
    along = x[0] * f[0] + x[1] * f[1] + x[2] * f[2]
    columns = list(f) + [x[k] * f[c] for k in range(3) for c in range(3)]
    columns += [norm * f[c] + x[c] * along for c in range(3)]
    for number, value in enumerate(columns):
        feat[pl.ds(number, rows, stride=FEATURES), :] = value
    scale = jnp.where(first, 1.0, -2.0)
    terms = [x[c] * scale for c in range(3)]
    terms += [jnp.where(first, norm, 1.0), jnp.where(first, 1.0, norm + eps_sq)]
    for number, value in enumerate(terms):
        gram[pl.ds(number, rows, stride=GRAM), :] = value
    return norm


def combine(sums, x, norm):
    rows = norm.shape[0]
    at = [sums[pl.ds(number, rows, stride=FEATURES), :] for number in range(15)]
    force, second = at[0:3], at[12:15]
    moment = [at[3 + 3 * k : 6 + 3 * k] for k in range(3)]
    trace = moment[0][0] + moment[1][1] + moment[2][2]
    along = x[0] * force[0] + x[1] * force[1] + x[2] * force[2] - trace
    size = norm + 2.0 * eps_sq
    out = []
    for c in range(3):
        mixed = x[0] * moment[0][c] + x[1] * moment[1][c] + x[2] * moment[2][c]
        turned = x[0] * moment[c][0] + x[1] * moment[c][1] + x[2] * moment[c][2]
        value = size * force[c] + second[c] - 2.0 * mixed - turned + x[c] * along
        out.append(value * stokes_coef)
    return out


def gram_product(gram, tiles):
    left = split(matrix(gram, 0, GRAM, tiles), 3)
    right = split(matrix(gram, 1, GRAM, tiles), 3)
    order = ((0, 0), (0, 1), (1, 0), (0, 2), (1, 1), (2, 0))
    return dot(
        jnp.concatenate([left[p] for p, _ in order], axis=0).astype(bf16),
        jnp.concatenate([right[q] for _, q in order], axis=0).astype(bf16),
        0,
        0,
    )


def feature_rows(feat, cell, tiles):
    parts = split(matrix(feat, cell, FEATURES, tiles), 3)
    terms = jnp.concatenate([part.astype(bf16) for part in parts], axis=0)
    return jnp.concatenate([terms, terms], axis=1)


def dot(left, right, left_dim, right_dim):
    return lax.dot_general(
        left, right, (((left_dim,), (right_dim,)), ((), ())), preferred_element_type=f32
    )


def fold(sums):
    return sums[0:FEATURES] + sums[FEATURES : 2 * FEATURES] + sums[2 * FEATURES :]


def weights(dist_sq):
    inverse = lax.rsqrt(dist_sq)
    cubed = inverse * inverse * inverse
    high = cubed.astype(bf16)
    low = (cubed - high.astype(f32)).astype(bf16)
    return high, low


def pair_velocities(cells, first, feats, grams, totals):
    tiles = cells[0][0][0].shape[0] // 2
    n = len(cells)
    norms = [lay_out(x, f, first, feats.at[i], grams.at[i]) for i, (x, f) in enumerate(cells)]
    squares = [gram_product(grams.at[i], tiles) for i in range(n)]
    rows = [[feature_rows(feats.at[i], cell, tiles) for cell in range(2)] for i in range(n)]
    results = []
    waiting = []

    def finish():
        i, sums = waiting.pop(0)
        for cell in range(2):
            value = fold(sums[cell])
            for t in range(tiles):
                place = (cell * tiles + t) * FEATURES
                totals[i, place : place + FEATURES, :] = value[:, t * LANES : (t + 1) * LANES]
        results.append(combine(totals.at[i], cells[i][0], norms[i]))

    for i in range(n):
        high, low = weights(squares[i])
        of_b = dot(rows[i][0], jnp.concatenate([high, low], axis=0), 1, 0)
        of_a = dot(rows[i][1], jnp.concatenate([high, low], axis=1), 1, 1)
        waiting.append((i, (of_a, of_b)))
        if len(waiting) > 1:
            finish()
    finish()
    return results


def row_base(cell, tiles):
    return cell // 8 * (8 * tiles) + lax.rem(cell, 8)


def away_of(kind, odd):
    return (0, 1 - 2 * odd, 2 * odd - 1)[kind]


def pack_kernel(sizes, cells, count, pos_hbm, frc_hbm, *refs):
    n_space, n_pairs, share, cell_dev, tiles = sizes
    outs = refs[:n_pairs]
    slots, used, pos, frc, sems = refs[n_pairs:]
    fetches = [
        pltpu.make_async_copy(pos_hbm, pos, sems.at[0]),
        pltpu.make_async_copy(frc_hbm, frc, sems.at[1]),
    ]
    for fetch in fetches:
        fetch.start()
    n_slots = cells.shape[1]
    owner = cells[0, 0] // cell_dev
    here = owner // n_pairs
    here_turn = lax.rem(owner, n_pairs)
    for bucket in range(3 * n_pairs):
        used[bucket] = 0
    for s in range(n_slots):
        owner = cells[1, s] // cell_dev
        there = owner // n_pairs
        turn = lax.rem(owner, n_pairs) ^ here_turn
        kind = jnp.where(there == here, 0, jnp.where(there // 2 == here // 2, 1, 2))
        bucket = kind * n_pairs + turn
        rank = used[bucket]
        used[bucket] = rank + 1
        slots[bucket * share + rank] = s
    for fetch in fetches:
        fetch.wait()
    lane = lax.broadcasted_iota(jnp.int32, (1, LANES), 1)
    plane = cell_dev * tiles
    last = share * 6 * tiles
    table = jnp.full((1, LANES), -1.0, f32)
    for m in range(3 * n_pairs):
        kind, turn = m // n_pairs, m % n_pairs
        out = outs[turn]
        label = jnp.full((1, LANES), -1.0, f32)
        for k in range(share):
            s = slots[m * share + k]
            a = lax.rem(cells[0, s], cell_dev)
            live = s < count[0]
            b = jnp.where(live, lax.rem(cells[1, s], cell_dev), -1)
            table = jnp.where(lane == m * share + k, jnp.where(live, a, -1).astype(f32), table)
            label = jnp.where(lane == k, b.astype(f32), label)
            base = row_base(a, tiles)
            for c in range(6):
                source = pos if c < 3 else frc
                row = (k * 6 + c) * tiles
                out[kind, row : row + tiles, :] = source[
                    pl.ds(base + c % 3 * plane, tiles, stride=8), :
                ]
        out[kind, last : last + 1, :] = label
    outs[0][0, last + 1 : last + 2, :] = table


def pair_kernel(sizes, kinds, started, marked, *refs):
    n_space, n_pairs, share, cell_dev, tiles = sizes
    n = len(kinds)
    messages, (pos, frc) = refs[:n], refs[n : n + 2]
    outs = refs[n + 2 + started :]
    (acc, reply), (inbox, feats, grams, totals, todo, middles) = outs[:2], outs[-6:]
    feats[...] = jnp.zeros_like(feats)
    grams[...] = jnp.zeros_like(grams)
    rows_in = share * 6 * tiles
    plane = cell_dev * tiles
    if not started:
        acc[...] = jnp.zeros_like(acc)
    if marked:
        outs[2][...] = jnp.zeros_like(outs[2])
    here = lax.axis_index("space")
    number = jnp.int32(0)
    first = 0
    for kind, message in zip(kinds, messages):
        away = jnp.int32(away_of(kind, lax.rem(here, 2)))
        there = lax.rem(here + away + n_space, n_space)
        half = 0.5 * slab_width * away.astype(f32)
        middle_a = slab_width * (there.astype(f32) + 0.5) - half
        middle_b = slab_width * (here.astype(f32) + 0.5) + half
        for block in range(message.shape[0]):
            inbox[first * rows_in : (first + 1) * rows_in, :] = message[block, 0:rows_in, :]
            label = message[block, rows_in : rows_in + 1, :].astype(jnp.int32)
            for k in range(share):
                b = label[0, k]
                todo[0, number] = first * share + k
                todo[1, number] = b
                middles[0, number] = middle_a
                middles[1, number] = middle_b
                number = number + jnp.where(b >= 0, 1, 0)
            first += 1

    first = lax.broadcasted_iota(jnp.int32, (2 * tiles, LANES), 0) < tiles

    def load(i):
        base = todo[0, i] * (6 * tiles)
        start = row_base(todo[1, i], tiles)
        values = []
        for c in range(6):
            ref = pos if c < 3 else frc
            values.append(
                jnp.concatenate(
                    [
                        inbox[pl.ds(base + c * tiles, tiles), :],
                        ref[pl.ds(start + c % 3 * plane, tiles, stride=8), :],
                    ],
                    axis=0,
                )
            )
        x = [values[0] - jnp.where(first, middles[0, i], middles[1, i])]
        x += [value - across_middle for value in values[1:3]]
        return x, values[3:]

    def store(i, velocity):
        base = todo[0, i] * (3 * tiles)
        start = row_base(todo[1, i], tiles)
        places = [pl.ds(start + c * plane, tiles, stride=8) for c in range(3)]
        added = [acc[places[c], :] + velocity[c][tiles:] for c in range(3)]
        for c in range(3):
            acc[places[c], :] = added[c]
            reply[pl.ds(base + c * tiles, tiles), :] = velocity[c][:tiles]

    def several(numbers):
        cells = [load(i) for i in numbers]
        results = pair_velocities(cells, first, feats, grams, totals)
        for i, result in zip(numbers, results):
            store(i, result)

    def four(i, _):
        several([4 * i + j for j in range(4)])
        return 0

    lax.fori_loop(0, number // 4, four, 0)
    left = lax.rem(number, 4)

    @pl.when(left >= 2)
    def _():
        several([number - left, number - left + 1])

    @pl.when(lax.rem(left, 2) == 1)
    def _():
        several([number - 1])


def add_kernel(sizes, where, acc, mine, *refs):
    n_space, n_pairs, share, cell_dev, tiles = sizes
    replies, out = refs[:-1], refs[-1]
    plane = cell_dev * tiles
    last = share * 6 * tiles
    table = mine[0, last + 1 : last + 2, :].astype(jnp.int32)
    out[...] = acc[...]
    for m, (operand, block) in enumerate(where):
        for k in range(share):
            a = table[0, m * share + k]
            live = a >= 0
            base = row_base(jnp.maximum(a, 0), tiles)
            places = [pl.ds(base + c * plane, tiles, stride=8) for c in range(3)]
            totals = []
            for c in range(3):
                row = (k * 3 + c) * tiles
                term = jnp.where(live, replies[operand][block, row : row + tiles, :], 0.0)
                totals.append(out[places[c], :] + term)
            for c in range(3):
                out[places[c], :] = totals[c]


def flat_rows(cells):
    count, _, points = cells.shape
    value = jnp.transpose(cells, (1, 0, 2)).reshape(3, count // 8, 8, points // LANES, LANES)
    return jnp.transpose(value, (0, 1, 3, 2, 4)).reshape(-1, LANES)


def cell_rows(rows, count, points):
    value = rows.reshape(3, count // 8, points // LANES, 8, LANES)
    value = jnp.transpose(value, (0, 1, 3, 2, 4)).reshape(3, count, points)
    return jnp.transpose(value, (1, 0, 2))


def body(positions, forces, pair_cells, pair_count):
    n_space = lax.axis_size("space")
    n_pairs = lax.axis_size("pairs")
    cell_dev, _, points = positions.shape
    n_slots = pair_cells.shape[1]
    share = n_slots // (3 * n_pairs)
    tiles = points // LANES
    sizes = (n_space, n_pairs, share, cell_dev, tiles)
    rows_in = share * 6 * tiles
    rows_out = share * 3 * tiles
    pos = flat_rows(positions)
    frc = flat_rows(forces)
    vmem = pl.BlockSpec(memory_space=pltpu.VMEM)
    smem = pl.BlockSpec(memory_space=pltpu.SMEM)
    hbm = pl.BlockSpec(memory_space=pltpu.HBM)
    message = jax.ShapeDtypeStruct((3, rows_in + 8, LANES), f32)
    total = jax.ShapeDtypeStruct((3 * cell_dev * tiles, LANES), f32)

    def across(value, turn):
        return lax.ppermute(value, "pairs", [(j, j ^ turn) for j in range(n_pairs)])

    def beyond(value, kind):
        moves = [(i, (i + away_of(kind, i % 2)) % n_space) for i in range(n_space)]
        return lax.ppermute(value, "space", moves)

    sent = pl.pallas_call(
        functools.partial(pack_kernel, sizes),
        out_shape=[message] * n_pairs,
        in_specs=[smem, smem, hbm, hbm],
        out_specs=[vmem] * n_pairs,
        scratch_shapes=[
            pltpu.SMEM((n_slots,), jnp.int32),
            pltpu.SMEM((3 * n_pairs,), jnp.int32),
            pltpu.VMEM(total.shape, f32),
            pltpu.VMEM(total.shape, f32),
            pltpu.SemaphoreType.DMA((2,)),
        ],
        compiler_params=pltpu.CompilerParams(vmem_limit_bytes=60 * 1024 * 1024),
        name="pack",
    )(pair_cells, pair_count, pos, frc)
    got = [sent[0]] + [across(sent[turn], turn) for turn in range(1, n_pairs)]

    def pairs(arrived, before, marked=False):
        kinds = [kind for kind, _ in arrived]
        values = [value for _, value in arrived]
        n = len(values)
        blocks = sum(value.shape[0] for value in values)
        return pl.pallas_call(
            functools.partial(pair_kernel, sizes, kinds, len(before), marked),
            out_shape=[total, jax.ShapeDtypeStruct((blocks * rows_out, LANES), f32)]
            + [jax.ShapeDtypeStruct((1, LANES), f32)] * marked,
            in_specs=[vmem] * (n + 2 + len(before)),
            out_specs=[vmem] * (2 + marked),
            scratch_shapes=[
                pltpu.VMEM((blocks * rows_in, LANES), f32),
                pltpu.VMEM((4, 2 * tiles * FEATURES, LANES), f32),
                pltpu.VMEM((4, 2 * tiles * GRAM, LANES), f32),
                pltpu.VMEM((4, 2 * tiles * FEATURES, LANES), f32),
                pltpu.SMEM((2, blocks * share + 1), jnp.int32),
                pltpu.SMEM((2, blocks * share + 1), f32),
            ],
            input_output_aliases={n + 2: 0} if before else {},
            compiler_params=pltpu.CompilerParams(vmem_limit_bytes=48 * 1024 * 1024),
            cost_estimate=pl.CostEstimate(
                flops=blocks * 1_000_000_000, bytes_accessed=2_000_000, transcendentals=2_000_000
            ),
            name="pairs",
        )(*values, pos, frc, *before)

    near, far = range(2), range(2, n_pairs)
    own = [sent[0][kind : kind + 1] for kind in range(3)]
    core = [got[1][kind : kind + 1] for kind in range(3)]
    out_1n = beyond(jnp.concatenate([own[1], core[1]]), 1)
    acc, reply_0n, nothing = pairs([(0, own[0]), (0, core[0])], [], True)
    rest = [got[turn] + nothing[None] for turn in far]
    out_1f = beyond(jnp.stack([value[1] for value in rest]), 1)
    out_2 = beyond(jnp.concatenate([own[2], core[2]] + [value[2:] for value in rest]), 2)
    acc, reply_m = pairs([(1, out_1n)] + [(0, got[turn][0:1]) for turn in far], [acc])
    acc, reply_f = pairs([(1, out_1f), (2, out_2)], [acc])
    reply_0n, reply_m, reply_f = (
        value.reshape(-1, rows_out, LANES) for value in (reply_0n, reply_m, reply_f)
    )
    cut = n_pairs - 2
    back_0 = jnp.concatenate([reply_0n, reply_m[2:]])
    back_1 = beyond(jnp.concatenate([reply_m[:2], reply_f[:cut]]), 1)
    back_2 = beyond(reply_f[cut:], 2)
    replies = []
    for turn in range(n_pairs):
        value = jnp.stack([back_0[turn], back_1[turn], back_2[turn]])
        replies.append(across(value, turn) if turn else value)
    where = [(turn, kind) for kind in range(3) for turn in range(n_pairs)]
    velocity = pl.pallas_call(
        functools.partial(add_kernel, sizes, where),
        out_shape=total,
        in_specs=[vmem] * (2 + len(replies)),
        out_specs=vmem,
        compiler_params=pltpu.CompilerParams(vmem_limit_bytes=48 * 1024 * 1024),
        name="add",
    )(acc, own[0], *replies)
    return cell_rows(velocity, cell_dev, points)


def solution(mesh):
    placed = (
        P(("space", "pairs"), None, None),
        P(("space", "pairs"), None, None),
        P(None, ("space", "pairs")),
        P(("space", "pairs")),
    )
    return jax.shard_map(
        body,
        mesh=mesh,
        in_specs=placed,
        out_specs=P(("space", "pairs"), None, None),
        check_vma=False,
    )
```

```python
import functools
import math

import jax
import jax.numpy as jnp
from jax import lax
from jax.experimental import pallas as pl
from jax.experimental.pallas import tpu as pltpu
from jax.sharding import PartitionSpec as P

stokes_coef = 1.0 / (8.0 * math.pi)
eps_sq = 0.01
slab_width = 3.0
across_middle = 1.0
LANES = 128
FEATURES = 16
GRAM = 8

f32 = jnp.float32
bf16 = jnp.bfloat16


def split(value, terms):
    parts = []
    for _ in range(terms - 1):
        part = value.astype(bf16).astype(f32)
        parts.append(part)
        value = value - part
    parts.append(value)
    return parts


def matrix(ref, cell, height, tiles):
    first = cell * tiles
    return jnp.concatenate(
        [ref[(first + t) * height : (first + t + 1) * height, :] for t in range(tiles)], axis=1
    )


def lay_out(x, f, first, feat, gram):
    rows = x[0].shape[0]
    norm = x[0] * x[0] + x[1] * x[1] + x[2] * x[2]
    along = x[0] * f[0] + x[1] * f[1] + x[2] * f[2]
    columns = list(f) + [x[k] * f[c] for k in range(3) for c in range(3)]
    columns += [norm * f[c] + x[c] * along for c in range(3)]
    for number, value in enumerate(columns):
        feat[pl.ds(number, rows, stride=FEATURES), :] = value
    scale = jnp.where(first, 1.0, -2.0)
    terms = [x[c] * scale for c in range(3)]
    terms += [jnp.where(first, norm, 1.0), jnp.where(first, 1.0, norm + eps_sq)]
    for number, value in enumerate(terms):
        gram[pl.ds(number, rows, stride=GRAM), :] = value
    return norm


def combine(sums, x, norm):
    rows = norm.shape[0]
    at = [sums[pl.ds(number, rows, stride=FEATURES), :] for number in range(15)]
    force, second = at[0:3], at[12:15]
    moment = [at[3 + 3 * k : 6 + 3 * k] for k in range(3)]
    trace = moment[0][0] + moment[1][1] + moment[2][2]
    along = x[0] * force[0] + x[1] * force[1] + x[2] * force[2] - trace
    size = norm + 2.0 * eps_sq
    out = []
    for c in range(3):
        mixed = x[0] * moment[0][c] + x[1] * moment[1][c] + x[2] * moment[2][c]
        turned = x[0] * moment[c][0] + x[1] * moment[c][1] + x[2] * moment[c][2]
        value = size * force[c] + second[c] - 2.0 * mixed - turned + x[c] * along
        out.append(value * stokes_coef)
    return out


def gram_product(gram, tiles):
    left = split(matrix(gram, 0, GRAM, tiles), 3)
    right = split(matrix(gram, 1, GRAM, tiles), 3)
    order = ((0, 0), (0, 1), (1, 0), (0, 2), (1, 1), (2, 0))
    return dot(
        jnp.concatenate([left[p] for p, _ in order], axis=0).astype(bf16),
        jnp.concatenate([right[q] for _, q in order], axis=0).astype(bf16),
        0,
        0,
    )


def feature_rows(feat, cell, tiles):
    parts = split(matrix(feat, cell, FEATURES, tiles), 3)
    return jnp.concatenate([part.astype(bf16) for part in parts], axis=0)


def dot(left, right, left_dim, right_dim):
    return lax.dot_general(
        left, right, (((left_dim,), (right_dim,)), ((), ())), preferred_element_type=f32
    )


def fold(high, low):
    third = high[2 * FEATURES :]
    both = high[: 2 * FEATURES] + low
    return both[:FEATURES] + both[FEATURES:] + third


def weights(dist_sq):
    inverse = lax.rsqrt(dist_sq)
    cubed = inverse * inverse * inverse
    high = cubed.astype(bf16)
    low = (cubed - high.astype(f32)).astype(bf16)
    return high, low


def pair_velocities(cells, first, feats, grams, totals):
    tiles = cells[0][0][0].shape[0] // 2
    n = len(cells)
    norms = [lay_out(x, f, first, feats.at[i], grams.at[i]) for i, (x, f) in enumerate(cells)]
    squares = [gram_product(grams.at[i], tiles) for i in range(n)]
    rows = [[feature_rows(feats.at[i], cell, tiles) for cell in range(2)] for i in range(n)]
    results = []
    waiting = []

    def finish():
        i, sums = waiting.pop(0)
        for cell in range(2):
            value = fold(*sums[cell])
            for t in range(tiles):
                place = (cell * tiles + t) * FEATURES
                totals[i, place : place + FEATURES, :] = value[:, t * LANES : (t + 1) * LANES]
        results.append(combine(totals.at[i], cells[i][0], norms[i]))

    for i in range(n):
        high, low = weights(squares[i])
        of_b = dot(rows[i][0], high, 1, 0), dot(rows[i][0][: 2 * FEATURES], low, 1, 0)
        of_a = dot(rows[i][1], high, 1, 1), dot(rows[i][1][: 2 * FEATURES], low, 1, 1)
        waiting.append((i, (of_a, of_b)))
        if len(waiting) > 1:
            finish()
    finish()
    return results


def row_base(cell, tiles):
    return cell // 8 * (8 * tiles) + lax.rem(cell, 8)


def away_of(kind, odd):
    return (0, 1 - 2 * odd, 2 * odd - 1)[kind]


def pack_kernel(sizes, cells, count, pos_hbm, frc_hbm, *refs):
    n_space, n_pairs, share, cell_dev, tiles = sizes
    outs = refs[:n_pairs]
    slots, used, pos, frc, sems = refs[n_pairs:]
    fetches = [
        pltpu.make_async_copy(pos_hbm, pos, sems.at[0]),
        pltpu.make_async_copy(frc_hbm, frc, sems.at[1]),
    ]
    for fetch in fetches:
        fetch.start()
    n_slots = cells.shape[1]
    owner = cells[0, 0] // cell_dev
    here = owner // n_pairs
    here_turn = lax.rem(owner, n_pairs)
    for bucket in range(3 * n_pairs):
        used[bucket] = 0
    for s in range(n_slots):
        owner = cells[1, s] // cell_dev
        there = owner // n_pairs
        turn = lax.rem(owner, n_pairs) ^ here_turn
        kind = jnp.where(there == here, 0, jnp.where(there // 2 == here // 2, 1, 2))
        bucket = kind * n_pairs + turn
        rank = used[bucket]
        used[bucket] = rank + 1
        slots[bucket * share + rank] = s
    for fetch in fetches:
        fetch.wait()
    lane = lax.broadcasted_iota(jnp.int32, (1, LANES), 1)
    plane = cell_dev * tiles
    last = share * 6 * tiles
    table = jnp.full((1, LANES), -1.0, f32)
    for m in range(3 * n_pairs):
        kind, turn = m // n_pairs, m % n_pairs
        out = outs[turn]
        label = jnp.full((1, LANES), -1.0, f32)
        for k in range(share):
            s = slots[m * share + k]
            a = lax.rem(cells[0, s], cell_dev)
            live = s < count[0]
            b = jnp.where(live, lax.rem(cells[1, s], cell_dev), -1)
            table = jnp.where(lane == m * share + k, jnp.where(live, a, -1).astype(f32), table)
            label = jnp.where(lane == k, b.astype(f32), label)
            base = row_base(a, tiles)
            for c in range(6):
                source = pos if c < 3 else frc
                row = (k * 6 + c) * tiles
                out[kind, row : row + tiles, :] = source[
                    pl.ds(base + c % 3 * plane, tiles, stride=8), :
                ]
        out[kind, last : last + 1, :] = label
    outs[0][0, last + 1 : last + 2, :] = table


def pair_kernel(sizes, kinds, started, marked, *refs):
    n_space, n_pairs, share, cell_dev, tiles = sizes
    n = len(kinds)
    messages, (pos, frc) = refs[:n], refs[n : n + 2]
    outs = refs[n + 2 + started :]
    (acc, reply), (inbox, feats, grams, totals, todo, middles) = outs[:2], outs[-6:]
    feats[...] = jnp.zeros_like(feats)
    grams[...] = jnp.zeros_like(grams)
    rows_in = share * 6 * tiles
    plane = cell_dev * tiles
    if not started:
        acc[...] = jnp.zeros_like(acc)
    if marked:
        outs[2][...] = jnp.zeros_like(outs[2])
    here = lax.axis_index("space")
    number = jnp.int32(0)
    first = 0
    for kind, message in zip(kinds, messages):
        away = jnp.int32(away_of(kind, lax.rem(here, 2)))
        there = lax.rem(here + away + n_space, n_space)
        half = 0.5 * slab_width * away.astype(f32)
        middle_a = slab_width * (there.astype(f32) + 0.5) - half
        middle_b = slab_width * (here.astype(f32) + 0.5) + half
        for block in range(message.shape[0]):
            inbox[first * rows_in : (first + 1) * rows_in, :] = message[block, 0:rows_in, :]
            label = message[block, rows_in : rows_in + 1, :].astype(jnp.int32)
            for k in range(share):
                b = label[0, k]
                todo[0, number] = first * share + k
                todo[1, number] = b
                middles[0, number] = middle_a
                middles[1, number] = middle_b
                number = number + jnp.where(b >= 0, 1, 0)
            first += 1

    first = lax.broadcasted_iota(jnp.int32, (2 * tiles, LANES), 0) < tiles

    def load(i):
        base = todo[0, i] * (6 * tiles)
        start = row_base(todo[1, i], tiles)
        values = []
        for c in range(6):
            ref = pos if c < 3 else frc
            values.append(
                jnp.concatenate(
                    [
                        inbox[pl.ds(base + c * tiles, tiles), :],
                        ref[pl.ds(start + c % 3 * plane, tiles, stride=8), :],
                    ],
                    axis=0,
                )
            )
        x = [values[0] - jnp.where(first, middles[0, i], middles[1, i])]
        x += [value - across_middle for value in values[1:3]]
        return x, values[3:]

    def store(i, velocity):
        base = todo[0, i] * (3 * tiles)
        start = row_base(todo[1, i], tiles)
        places = [pl.ds(start + c * plane, tiles, stride=8) for c in range(3)]
        added = [acc[places[c], :] + velocity[c][tiles:] for c in range(3)]
        for c in range(3):
            acc[places[c], :] = added[c]
            reply[pl.ds(base + c * tiles, tiles), :] = velocity[c][:tiles]

    def several(numbers):
        cells = [load(i) for i in numbers]
        results = pair_velocities(cells, first, feats, grams, totals)
        for i, result in zip(numbers, results):
            store(i, result)

    def four(i, _):
        several([4 * i + j for j in range(4)])
        return 0

    lax.fori_loop(0, number // 4, four, 0)
    left = lax.rem(number, 4)

    @pl.when(left >= 2)
    def _():
        several([number - left, number - left + 1])

    @pl.when(lax.rem(left, 2) == 1)
    def _():
        several([number - 1])


def add_kernel(sizes, where, acc, mine, *refs):
    n_space, n_pairs, share, cell_dev, tiles = sizes
    replies, out = refs[:-1], refs[-1]
    plane = cell_dev * tiles
    last = share * 6 * tiles
    table = mine[0, last + 1 : last + 2, :].astype(jnp.int32)
    out[...] = acc[...]
    for m, (operand, block) in enumerate(where):
        for k in range(share):
            a = table[0, m * share + k]
            live = a >= 0
            base = row_base(jnp.maximum(a, 0), tiles)
            places = [pl.ds(base + c * plane, tiles, stride=8) for c in range(3)]
            totals = []
            for c in range(3):
                row = (k * 3 + c) * tiles
                term = jnp.where(live, replies[operand][block, row : row + tiles, :], 0.0)
                totals.append(out[places[c], :] + term)
            for c in range(3):
                out[places[c], :] = totals[c]


def flat_rows(cells):
    count, _, points = cells.shape
    value = jnp.transpose(cells, (1, 0, 2)).reshape(3, count // 8, 8, points // LANES, LANES)
    return jnp.transpose(value, (0, 1, 3, 2, 4)).reshape(-1, LANES)


def cell_rows(rows, count, points):
    value = rows.reshape(3, count // 8, points // LANES, 8, LANES)
    value = jnp.transpose(value, (0, 1, 3, 2, 4)).reshape(3, count, points)
    return jnp.transpose(value, (1, 0, 2))


def body(positions, forces, pair_cells, pair_count):
    n_space = lax.axis_size("space")
    n_pairs = lax.axis_size("pairs")
    cell_dev, _, points = positions.shape
    n_slots = pair_cells.shape[1]
    share = n_slots // (3 * n_pairs)
    tiles = points // LANES
    sizes = (n_space, n_pairs, share, cell_dev, tiles)
    rows_in = share * 6 * tiles
    rows_out = share * 3 * tiles
    pos = flat_rows(positions)
    frc = flat_rows(forces)
    vmem = pl.BlockSpec(memory_space=pltpu.VMEM)
    smem = pl.BlockSpec(memory_space=pltpu.SMEM)
    hbm = pl.BlockSpec(memory_space=pltpu.HBM)
    message = jax.ShapeDtypeStruct((3, rows_in + 8, LANES), f32)
    total = jax.ShapeDtypeStruct((3 * cell_dev * tiles, LANES), f32)

    def across(value, turn):
        return lax.ppermute(value, "pairs", [(j, j ^ turn) for j in range(n_pairs)])

    def beyond(value, kind):
        moves = [(i, (i + away_of(kind, i % 2)) % n_space) for i in range(n_space)]
        return lax.ppermute(value, "space", moves)

    sent = pl.pallas_call(
        functools.partial(pack_kernel, sizes),
        out_shape=[message] * n_pairs,
        in_specs=[smem, smem, hbm, hbm],
        out_specs=[vmem] * n_pairs,
        scratch_shapes=[
            pltpu.SMEM((n_slots,), jnp.int32),
            pltpu.SMEM((3 * n_pairs,), jnp.int32),
            pltpu.VMEM(total.shape, f32),
            pltpu.VMEM(total.shape, f32),
            pltpu.SemaphoreType.DMA((2,)),
        ],
        compiler_params=pltpu.CompilerParams(vmem_limit_bytes=60 * 1024 * 1024),
        name="pack",
    )(pair_cells, pair_count, pos, frc)
    got = [sent[0]] + [across(sent[turn], turn) for turn in range(1, n_pairs)]

    def pairs(arrived, before, marked=False):
        kinds = [kind for kind, _ in arrived]
        values = [value for _, value in arrived]
        n = len(values)
        blocks = sum(value.shape[0] for value in values)
        return pl.pallas_call(
            functools.partial(pair_kernel, sizes, kinds, len(before), marked),
            out_shape=[total, jax.ShapeDtypeStruct((blocks * rows_out, LANES), f32)]
            + [jax.ShapeDtypeStruct((1, LANES), f32)] * marked,
            in_specs=[vmem] * (n + 2 + len(before)),
            out_specs=[vmem] * (2 + marked),
            scratch_shapes=[
                pltpu.VMEM((blocks * rows_in, LANES), f32),
                pltpu.VMEM((4, 2 * tiles * FEATURES, LANES), f32),
                pltpu.VMEM((4, 2 * tiles * GRAM, LANES), f32),
                pltpu.VMEM((4, 2 * tiles * FEATURES, LANES), f32),
                pltpu.SMEM((2, blocks * share + 1), jnp.int32),
                pltpu.SMEM((2, blocks * share + 1), f32),
            ],
            input_output_aliases={n + 2: 0} if before else {},
            compiler_params=pltpu.CompilerParams(vmem_limit_bytes=48 * 1024 * 1024),
            cost_estimate=pl.CostEstimate(
                flops=blocks * 1_000_000_000, bytes_accessed=2_000_000, transcendentals=2_000_000
            ),
            name="pairs",
        )(*values, pos, frc, *before)

    near, far = range(2), range(2, n_pairs)
    own = [sent[0][kind : kind + 1] for kind in range(3)]
    core = [got[1][kind : kind + 1] for kind in range(3)]
    out_1n = beyond(jnp.concatenate([own[1], core[1]]), 1)
    acc, reply_0n, nothing = pairs([(0, own[0]), (0, core[0])], [], True)
    rest = [got[turn] + nothing[None] for turn in far]
    out_1f = beyond(jnp.stack([value[1] for value in rest]), 1)
    out_2 = beyond(jnp.concatenate([own[2], core[2]] + [value[2:] for value in rest]), 2)
    acc, reply_m = pairs([(1, out_1n)] + [(0, got[turn][0:1]) for turn in far], [acc])
    acc, reply_1f = pairs([(1, out_1f)], [acc])
    acc, reply_2, later = pairs([(2, out_2)], [acc], True)
    reply_0n, reply_m, reply_1f, reply_2 = (
        value.reshape(-1, rows_out, LANES) for value in (reply_0n, reply_m, reply_1f, reply_2)
    )
    back_0 = jnp.concatenate([reply_0n, reply_m[2:]])
    back_1 = beyond(jnp.concatenate([reply_m[:2], reply_1f]) + later[None], 1)
    back_2 = beyond(reply_2, 2)
    replies = []
    for turn in range(n_pairs):
        value = jnp.stack([back_0[turn], back_1[turn], back_2[turn]])
        replies.append(across(value, turn) if turn else value)
    where = [(turn, kind) for kind in range(3) for turn in range(n_pairs)]
    velocity = pl.pallas_call(
        functools.partial(add_kernel, sizes, where),
        out_shape=total,
        in_specs=[vmem] * (2 + len(replies)),
        out_specs=vmem,
        compiler_params=pltpu.CompilerParams(vmem_limit_bytes=48 * 1024 * 1024),
        name="add",
    )(acc, own[0], *replies)
    return cell_rows(velocity, cell_dev, points)


def solution(mesh):
    placed = (
        P(("space", "pairs"), None, None),
        P(("space", "pairs"), None, None),
        P(None, ("space", "pairs")),
        P(("space", "pairs")),
    )
    return jax.shard_map(
        body,
        mesh=mesh,
        in_specs=placed,
        out_specs=P(("space", "pairs"), None, None),
        check_vma=False,
    )
```

```python
import functools
import math

import jax
import jax.numpy as jnp
from jax import lax
from jax.experimental import pallas as pl
from jax.experimental.pallas import tpu as pltpu
from jax.sharding import PartitionSpec as P

stokes_coef = 1.0 / (8.0 * math.pi)
eps_sq = 0.01
slab_width = 3.0
across_middle = 1.0
LANES = 128
FEATURES = 16
GRAM = 8

f32 = jnp.float32
bf16 = jnp.bfloat16


def split(value, terms):
    parts = []
    for _ in range(terms - 1):
        part = value.astype(bf16).astype(f32)
        parts.append(part)
        value = value - part
    parts.append(value)
    return parts


def matrix(ref, cell, height, tiles):
    first = cell * tiles
    return jnp.concatenate(
        [ref[(first + t) * height : (first + t + 1) * height, :] for t in range(tiles)], axis=1
    )


def lay_out(x, f, first, feat, gram):
    rows = x[0].shape[0]
    norm = x[0] * x[0] + x[1] * x[1] + x[2] * x[2]
    along = x[0] * f[0] + x[1] * f[1] + x[2] * f[2]
    columns = list(f) + [x[k] * f[c] for k in range(3) for c in range(3)]
    columns += [norm * f[c] + x[c] * along for c in range(3)]
    for number, value in enumerate(columns):
        feat[pl.ds(number, rows, stride=FEATURES), :] = value
    scale = jnp.where(first, 1.0, -2.0)
    terms = [x[c] * scale for c in range(3)]
    terms += [jnp.where(first, norm, 1.0), jnp.where(first, 1.0, norm + eps_sq)]
    for number, value in enumerate(terms):
        gram[pl.ds(number, rows, stride=GRAM), :] = value
    return norm


def combine(sums, x, norm):
    rows = norm.shape[0]
    at = [sums[pl.ds(number, rows, stride=FEATURES), :] for number in range(15)]
    force, second = at[0:3], at[12:15]
    moment = [at[3 + 3 * k : 6 + 3 * k] for k in range(3)]
    trace = moment[0][0] + moment[1][1] + moment[2][2]
    along = x[0] * force[0] + x[1] * force[1] + x[2] * force[2] - trace
    size = norm + 2.0 * eps_sq
    out = []
    for c in range(3):
        mixed = x[0] * moment[0][c] + x[1] * moment[1][c] + x[2] * moment[2][c]
        turned = x[0] * moment[c][0] + x[1] * moment[c][1] + x[2] * moment[c][2]
        value = size * force[c] + second[c] - 2.0 * mixed - turned + x[c] * along
        out.append(value * stokes_coef)
    return out


def gram_product(gram, tiles):
    left = split(matrix(gram, 0, GRAM, tiles), 3)
    right = split(matrix(gram, 1, GRAM, tiles), 3)
    order = ((0, 0), (0, 1), (1, 0), (0, 2), (1, 1), (2, 0))
    return dot(
        jnp.concatenate([left[p] for p, _ in order], axis=0).astype(bf16),
        jnp.concatenate([right[q] for _, q in order], axis=0).astype(bf16),
        0,
        0,
    )


def feature_rows(feat, cell, tiles):
    parts = split(matrix(feat, cell, FEATURES, tiles), 3)
    return jnp.concatenate([part.astype(bf16) for part in parts], axis=0)


def dot(left, right, left_dim, right_dim):
    return lax.dot_general(
        left, right, (((left_dim,), (right_dim,)), ((), ())), preferred_element_type=f32
    )


def fold(high, low):
    third = high[2 * FEATURES :]
    both = high[: 2 * FEATURES] + low
    return both[:FEATURES] + both[FEATURES:] + third


def weights(dist_sq):
    inverse = lax.rsqrt(dist_sq)
    cubed = inverse * inverse * inverse
    high = cubed.astype(bf16)
    low = (cubed - high.astype(f32)).astype(bf16)
    return high, low


def pair_velocities(cells, first, feats, grams, totals):
    tiles = cells[0][0][0].shape[0] // 2
    n = len(cells)
    norms = [lay_out(x, f, first, feats.at[i], grams.at[i]) for i, (x, f) in enumerate(cells)]
    squares = [gram_product(grams.at[i], tiles) for i in range(n)]
    rows = [[feature_rows(feats.at[i], cell, tiles) for cell in range(2)] for i in range(n)]
    results = []
    waiting = []

    def finish():
        i, sums = waiting.pop(0)
        for cell in range(2):
            value = fold(*sums[cell])
            for t in range(tiles):
                place = (cell * tiles + t) * FEATURES
                totals[i, place : place + FEATURES, :] = value[:, t * LANES : (t + 1) * LANES]
        results.append(combine(totals.at[i], cells[i][0], norms[i]))

    for i in range(n):
        high, low = weights(squares[i])
        of_b = dot(rows[i][0], high, 1, 0), dot(rows[i][0][: 2 * FEATURES], low, 1, 0)
        of_a = dot(rows[i][1], high, 1, 1), dot(rows[i][1][: 2 * FEATURES], low, 1, 1)
        waiting.append((i, (of_a, of_b)))
        if len(waiting) > 1:
            finish()
    finish()
    return results


def row_base(cell, tiles):
    return cell // 8 * (8 * tiles) + lax.rem(cell, 8)


def away_of(kind, odd):
    return (0, 1 - 2 * odd, 2 * odd - 1)[kind]


def pack_kernel(sizes, cells, count, pos_hbm, frc_hbm, *refs):
    n_space, n_pairs, share, cell_dev, tiles = sizes
    outs, second = refs[:n_pairs], refs[n_pairs]
    slots, used, pos, frc, sems = refs[n_pairs + 1 :]
    fetches = [
        pltpu.make_async_copy(pos_hbm, pos, sems.at[0]),
        pltpu.make_async_copy(frc_hbm, frc, sems.at[1]),
    ]
    for fetch in fetches:
        fetch.start()
    n_slots = cells.shape[1]
    owner = cells[0, 0] // cell_dev
    here = owner // n_pairs
    here_turn = lax.rem(owner, n_pairs)
    for bucket in range(3 * n_pairs):
        used[bucket] = 0
    for s in range(n_slots):
        owner = cells[1, s] // cell_dev
        there = owner // n_pairs
        turn = lax.rem(owner, n_pairs) ^ here_turn
        kind = jnp.where(there == here, 0, jnp.where(there // 2 == here // 2, 1, 2))
        bucket = kind * n_pairs + turn
        rank = used[bucket]
        used[bucket] = rank + 1
        slots[bucket * share + rank] = s
    for fetch in fetches:
        fetch.wait()
    lane = lax.broadcasted_iota(jnp.int32, (1, LANES), 1)
    plane = cell_dev * tiles
    last = share * 6 * tiles
    table = jnp.full((1, LANES), -1.0, f32)
    for m in range(3 * n_pairs):
        kind, turn = m // n_pairs, m % n_pairs
        out = second.at[turn] if kind == 2 else outs[turn].at[kind]
        label = jnp.full((1, LANES), -1.0, f32)
        for k in range(share):
            s = slots[m * share + k]
            a = lax.rem(cells[0, s], cell_dev)
            live = s < count[0]
            b = jnp.where(live, lax.rem(cells[1, s], cell_dev), -1)
            table = jnp.where(lane == m * share + k, jnp.where(live, a, -1).astype(f32), table)
            label = jnp.where(lane == k, b.astype(f32), label)
            base = row_base(a, tiles)
            for c in range(6):
                source = pos if c < 3 else frc
                row = (k * 6 + c) * tiles
                out[row : row + tiles, :] = source[
                    pl.ds(base + c % 3 * plane, tiles, stride=8), :
                ]
        out[last : last + 1, :] = label
    outs[0][0, last + 1 : last + 2, :] = table


def pair_kernel(sizes, kinds, started, marked, *refs):
    n_space, n_pairs, share, cell_dev, tiles = sizes
    n = len(kinds)
    messages, (pos, frc) = refs[:n], refs[n : n + 2]
    outs = refs[n + 2 + started :]
    (acc, reply), (inbox, feats, grams, totals, todo, middles) = outs[:2], outs[-6:]
    feats[...] = jnp.zeros_like(feats)
    grams[...] = jnp.zeros_like(grams)
    rows_in = share * 6 * tiles
    plane = cell_dev * tiles
    if not started:
        acc[...] = jnp.zeros_like(acc)
    if marked:
        outs[2][...] = jnp.zeros_like(outs[2])
    here = lax.axis_index("space")
    number = jnp.int32(0)
    first = 0
    for kind, message in zip(kinds, messages):
        away = jnp.int32(away_of(kind, lax.rem(here, 2)))
        there = lax.rem(here + away + n_space, n_space)
        half = 0.5 * slab_width * away.astype(f32)
        middle_a = slab_width * (there.astype(f32) + 0.5) - half
        middle_b = slab_width * (here.astype(f32) + 0.5) + half
        for block in range(message.shape[0]):
            inbox[first * rows_in : (first + 1) * rows_in, :] = message[block, 0:rows_in, :]
            label = message[block, rows_in : rows_in + 1, :].astype(jnp.int32)
            for k in range(share):
                b = label[0, k]
                todo[0, number] = first * share + k
                todo[1, number] = b
                middles[0, number] = middle_a
                middles[1, number] = middle_b
                number = number + jnp.where(b >= 0, 1, 0)
            first += 1

    first = lax.broadcasted_iota(jnp.int32, (2 * tiles, LANES), 0) < tiles

    def load(i):
        base = todo[0, i] * (6 * tiles)
        start = row_base(todo[1, i], tiles)
        values = []
        for c in range(6):
            ref = pos if c < 3 else frc
            values.append(
                jnp.concatenate(
                    [
                        inbox[pl.ds(base + c * tiles, tiles), :],
                        ref[pl.ds(start + c % 3 * plane, tiles, stride=8), :],
                    ],
                    axis=0,
                )
            )
        x = [values[0] - jnp.where(first, middles[0, i], middles[1, i])]
        x += [value - across_middle for value in values[1:3]]
        return x, values[3:]

    def store(i, velocity):
        base = todo[0, i] * (3 * tiles)
        start = row_base(todo[1, i], tiles)
        places = [pl.ds(start + c * plane, tiles, stride=8) for c in range(3)]
        added = [acc[places[c], :] + velocity[c][tiles:] for c in range(3)]
        for c in range(3):
            acc[places[c], :] = added[c]
            reply[pl.ds(base + c * tiles, tiles), :] = velocity[c][:tiles]

    def several(numbers):
        cells = [load(i) for i in numbers]
        results = pair_velocities(cells, first, feats, grams, totals)
        for i, result in zip(numbers, results):
            store(i, result)

    def four(i, _):
        several([4 * i + j for j in range(4)])
        return 0

    lax.fori_loop(0, number // 4, four, 0)
    left = lax.rem(number, 4)

    @pl.when(left >= 2)
    def _():
        several([number - left, number - left + 1])

    @pl.when(lax.rem(left, 2) == 1)
    def _():
        several([number - 1])


def add_kernel(sizes, where, acc, mine, *refs):
    n_space, n_pairs, share, cell_dev, tiles = sizes
    replies, out = refs[:-1], refs[-1]
    plane = cell_dev * tiles
    last = share * 6 * tiles
    table = mine[0, last + 1 : last + 2, :].astype(jnp.int32)
    out[...] = acc[...]
    for m, (operand, block) in enumerate(where):
        for k in range(share):
            a = table[0, m * share + k]
            live = a >= 0
            base = row_base(jnp.maximum(a, 0), tiles)
            places = [pl.ds(base + c * plane, tiles, stride=8) for c in range(3)]
            totals = []
            for c in range(3):
                row = (k * 3 + c) * tiles
                term = jnp.where(live, replies[operand][block, row : row + tiles, :], 0.0)
                totals.append(out[places[c], :] + term)
            for c in range(3):
                out[places[c], :] = totals[c]


def flat_rows(cells):
    count, _, points = cells.shape
    value = jnp.transpose(cells, (1, 0, 2)).reshape(3, count // 8, 8, points // LANES, LANES)
    return jnp.transpose(value, (0, 1, 3, 2, 4)).reshape(-1, LANES)


def cell_rows(rows, count, points):
    value = rows.reshape(3, count // 8, points // LANES, 8, LANES)
    value = jnp.transpose(value, (0, 1, 3, 2, 4)).reshape(3, count, points)
    return jnp.transpose(value, (1, 0, 2))


def body(positions, forces, pair_cells, pair_count):
    n_space = lax.axis_size("space")
    n_pairs = lax.axis_size("pairs")
    cell_dev, _, points = positions.shape
    n_slots = pair_cells.shape[1]
    share = n_slots // (3 * n_pairs)
    tiles = points // LANES
    sizes = (n_space, n_pairs, share, cell_dev, tiles)
    rows_in = share * 6 * tiles
    rows_out = share * 3 * tiles
    pos = flat_rows(positions)
    frc = flat_rows(forces)
    vmem = pl.BlockSpec(memory_space=pltpu.VMEM)
    smem = pl.BlockSpec(memory_space=pltpu.SMEM)
    hbm = pl.BlockSpec(memory_space=pltpu.HBM)
    message = jax.ShapeDtypeStruct((2, rows_in + 8, LANES), f32)
    messages = jax.ShapeDtypeStruct((n_pairs, rows_in + 8, LANES), f32)
    total = jax.ShapeDtypeStruct((3 * cell_dev * tiles, LANES), f32)

    def across(value, turn):
        return lax.ppermute(value, "pairs", [(j, j ^ turn) for j in range(n_pairs)])

    def beyond(value, kind):
        moves = [(i, (i + away_of(kind, i % 2)) % n_space) for i in range(n_space)]
        return lax.ppermute(value, "space", moves)

    *sent, second = pl.pallas_call(
        functools.partial(pack_kernel, sizes),
        out_shape=[message] * n_pairs + [messages],
        in_specs=[smem, smem, hbm, hbm],
        out_specs=[vmem] * (n_pairs + 1),
        scratch_shapes=[
            pltpu.SMEM((n_slots,), jnp.int32),
            pltpu.SMEM((3 * n_pairs,), jnp.int32),
            pltpu.VMEM(total.shape, f32),
            pltpu.VMEM(total.shape, f32),
            pltpu.SemaphoreType.DMA((2,)),
        ],
        compiler_params=pltpu.CompilerParams(vmem_limit_bytes=60 * 1024 * 1024),
        name="pack",
    )(pair_cells, pair_count, pos, frc)
    second = beyond(second, 2)
    got = [sent[0]] + [across(sent[turn], turn) for turn in range(1, n_pairs)]

    def pairs(arrived, before, marked=False):
        kinds = [kind for kind, _ in arrived]
        values = [value for _, value in arrived]
        n = len(values)
        blocks = sum(value.shape[0] for value in values)
        return pl.pallas_call(
            functools.partial(pair_kernel, sizes, kinds, len(before), marked),
            out_shape=[total, jax.ShapeDtypeStruct((blocks * rows_out, LANES), f32)]
            + [jax.ShapeDtypeStruct((1, LANES), f32)] * marked,
            in_specs=[vmem] * (n + 2 + len(before)),
            out_specs=[vmem] * (2 + marked),
            scratch_shapes=[
                pltpu.VMEM((blocks * rows_in, LANES), f32),
                pltpu.VMEM((4, 2 * tiles * FEATURES, LANES), f32),
                pltpu.VMEM((4, 2 * tiles * GRAM, LANES), f32),
                pltpu.VMEM((4, 2 * tiles * FEATURES, LANES), f32),
                pltpu.SMEM((2, blocks * share + 1), jnp.int32),
                pltpu.SMEM((2, blocks * share + 1), f32),
            ],
            input_output_aliases={n + 2: 0} if before else {},
            compiler_params=pltpu.CompilerParams(vmem_limit_bytes=48 * 1024 * 1024),
            cost_estimate=pl.CostEstimate(
                flops=blocks * 1_000_000_000, bytes_accessed=2_000_000, transcendentals=2_000_000
            ),
            name="pairs",
        )(*values, pos, frc, *before)

    far = range(2, n_pairs)
    far = range(2, n_pairs)
    own = [sent[0][kind : kind + 1] for kind in range(2)]
    core = [got[1][kind : kind + 1] for kind in range(2)]
    acc, reply_0n, nothing = pairs([(0, own[0]), (0, core[0])], [], True)
    first = [own[1], core[1]] + [got[turn][1:2] + nothing[None] for turn in far]
    first = beyond(jnp.concatenate(first), 1)
    second = second + nothing[None]
    passed = [across(second[turn : turn + 1], turn) for turn in range(1, n_pairs)]
    acc, reply_m = pairs([(0, got[turn][0:1]) for turn in far] + [(2, second[0:1])], [acc])
    acc, reply_f = pairs([(1, first)] + [(2, value) for value in passed], [acc])
    reply_0n, reply_m, reply_f = (
        value.reshape(-1, rows_out, LANES) for value in (reply_0n, reply_m, reply_f)
    )
    back_0 = jnp.concatenate([reply_0n, reply_m[:-1]])
    back_1 = beyond(reply_f[:n_pairs], 1)
    back_2 = beyond(jnp.concatenate([reply_m[-1:], reply_f[n_pairs:]]), 2)
    replies = []
    for turn in range(n_pairs):
        value = jnp.stack([back_0[turn], back_1[turn], back_2[turn]])
        replies.append(across(value, turn) if turn else value)
    where = [(turn, kind) for kind in range(3) for turn in range(n_pairs)]
    velocity = pl.pallas_call(
        functools.partial(add_kernel, sizes, where),
        out_shape=total,
        in_specs=[vmem] * (2 + len(replies)),
        out_specs=vmem,
        compiler_params=pltpu.CompilerParams(vmem_limit_bytes=48 * 1024 * 1024),
        name="add",
    )(acc, own[0], *replies)
    return cell_rows(velocity, cell_dev, points)


def solution(mesh):
    placed = (
        P(("space", "pairs"), None, None),
        P(("space", "pairs"), None, None),
        P(None, ("space", "pairs")),
        P(("space", "pairs")),
    )
    return jax.shard_map(
        body,
        mesh=mesh,
        in_specs=placed,
        out_specs=P(("space", "pairs"), None, None),
        check_vma=False,
    )
```

```python
import functools
import math

import jax
import jax.numpy as jnp
from jax import lax
from jax.experimental import pallas as pl
from jax.experimental.pallas import tpu as pltpu
from jax.sharding import PartitionSpec as P

stokes_coef = 1.0 / (8.0 * math.pi)
eps_sq = 0.01
slab_width = 3.0
across_middle = 1.0
LANES = 128
FEATURES = 16
GRAM = 8
PIECES = 4

f32 = jnp.float32
bf16 = jnp.bfloat16


def split(value, terms):
    parts = []
    for _ in range(terms - 1):
        part = value.astype(bf16).astype(f32)
        parts.append(part)
        value = value - part
    parts.append(value)
    return parts


def matrix(ref, cell, height, tiles):
    first = cell * tiles
    return jnp.concatenate(
        [ref[(first + t) * height : (first + t + 1) * height, :] for t in range(tiles)], axis=1
    )


def lay_out(x, f, first, feat, gram):
    rows = x[0].shape[0]
    norm = x[0] * x[0] + x[1] * x[1] + x[2] * x[2]
    along = x[0] * f[0] + x[1] * f[1] + x[2] * f[2]
    columns = list(f) + [x[k] * f[c] for k in range(3) for c in range(3)]
    columns += [norm * f[c] + x[c] * along for c in range(3)]
    for number, value in enumerate(columns):
        feat[pl.ds(number, rows, stride=FEATURES), :] = value
    scale = jnp.where(first, 1.0, -2.0)
    terms = [x[c] * scale for c in range(3)]
    terms += [jnp.where(first, norm, 1.0), jnp.where(first, 1.0, norm + eps_sq)]
    for number, value in enumerate(terms):
        gram[pl.ds(number, rows, stride=GRAM), :] = value
    return norm


def combine(sums, x, norm):
    rows = norm.shape[0]
    at = [sums[pl.ds(number, rows, stride=FEATURES), :] for number in range(15)]
    force, second = at[0:3], at[12:15]
    moment = [at[3 + 3 * k : 6 + 3 * k] for k in range(3)]
    trace = moment[0][0] + moment[1][1] + moment[2][2]
    along = x[0] * force[0] + x[1] * force[1] + x[2] * force[2] - trace
    size = norm + 2.0 * eps_sq
    out = []
    for c in range(3):
        mixed = x[0] * moment[0][c] + x[1] * moment[1][c] + x[2] * moment[2][c]
        turned = x[0] * moment[c][0] + x[1] * moment[c][1] + x[2] * moment[c][2]
        value = size * force[c] + second[c] - 2.0 * mixed - turned + x[c] * along
        out.append(value * stokes_coef)
    return out


def gram_product(gram, tiles):
    left = split(matrix(gram, 0, GRAM, tiles), 3)
    right = split(matrix(gram, 1, GRAM, tiles), 3)
    order = ((0, 0), (0, 1), (1, 0), (0, 2), (1, 1), (2, 0))
    return dot(
        jnp.concatenate([left[p] for p, _ in order], axis=0).astype(bf16),
        jnp.concatenate([right[q] for _, q in order], axis=0).astype(bf16),
        0,
        0,
    )


def feature_rows(feat, cell, tiles):
    parts = split(matrix(feat, cell, FEATURES, tiles), 3)
    return jnp.concatenate([part.astype(bf16) for part in parts], axis=0)


def dot(left, right, left_dim, right_dim):
    return lax.dot_general(
        left, right, (((left_dim,), (right_dim,)), ((), ())), preferred_element_type=f32
    )


def fold(high, low):
    third = high[2 * FEATURES :]
    both = high[: 2 * FEATURES] + low
    return both[:FEATURES] + both[FEATURES:] + third


def weights(dist_sq):
    inverse = lax.rsqrt(dist_sq)
    cubed = inverse * inverse * inverse
    high = cubed.astype(bf16)
    low = (cubed - high.astype(f32)).astype(bf16)
    return high, low


def pair_velocities(cells, first, feats, grams, totals):
    tiles = cells[0][0][0].shape[0] // 2
    n = len(cells)
    norms = [lay_out(x, f, first, feats.at[i], grams.at[i]) for i, (x, f) in enumerate(cells)]
    squares = [gram_product(grams.at[i], tiles) for i in range(n)]
    rows = [[feature_rows(feats.at[i], cell, tiles) for cell in range(2)] for i in range(n)]
    results = []
    waiting = []

    def finish():
        i, sums = waiting.pop(0)
        for cell in range(2):
            value = fold(*sums[cell])
            for t in range(tiles):
                place = (cell * tiles + t) * FEATURES
                totals[i, place : place + FEATURES, :] = value[:, t * LANES : (t + 1) * LANES]
        results.append(combine(totals.at[i], cells[i][0], norms[i]))

    for i in range(n):
        high, low = weights(squares[i])
        of_b = dot(rows[i][0], high, 1, 0), dot(rows[i][0][: 2 * FEATURES], low, 1, 0)
        of_a = dot(rows[i][1], high, 1, 1), dot(rows[i][1][: 2 * FEATURES], low, 1, 1)
        waiting.append((i, (of_a, of_b)))
        if len(waiting) > 1:
            finish()
    finish()
    return results


def row_base(cell, tiles):
    return cell // 8 * (8 * tiles) + lax.rem(cell, 8)


def away_of(kind, odd):
    return (0, 1 - 2 * odd, 2 * odd - 1)[kind]


def pack_kernel(sizes, cells, count, pos_hbm, frc_hbm, *refs):
    n_space, n_pairs, share, cell_dev, tiles = sizes
    outs = refs[:n_pairs]
    slots, used, pos, frc, sems = refs[n_pairs:]
    fetches = []
    piece = pos.shape[0] // PIECES
    for source, target in ((pos_hbm, pos), (frc_hbm, frc)):
        for i in range(PIECES):
            rows = pl.ds(i * piece, piece)
            fetches.append(
                pltpu.make_async_copy(source.at[rows], target.at[rows], sems.at[len(fetches)])
            )
            fetches[-1].start()
    n_slots = cells.shape[1]
    owner = cells[0, 0] // cell_dev
    here = owner // n_pairs
    here_turn = lax.rem(owner, n_pairs)
    for bucket in range(3 * n_pairs):
        used[bucket] = 0
    for s in range(n_slots):
        owner = cells[1, s] // cell_dev
        there = owner // n_pairs
        turn = lax.rem(owner, n_pairs) ^ here_turn
        kind = jnp.where(there == here, 0, jnp.where(there // 2 == here // 2, 1, 2))
        bucket = kind * n_pairs + turn
        rank = used[bucket]
        used[bucket] = rank + 1
        slots[bucket * share + rank] = s
    for fetch in fetches:
        fetch.wait()
    lane = lax.broadcasted_iota(jnp.int32, (1, LANES), 1)
    plane = cell_dev * tiles
    last = share * 6 * tiles
    table = jnp.full((1, LANES), -1.0, f32)
    for m in range(3 * n_pairs):
        kind, turn = m // n_pairs, m % n_pairs
        out = outs[turn]
        label = jnp.full((1, LANES), -1.0, f32)
        for k in range(share):
            s = slots[m * share + k]
            a = lax.rem(cells[0, s], cell_dev)
            live = s < count[0]
            b = jnp.where(live, lax.rem(cells[1, s], cell_dev), -1)
            table = jnp.where(lane == m * share + k, jnp.where(live, a, -1).astype(f32), table)
            label = jnp.where(lane == k, b.astype(f32), label)
            base = row_base(a, tiles)
            for c in range(6):
                source = pos if c < 3 else frc
                row = (k * 6 + c) * tiles
                out[kind, row : row + tiles, :] = source[
                    pl.ds(base + c % 3 * plane, tiles, stride=8), :
                ]
        out[kind, last : last + 1, :] = label
    outs[0][0, last + 1 : last + 2, :] = table


def pair_kernel(sizes, kinds, started, marked, *refs):
    n_space, n_pairs, share, cell_dev, tiles = sizes
    n = len(kinds)
    messages, (pos, frc) = refs[:n], refs[n : n + 2]
    outs = refs[n + 2 + started :]
    (acc, reply), (inbox, feats, grams, totals, todo, middles) = outs[:2], outs[-6:]
    feats[...] = jnp.zeros_like(feats)
    grams[...] = jnp.zeros_like(grams)
    rows_in = share * 6 * tiles
    plane = cell_dev * tiles
    if not started:
        acc[...] = jnp.zeros_like(acc)
    if marked:
        outs[2][...] = jnp.zeros_like(outs[2])
    here = lax.axis_index("space")
    number = jnp.int32(0)
    first = 0
    for kind, message in zip(kinds, messages):
        away = jnp.int32(away_of(kind, lax.rem(here, 2)))
        there = lax.rem(here + away + n_space, n_space)
        half = 0.5 * slab_width * away.astype(f32)
        middle_a = slab_width * (there.astype(f32) + 0.5) - half
        middle_b = slab_width * (here.astype(f32) + 0.5) + half
        for block in range(message.shape[0]):
            inbox[first * rows_in : (first + 1) * rows_in, :] = message[block, 0:rows_in, :]
            label = message[block, rows_in : rows_in + 1, :].astype(jnp.int32)
            for k in range(share):
                b = label[0, k]
                todo[0, number] = first * share + k
                todo[1, number] = b
                middles[0, number] = middle_a
                middles[1, number] = middle_b
                number = number + jnp.where(b >= 0, 1, 0)
            first += 1

    first = lax.broadcasted_iota(jnp.int32, (2 * tiles, LANES), 0) < tiles

    def load(i):
        base = todo[0, i] * (6 * tiles)
        start = row_base(todo[1, i], tiles)
        values = []
        for c in range(6):
            ref = pos if c < 3 else frc
            values.append(
                jnp.concatenate(
                    [
                        inbox[pl.ds(base + c * tiles, tiles), :],
                        ref[pl.ds(start + c % 3 * plane, tiles, stride=8), :],
                    ],
                    axis=0,
                )
            )
        x = [values[0] - jnp.where(first, middles[0, i], middles[1, i])]
        x += [value - across_middle for value in values[1:3]]
        return x, values[3:]

    def store(i, velocity):
        base = todo[0, i] * (3 * tiles)
        start = row_base(todo[1, i], tiles)
        places = [pl.ds(start + c * plane, tiles, stride=8) for c in range(3)]
        added = [acc[places[c], :] + velocity[c][tiles:] for c in range(3)]
        for c in range(3):
            acc[places[c], :] = added[c]
            reply[pl.ds(base + c * tiles, tiles), :] = velocity[c][:tiles]

    def several(numbers):
        cells = [load(i) for i in numbers]
        results = pair_velocities(cells, first, feats, grams, totals)
        for i, result in zip(numbers, results):
            store(i, result)

    def four(i, _):
        several([4 * i + j for j in range(4)])
        return 0

    lax.fori_loop(0, number // 4, four, 0)
    left = lax.rem(number, 4)

    @pl.when(left >= 2)
    def _():
        several([number - left, number - left + 1])

    @pl.when(lax.rem(left, 2) == 1)
    def _():
        several([number - 1])


def add_kernel(sizes, where, acc, mine, *refs):
    n_space, n_pairs, share, cell_dev, tiles = sizes
    replies, out = refs[:-1], refs[-1]
    plane = cell_dev * tiles
    last = share * 6 * tiles
    table = mine[0, last + 1 : last + 2, :].astype(jnp.int32)
    out[...] = acc[...]
    for m, (operand, block) in enumerate(where):
        for k in range(share):
            a = table[0, m * share + k]
            live = a >= 0
            base = row_base(jnp.maximum(a, 0), tiles)
            places = [pl.ds(base + c * plane, tiles, stride=8) for c in range(3)]
            totals = []
            for c in range(3):
                row = (k * 3 + c) * tiles
                term = jnp.where(live, replies[operand][block, row : row + tiles, :], 0.0)
                totals.append(out[places[c], :] + term)
            for c in range(3):
                out[places[c], :] = totals[c]


def flat_rows(cells):
    count, _, points = cells.shape
    value = jnp.transpose(cells, (1, 0, 2)).reshape(3, count // 8, 8, points // LANES, LANES)
    return jnp.transpose(value, (0, 1, 3, 2, 4)).reshape(-1, LANES)


def cell_rows(rows, count, points):
    value = rows.reshape(3, count // 8, points // LANES, 8, LANES)
    value = jnp.transpose(value, (0, 1, 3, 2, 4)).reshape(3, count, points)
    return jnp.transpose(value, (1, 0, 2))


def body(positions, forces, pair_cells, pair_count):
    n_space = lax.axis_size("space")
    n_pairs = lax.axis_size("pairs")
    cell_dev, _, points = positions.shape
    n_slots = pair_cells.shape[1]
    share = n_slots // (3 * n_pairs)
    tiles = points // LANES
    sizes = (n_space, n_pairs, share, cell_dev, tiles)
    rows_in = share * 6 * tiles
    rows_out = share * 3 * tiles
    pos = flat_rows(positions)
    frc = flat_rows(forces)
    vmem = pl.BlockSpec(memory_space=pltpu.VMEM)
    smem = pl.BlockSpec(memory_space=pltpu.SMEM)
    hbm = pl.BlockSpec(memory_space=pltpu.HBM)
    message = jax.ShapeDtypeStruct((3, rows_in + 8, LANES), f32)
    total = jax.ShapeDtypeStruct((3 * cell_dev * tiles, LANES), f32)

    def across(value, turn):
        return lax.ppermute(value, "pairs", [(j, j ^ turn) for j in range(n_pairs)])

    def beyond(value, kind):
        moves = [(i, (i + away_of(kind, i % 2)) % n_space) for i in range(n_space)]
        return lax.ppermute(value, "space", moves)

    sent = pl.pallas_call(
        functools.partial(pack_kernel, sizes),
        out_shape=[message] * n_pairs,
        in_specs=[smem, smem, hbm, hbm],
        out_specs=[vmem] * n_pairs,
        scratch_shapes=[
            pltpu.SMEM((n_slots,), jnp.int32),
            pltpu.SMEM((3 * n_pairs,), jnp.int32),
            pltpu.VMEM(total.shape, f32),
            pltpu.VMEM(total.shape, f32),
            pltpu.SemaphoreType.DMA((2 * PIECES,)),
        ],
        compiler_params=pltpu.CompilerParams(vmem_limit_bytes=60 * 1024 * 1024),
        name="pack",
    )(pair_cells, pair_count, pos, frc)
    got = [sent[0]] + [across(sent[turn], turn) for turn in range(1, n_pairs)]

    def pairs(arrived, before, marked=False):
        kinds = [kind for kind, _ in arrived]
        values = [value for _, value in arrived]
        n = len(values)
        blocks = sum(value.shape[0] for value in values)
        return pl.pallas_call(
            functools.partial(pair_kernel, sizes, kinds, len(before), marked),
            out_shape=[total, jax.ShapeDtypeStruct((blocks * rows_out, LANES), f32)]
            + [jax.ShapeDtypeStruct((1, LANES), f32)] * marked,
            in_specs=[vmem] * (n + 2 + len(before)),
            out_specs=[vmem] * (2 + marked),
            scratch_shapes=[
                pltpu.VMEM((blocks * rows_in, LANES), f32),
                pltpu.VMEM((4, 2 * tiles * FEATURES, LANES), f32),
                pltpu.VMEM((4, 2 * tiles * GRAM, LANES), f32),
                pltpu.VMEM((4, 2 * tiles * FEATURES, LANES), f32),
                pltpu.SMEM((2, blocks * share + 1), jnp.int32),
                pltpu.SMEM((2, blocks * share + 1), f32),
            ],
            input_output_aliases={n + 2: 0} if before else {},
            compiler_params=pltpu.CompilerParams(vmem_limit_bytes=48 * 1024 * 1024),
            cost_estimate=pl.CostEstimate(
                flops=blocks * 1_000_000_000, bytes_accessed=2_000_000, transcendentals=2_000_000
            ),
            name="pairs",
        )(*values, pos, frc, *before)

    near, far = range(2), range(2, n_pairs)
    own = [sent[0][kind : kind + 1] for kind in range(3)]
    core = [got[1][kind : kind + 1] for kind in range(3)]
    out_1n = beyond(jnp.concatenate([own[1], core[1]]), 1)
    acc, reply_0n, nothing = pairs([(0, own[0]), (0, core[0])], [], True)
    rest = [got[turn] + nothing[None] for turn in far]
    out_1f = beyond(jnp.stack([value[1] for value in rest]), 1)
    out_2 = beyond(jnp.concatenate([own[2], core[2]] + [value[2:] for value in rest]), 2)
    acc, reply_m = pairs([(1, out_1n)] + [(0, got[turn][0:1]) for turn in far], [acc])
    acc, reply_f = pairs([(1, out_1f), (2, out_2)], [acc])
    reply_0n, reply_m, reply_f = (
        value.reshape(-1, rows_out, LANES) for value in (reply_0n, reply_m, reply_f)
    )
    cut = n_pairs - 2
    back_0 = jnp.concatenate([reply_0n, reply_m[2:]])
    back_1 = beyond(jnp.concatenate([reply_m[:2], reply_f[:cut]]), 1)
    back_2 = beyond(reply_f[cut:], 2)
    replies = []
    for turn in range(n_pairs):
        value = jnp.stack([back_0[turn], back_1[turn], back_2[turn]])
        replies.append(across(value, turn) if turn else value)
    where = [(turn, kind) for kind in range(3) for turn in range(n_pairs)]
    velocity = pl.pallas_call(
        functools.partial(add_kernel, sizes, where),
        out_shape=total,
        in_specs=[vmem] * (2 + len(replies)),
        out_specs=vmem,
        compiler_params=pltpu.CompilerParams(vmem_limit_bytes=48 * 1024 * 1024),
        name="add",
    )(acc, own[0], *replies)
    return cell_rows(velocity, cell_dev, points)


def solution(mesh):
    placed = (
        P(("space", "pairs"), None, None),
        P(("space", "pairs"), None, None),
        P(None, ("space", "pairs")),
        P(("space", "pairs")),
    )
    return jax.shard_map(
        body,
        mesh=mesh,
        in_specs=placed,
        out_specs=P(("space", "pairs"), None, None),
        check_vma=False,
    )
```

```python
import functools
import math

import jax
import jax.numpy as jnp
from jax import lax
from jax.experimental import pallas as pl
from jax.experimental.pallas import tpu as pltpu
from jax.sharding import PartitionSpec as P

stokes_coef = 1.0 / (8.0 * math.pi)
eps_sq = 0.01
slab_width = 3.0
across_middle = 1.0
LANES = 128
FEATURES = 16
GRAM = 8

f32 = jnp.float32
bf16 = jnp.bfloat16


def split(value, terms):
    parts = []
    for _ in range(terms - 1):
        part = value.astype(bf16).astype(f32)
        parts.append(part)
        value = value - part
    parts.append(value)
    return parts


def matrix(ref, cell, height, tiles):
    first = cell * tiles
    return jnp.concatenate(
        [ref[(first + t) * height : (first + t + 1) * height, :] for t in range(tiles)], axis=1
    )


def lay_out(x, f, first, feat, gram):
    rows = x[0].shape[0]
    norm = x[0] * x[0] + x[1] * x[1] + x[2] * x[2]
    along = x[0] * f[0] + x[1] * f[1] + x[2] * f[2]
    columns = list(f) + [x[k] * f[c] for k in range(3) for c in range(3)]
    columns += [norm * f[c] + x[c] * along for c in range(3)]
    for number, value in enumerate(columns):
        feat[pl.ds(number, rows, stride=FEATURES), :] = value
    scale = jnp.where(first, 1.0, -2.0)
    terms = [x[c] * scale for c in range(3)]
    terms += [jnp.where(first, norm, 1.0), jnp.where(first, 1.0, norm + eps_sq)]
    for number, value in enumerate(terms):
        gram[pl.ds(number, rows, stride=GRAM), :] = value
    return norm


def combine(sums, x, norm):
    rows = norm.shape[0]
    at = [sums[pl.ds(number, rows, stride=FEATURES), :] for number in range(15)]
    force, second = at[0:3], at[12:15]
    moment = [at[3 + 3 * k : 6 + 3 * k] for k in range(3)]
    trace = moment[0][0] + moment[1][1] + moment[2][2]
    along = x[0] * force[0] + x[1] * force[1] + x[2] * force[2] - trace
    size = norm + 2.0 * eps_sq
    out = []
    for c in range(3):
        mixed = x[0] * moment[0][c] + x[1] * moment[1][c] + x[2] * moment[2][c]
        turned = x[0] * moment[c][0] + x[1] * moment[c][1] + x[2] * moment[c][2]
        value = size * force[c] + second[c] - 2.0 * mixed - turned + x[c] * along
        out.append(value * stokes_coef)
    return out


def gram_product(gram, tiles):
    left = split(matrix(gram, 0, GRAM, tiles), 3)
    right = split(matrix(gram, 1, GRAM, tiles), 3)
    order = ((0, 0), (0, 1), (1, 0), (0, 2), (1, 1), (2, 0))
    return dot(
        jnp.concatenate([left[p] for p, _ in order], axis=0).astype(bf16),
        jnp.concatenate([right[q] for _, q in order], axis=0).astype(bf16),
        0,
        0,
    )


def feature_rows(feat, cell, tiles):
    parts = split(matrix(feat, cell, FEATURES, tiles), 3)
    return jnp.concatenate([part.astype(bf16) for part in parts], axis=0)


def dot(left, right, left_dim, right_dim):
    return lax.dot_general(
        left, right, (((left_dim,), (right_dim,)), ((), ())), preferred_element_type=f32
    )


def fold(high, low):
    third = high[2 * FEATURES :]
    both = high[: 2 * FEATURES] + low
    return both[:FEATURES] + both[FEATURES:] + third


def weights(dist_sq):
    inverse = lax.rsqrt(dist_sq)
    cubed = inverse * inverse * inverse
    high = cubed.astype(bf16)
    low = (cubed - high.astype(f32)).astype(bf16)
    return high, low


def pair_velocities(cells, first, feats, grams, totals):
    tiles = cells[0][0][0].shape[0] // 2
    n = len(cells)
    norms = [lay_out(x, f, first, feats.at[i], grams.at[i]) for i, (x, f) in enumerate(cells)]
    squares = [gram_product(grams.at[i], tiles) for i in range(n)]
    rows = [[feature_rows(feats.at[i], cell, tiles) for cell in range(2)] for i in range(n)]
    results = []
    waiting = []

    def finish():
        i, sums = waiting.pop(0)
        for cell in range(2):
            value = fold(*sums[cell])
            for t in range(tiles):
                place = (cell * tiles + t) * FEATURES
                totals[i, place : place + FEATURES, :] = value[:, t * LANES : (t + 1) * LANES]
        results.append(combine(totals.at[i], cells[i][0], norms[i]))

    for i in range(n):
        high, low = weights(squares[i])
        of_b = dot(rows[i][0], high, 1, 0), dot(rows[i][0][: 2 * FEATURES], low, 1, 0)
        of_a = dot(rows[i][1], high, 1, 1), dot(rows[i][1][: 2 * FEATURES], low, 1, 1)
        waiting.append((i, (of_a, of_b)))
        if len(waiting) > 1:
            finish()
    finish()
    return results


def row_base(cell, tiles):
    return cell // 8 * (8 * tiles) + lax.rem(cell, 8)


def away_of(kind, odd):
    return (0, 1 - 2 * odd, 2 * odd - 1)[kind]


def pack_kernel(sizes, cells, count, pos_hbm, frc_hbm, *refs):
    n_space, n_pairs, share, cell_dev, tiles = sizes
    outs = refs[:n_pairs]
    pos, frc, sems = refs[n_pairs:]
    fetches = [
        pltpu.make_async_copy(pos_hbm, pos, sems.at[0]),
        pltpu.make_async_copy(frc_hbm, frc, sems.at[1]),
    ]
    for fetch in fetches:
        fetch.start()
    n_slots = cells.shape[1]
    shape = (n_slots, n_slots)
    down = lax.broadcasted_iota(jnp.int32, shape, 0)
    along = lax.broadcasted_iota(jnp.int32, shape, 1)
    here = lax.axis_index("space")
    here_turn = lax.axis_index("pairs")

    def bucket(cell):
        there = cell >> (cell_dev * n_pairs).bit_length() - 1
        turn = (cell >> cell_dev.bit_length() - 1) & (n_pairs - 1) ^ here_turn
        kind = jnp.where(there == here, 0, jnp.where(there >> 1 == here >> 1, 1, 2))
        return kind * n_pairs + turn

    def column(row):
        return jnp.sum(jnp.where(down == along, row, 0), axis=1, keepdims=True)

    second = column(cells[1:2, :])
    same = (bucket(second) == bucket(cells[1:2, :])) & (along < down)
    rank = jnp.sum(jnp.where(same, 1, 0), axis=1, keepdims=True)
    live = lax.broadcasted_iota(jnp.int32, (n_slots, 1), 0) < count[0]
    chosen = bucket(second) * share + rank == along

    def by_place(values):
        local = jnp.where(live, values & (cell_dev - 1), -1)
        return jnp.sum(jnp.where(chosen, local, 0), axis=0, keepdims=True)

    label = by_place(second)
    table = by_place(column(cells[0:1, :]))
    last = share * 6 * tiles
    plane = cell_dev * tiles
    for fetch in fetches:
        fetch.wait()
    for m in range(3 * n_pairs):
        kind, turn = m // n_pairs, m % n_pairs
        out = outs[turn]
        for k in range(share):
            base = row_base(jnp.maximum(table[0, m * share + k], 0), tiles)
            for c in range(6):
                source = pos if c < 3 else frc
                row = (k * 6 + c) * tiles
                out[kind, row : row + tiles, :] = source[
                    pl.ds(base + c % 3 * plane, tiles, stride=8), :
                ]
        out[kind, last : last + 1, 0:n_slots] = label.astype(f32)
    outs[0][0, last + 1 : last + 2, 0:n_slots] = table.astype(f32)


def pair_kernel(sizes, kinds, started, marked, *refs):
    n_space, n_pairs, share, cell_dev, tiles = sizes
    n = len(kinds)
    messages, (pos, frc) = refs[:n], refs[n : n + 2]
    outs = refs[n + 2 + started :]
    (acc, reply), (inbox, feats, grams, totals, todo, middles) = outs[:2], outs[-6:]
    feats[...] = jnp.zeros_like(feats)
    grams[...] = jnp.zeros_like(grams)
    rows_in = share * 6 * tiles
    n_slots = 3 * n_pairs * share
    plane = cell_dev * tiles
    if not started:
        acc[...] = jnp.zeros_like(acc)
    if marked:
        outs[2][...] = jnp.zeros_like(outs[2])
    here = lax.axis_index("space")
    number = jnp.int32(0)
    first = 0
    for (kind, turns), message in zip(kinds, messages):
        away = jnp.int32(away_of(kind, lax.rem(here, 2)))
        there = lax.rem(here + away + n_space, n_space)
        half = 0.5 * slab_width * away.astype(f32)
        middle_a = slab_width * (there.astype(f32) + 0.5) - half
        middle_b = slab_width * (here.astype(f32) + 0.5) + half
        for block, turn in enumerate(turns):
            inbox[first * rows_in : (first + 1) * rows_in, :] = message[block, 0:rows_in, :]
            label = message[block, rows_in : rows_in + 1, 0:n_slots].astype(jnp.int32)
            for k in range(share):
                b = label[0, (kind * n_pairs + turn) * share + k]
                todo[0, number] = first * share + k
                todo[1, number] = b
                middles[0, number] = middle_a
                middles[1, number] = middle_b
                number = number + jnp.where(b >= 0, 1, 0)
            first += 1

    first = lax.broadcasted_iota(jnp.int32, (2 * tiles, LANES), 0) < tiles

    def load(i):
        base = todo[0, i] * (6 * tiles)
        start = row_base(todo[1, i], tiles)
        values = []
        for c in range(6):
            ref = pos if c < 3 else frc
            values.append(
                jnp.concatenate(
                    [
                        inbox[pl.ds(base + c * tiles, tiles), :],
                        ref[pl.ds(start + c % 3 * plane, tiles, stride=8), :],
                    ],
                    axis=0,
                )
            )
        x = [values[0] - jnp.where(first, middles[0, i], middles[1, i])]
        x += [value - across_middle for value in values[1:3]]
        return x, values[3:]

    def store(i, velocity):
        base = todo[0, i] * (3 * tiles)
        start = row_base(todo[1, i], tiles)
        places = [pl.ds(start + c * plane, tiles, stride=8) for c in range(3)]
        added = [acc[places[c], :] + velocity[c][tiles:] for c in range(3)]
        for c in range(3):
            acc[places[c], :] = added[c]
            reply[pl.ds(base + c * tiles, tiles), :] = velocity[c][:tiles]

    def several(numbers):
        cells = [load(i) for i in numbers]
        results = pair_velocities(cells, first, feats, grams, totals)
        for i, result in zip(numbers, results):
            store(i, result)

    def four(i, _):
        several([4 * i + j for j in range(4)])
        return 0

    lax.fori_loop(0, number // 4, four, 0)
    left = lax.rem(number, 4)

    @pl.when(left >= 2)
    def _():
        several([number - left, number - left + 1])

    @pl.when(lax.rem(left, 2) == 1)
    def _():
        several([number - 1])


def add_kernel(sizes, where, acc, mine, *refs):
    n_space, n_pairs, share, cell_dev, tiles = sizes
    replies, out = refs[:-1], refs[-1]
    plane = cell_dev * tiles
    last = share * 6 * tiles
    table = mine[0, last + 1 : last + 2, 0 : 3 * n_pairs * share].astype(jnp.int32)
    out[...] = acc[...]
    for m, (operand, block) in enumerate(where):
        for k in range(share):
            a = table[0, m * share + k]
            live = a >= 0
            base = row_base(jnp.maximum(a, 0), tiles)
            places = [pl.ds(base + c * plane, tiles, stride=8) for c in range(3)]
            totals = []
            for c in range(3):
                row = (k * 3 + c) * tiles
                term = jnp.where(live, replies[operand][block, row : row + tiles, :], 0.0)
                totals.append(out[places[c], :] + term)
            for c in range(3):
                out[places[c], :] = totals[c]


def flat_rows(cells):
    count, _, points = cells.shape
    value = jnp.transpose(cells, (1, 0, 2)).reshape(3, count // 8, 8, points // LANES, LANES)
    return jnp.transpose(value, (0, 1, 3, 2, 4)).reshape(-1, LANES)


def cell_rows(rows, count, points):
    value = rows.reshape(3, count // 8, points // LANES, 8, LANES)
    value = jnp.transpose(value, (0, 1, 3, 2, 4)).reshape(3, count, points)
    return jnp.transpose(value, (1, 0, 2))


def body(positions, forces, pair_cells, pair_count):
    n_space = lax.axis_size("space")
    n_pairs = lax.axis_size("pairs")
    cell_dev, _, points = positions.shape
    n_slots = pair_cells.shape[1]
    share = n_slots // (3 * n_pairs)
    tiles = points // LANES
    sizes = (n_space, n_pairs, share, cell_dev, tiles)
    rows_in = share * 6 * tiles
    rows_out = share * 3 * tiles
    pos = flat_rows(positions)
    frc = flat_rows(forces)
    vmem = pl.BlockSpec(memory_space=pltpu.VMEM)
    smem = pl.BlockSpec(memory_space=pltpu.SMEM)
    hbm = pl.BlockSpec(memory_space=pltpu.HBM)
    message = jax.ShapeDtypeStruct((3, rows_in + 8, LANES), f32)
    total = jax.ShapeDtypeStruct((3 * cell_dev * tiles, LANES), f32)

    def across(value, turn):
        return lax.ppermute(value, "pairs", [(j, j ^ turn) for j in range(n_pairs)])

    def beyond(value, kind):
        moves = [(i, (i + away_of(kind, i % 2)) % n_space) for i in range(n_space)]
        return lax.ppermute(value, "space", moves)

    sent = pl.pallas_call(
        functools.partial(pack_kernel, sizes),
        out_shape=[message] * n_pairs,
        in_specs=[vmem, smem, hbm, hbm],
        out_specs=[vmem] * n_pairs,
        scratch_shapes=[
            pltpu.VMEM(total.shape, f32),
            pltpu.VMEM(total.shape, f32),
            pltpu.SemaphoreType.DMA((2,)),
        ],
        compiler_params=pltpu.CompilerParams(vmem_limit_bytes=60 * 1024 * 1024),
        name="pack",
    )(pair_cells, pair_count, pos, frc)
    got = [sent[0]] + [across(sent[turn], turn) for turn in range(1, n_pairs)]

    def pairs(arrived, before, marked=False):
        kinds = [(kind, turns) for kind, turns, _ in arrived]
        values = [value for _, _, value in arrived]
        n = len(values)
        blocks = sum(value.shape[0] for value in values)
        return pl.pallas_call(
            functools.partial(pair_kernel, sizes, kinds, len(before), marked),
            out_shape=[total, jax.ShapeDtypeStruct((blocks * rows_out, LANES), f32)]
            + [jax.ShapeDtypeStruct((1, LANES), f32)] * marked,
            in_specs=[vmem] * (n + 2 + len(before)),
            out_specs=[vmem] * (2 + marked),
            scratch_shapes=[
                pltpu.VMEM((blocks * rows_in, LANES), f32),
                pltpu.VMEM((4, 2 * tiles * FEATURES, LANES), f32),
                pltpu.VMEM((4, 2 * tiles * GRAM, LANES), f32),
                pltpu.VMEM((4, 2 * tiles * FEATURES, LANES), f32),
                pltpu.SMEM((2, blocks * share + 1), jnp.int32),
                pltpu.SMEM((2, blocks * share + 1), f32),
            ],
            input_output_aliases={n + 2: 0} if before else {},
            compiler_params=pltpu.CompilerParams(vmem_limit_bytes=48 * 1024 * 1024),
            cost_estimate=pl.CostEstimate(
                flops=blocks * 1_000_000_000, bytes_accessed=2_000_000, transcendentals=2_000_000
            ),
            name="pairs",
        )(*values, pos, frc, *before)

    near, far = range(2), range(2, n_pairs)
    own = [sent[0][kind : kind + 1] for kind in range(3)]
    core = [got[1][kind : kind + 1] for kind in range(3)]
    out_1n = beyond(jnp.concatenate([own[1], core[1]]), 1)
    acc, reply_0n, nothing = pairs([(0, (0,), own[0]), (0, (1,), core[0])], [], True)
    rest = [got[turn] + nothing[None] for turn in far]
    out_1f = beyond(jnp.stack([value[1] for value in rest]), 1)
    out_2 = beyond(jnp.concatenate([own[2], core[2]] + [value[2:] for value in rest]), 2)
    acc, reply_m = pairs(
        [(1, near, out_1n)] + [(0, (turn,), got[turn][0:1]) for turn in far], [acc]
    )
    acc, reply_f = pairs([(1, far, out_1f), (2, range(n_pairs), out_2)], [acc])
    reply_0n, reply_m, reply_f = (
        value.reshape(-1, rows_out, LANES) for value in (reply_0n, reply_m, reply_f)
    )
    cut = n_pairs - 2
    back_0 = jnp.concatenate([reply_0n, reply_m[2:]])
    back_1 = beyond(jnp.concatenate([reply_m[:2], reply_f[:cut]]), 1)
    back_2 = beyond(reply_f[cut:], 2)
    replies = []
    for turn in range(n_pairs):
        value = jnp.stack([back_0[turn], back_1[turn], back_2[turn]])
        replies.append(across(value, turn) if turn else value)
    where = [(turn, kind) for kind in range(3) for turn in range(n_pairs)]
    velocity = pl.pallas_call(
        functools.partial(add_kernel, sizes, where),
        out_shape=total,
        in_specs=[vmem] * (2 + len(replies)),
        out_specs=vmem,
        compiler_params=pltpu.CompilerParams(vmem_limit_bytes=48 * 1024 * 1024),
        name="add",
    )(acc, own[0], *replies)
    return cell_rows(velocity, cell_dev, points)


def solution(mesh):
    placed = (
        P(("space", "pairs"), None, None),
        P(("space", "pairs"), None, None),
        P(None, ("space", "pairs")),
        P(("space", "pairs")),
    )
    return jax.shard_map(
        body,
        mesh=mesh,
        in_specs=placed,
        out_specs=P(("space", "pairs"), None, None),
        check_vma=False,
    )
```

```python
import functools
import math

import jax
import jax.numpy as jnp
from jax import lax
from jax.experimental import pallas as pl
from jax.experimental.pallas import tpu as pltpu
from jax.sharding import PartitionSpec as P

stokes_coef = 1.0 / (8.0 * math.pi)
eps_sq = 0.01
slab_width = 3.0
across_middle = 1.0
LANES = 128
FEATURES = 16
GRAM = 8

f32 = jnp.float32
bf16 = jnp.bfloat16


def split(value, terms):
    parts = []
    for _ in range(terms - 1):
        part = value.astype(bf16).astype(f32)
        parts.append(part)
        value = value - part
    parts.append(value)
    return parts


def matrix(ref, cell, height, tiles):
    first = cell * tiles
    return jnp.concatenate(
        [ref[(first + t) * height : (first + t + 1) * height, :] for t in range(tiles)], axis=1
    )


def lay_out(x, f, first, feat, gram):
    rows = x[0].shape[0]
    norm = x[0] * x[0] + x[1] * x[1] + x[2] * x[2]
    along = x[0] * f[0] + x[1] * f[1] + x[2] * f[2]
    columns = list(f) + [x[k] * f[c] for k in range(3) for c in range(3)]
    columns += [norm * f[c] + x[c] * along for c in range(3)]
    for number, value in enumerate(columns):
        feat[pl.ds(number, rows, stride=FEATURES), :] = value
    scale = jnp.where(first, 1.0, -2.0)
    terms = [x[c] * scale for c in range(3)]
    terms += [jnp.where(first, norm, 1.0), jnp.where(first, 1.0, norm + eps_sq)]
    for number, value in enumerate(terms):
        gram[pl.ds(number, rows, stride=GRAM), :] = value
    return norm


def combine(sums, x, norm):
    rows = norm.shape[0]
    at = [sums[pl.ds(number, rows, stride=FEATURES), :] for number in range(15)]
    force, second = at[0:3], at[12:15]
    moment = [at[3 + 3 * k : 6 + 3 * k] for k in range(3)]
    trace = moment[0][0] + moment[1][1] + moment[2][2]
    along = x[0] * force[0] + x[1] * force[1] + x[2] * force[2] - trace
    size = norm + 2.0 * eps_sq
    out = []
    for c in range(3):
        mixed = x[0] * moment[0][c] + x[1] * moment[1][c] + x[2] * moment[2][c]
        turned = x[0] * moment[c][0] + x[1] * moment[c][1] + x[2] * moment[c][2]
        value = size * force[c] + second[c] - 2.0 * mixed - turned + x[c] * along
        out.append(value * stokes_coef)
    return out


def gram_product(gram, tiles):
    left = split(matrix(gram, 0, GRAM, tiles), 3)
    right = split(matrix(gram, 1, GRAM, tiles), 3)
    order = ((0, 0), (0, 1), (1, 0), (0, 2), (1, 1), (2, 0))
    return dot(
        jnp.concatenate([left[p] for p, _ in order], axis=0).astype(bf16),
        jnp.concatenate([right[q] for _, q in order], axis=0).astype(bf16),
        0,
        0,
    )


def feature_rows(feat, cell, tiles):
    parts = split(matrix(feat, cell, FEATURES, tiles), 3)
    return jnp.concatenate([part.astype(bf16) for part in parts], axis=0)


def dot(left, right, left_dim, right_dim):
    return lax.dot_general(
        left, right, (((left_dim,), (right_dim,)), ((), ())), preferred_element_type=f32
    )


def fold(high, low):
    third = high[2 * FEATURES :]
    both = high[: 2 * FEATURES] + low
    return both[:FEATURES] + both[FEATURES:] + third


def weights(dist_sq):
    inverse = lax.rsqrt(dist_sq)
    cubed = inverse * inverse * inverse
    high = cubed.astype(bf16)
    low = (cubed - high.astype(f32)).astype(bf16)
    return high, low


def pair_velocities(cells, first, feats, grams, totals):
    tiles = cells[0][0][0].shape[0] // 2
    n = len(cells)
    norms = [lay_out(x, f, first, feats.at[i], grams.at[i]) for i, (x, f) in enumerate(cells)]
    squares = [gram_product(grams.at[i], tiles) for i in range(n)]
    rows = [[feature_rows(feats.at[i], cell, tiles) for cell in range(2)] for i in range(n)]
    results = []
    waiting = []

    def finish():
        i, sums = waiting.pop(0)
        for cell in range(2):
            value = fold(*sums[cell])
            for t in range(tiles):
                place = (cell * tiles + t) * FEATURES
                totals[i, place : place + FEATURES, :] = value[:, t * LANES : (t + 1) * LANES]
        results.append(combine(totals.at[i], cells[i][0], norms[i]))

    for i in range(n):
        high, low = weights(squares[i])
        of_b = dot(rows[i][0], high, 1, 0), dot(rows[i][0][: 2 * FEATURES], low, 1, 0)
        of_a = dot(rows[i][1], high, 1, 1), dot(rows[i][1][: 2 * FEATURES], low, 1, 1)
        waiting.append((i, (of_a, of_b)))
        if len(waiting) > 1:
            finish()
    finish()
    return results


def row_base(cell, tiles):
    return cell // 8 * (8 * tiles) + lax.rem(cell, 8)


def away_of(kind, odd):
    return (0, 1 - 2 * odd, 2 * odd - 1)[kind]


def pack_kernel(sizes, cells_hbm, count, pos_hbm, frc_hbm, *refs):
    n_space, n_pairs, share, cell_dev, tiles = sizes
    outs = refs[:n_pairs]
    cells, pos, frc, sems = refs[n_pairs:]
    fetches = [
        pltpu.make_async_copy(cells_hbm, cells, sems.at[0]),
        pltpu.make_async_copy(pos_hbm, pos, sems.at[1]),
        pltpu.make_async_copy(frc_hbm, frc, sems.at[2]),
    ]
    for fetch in fetches:
        fetch.start()
    fetches.pop(0).wait()
    n_slots = cells.shape[1]
    shape = (n_slots, n_slots)
    down = lax.broadcasted_iota(jnp.int32, shape, 0)
    along = lax.broadcasted_iota(jnp.int32, shape, 1)
    here = lax.axis_index("space")
    here_turn = lax.axis_index("pairs")

    def bucket(cell):
        there = cell >> (cell_dev * n_pairs).bit_length() - 1
        turn = (cell >> cell_dev.bit_length() - 1) & (n_pairs - 1) ^ here_turn
        kind = jnp.where(there == here, 0, jnp.where(there >> 1 == here >> 1, 1, 2))
        return kind * n_pairs + turn

    def column(row):
        return jnp.sum(jnp.where(down == along, row, 0), axis=1, keepdims=True)

    second = column(cells[1:2, :])
    same = (bucket(second) == bucket(cells[1:2, :])) & (along < down)
    rank = jnp.sum(jnp.where(same, 1, 0), axis=1, keepdims=True)
    live = lax.broadcasted_iota(jnp.int32, (n_slots, 1), 0) < count[0]
    chosen = bucket(second) * share + rank == along

    def by_place(values):
        local = jnp.where(live, values & (cell_dev - 1), -1)
        return jnp.sum(jnp.where(chosen, local, 0), axis=0, keepdims=True)

    label = by_place(second)
    table = by_place(column(cells[0:1, :]))
    last = share * 6 * tiles
    plane = cell_dev * tiles
    for fetch in fetches:
        fetch.wait()
    for m in range(3 * n_pairs):
        kind, turn = m // n_pairs, m % n_pairs
        out = outs[turn]
        for k in range(share):
            base = row_base(jnp.maximum(table[0, m * share + k], 0), tiles)
            for c in range(6):
                source = pos if c < 3 else frc
                row = (k * 6 + c) * tiles
                out[kind, row : row + tiles, :] = source[
                    pl.ds(base + c % 3 * plane, tiles, stride=8), :
                ]
        out[kind, last : last + 1, 0:n_slots] = label.astype(f32)
    outs[0][0, last + 1 : last + 2, 0:n_slots] = table.astype(f32)


def pair_kernel(sizes, kinds, started, marked, *refs):
    n_space, n_pairs, share, cell_dev, tiles = sizes
    n = len(kinds)
    messages, (pos, frc) = refs[:n], refs[n : n + 2]
    outs = refs[n + 2 + started :]
    (acc, reply), (inbox, feats, grams, totals, todo, middles) = outs[:2], outs[-6:]
    feats[...] = jnp.zeros_like(feats)
    grams[...] = jnp.zeros_like(grams)
    rows_in = share * 6 * tiles
    n_slots = 3 * n_pairs * share
    plane = cell_dev * tiles
    if not started:
        acc[...] = jnp.zeros_like(acc)
    if marked:
        outs[2][...] = jnp.zeros_like(outs[2])
    here = lax.axis_index("space")
    number = jnp.int32(0)
    first = 0
    for (kind, turns), message in zip(kinds, messages):
        away = jnp.int32(away_of(kind, lax.rem(here, 2)))
        there = lax.rem(here + away + n_space, n_space)
        half = 0.5 * slab_width * away.astype(f32)
        middle_a = slab_width * (there.astype(f32) + 0.5) - half
        middle_b = slab_width * (here.astype(f32) + 0.5) + half
        for block, turn in enumerate(turns):
            inbox[first * rows_in : (first + 1) * rows_in, :] = message[block, 0:rows_in, :]
            label = message[block, rows_in : rows_in + 1, 0:n_slots].astype(jnp.int32)
            for k in range(share):
                b = label[0, (kind * n_pairs + turn) * share + k]
                todo[0, number] = first * share + k
                todo[1, number] = b
                middles[0, number] = middle_a
                middles[1, number] = middle_b
                number = number + jnp.where(b >= 0, 1, 0)
            first += 1

    first = lax.broadcasted_iota(jnp.int32, (2 * tiles, LANES), 0) < tiles

    def load(i):
        base = todo[0, i] * (6 * tiles)
        start = row_base(todo[1, i], tiles)
        values = []
        for c in range(6):
            ref = pos if c < 3 else frc
            values.append(
                jnp.concatenate(
                    [
                        inbox[pl.ds(base + c * tiles, tiles), :],
                        ref[pl.ds(start + c % 3 * plane, tiles, stride=8), :],
                    ],
                    axis=0,
                )
            )
        x = [values[0] - jnp.where(first, middles[0, i], middles[1, i])]
        x += [value - across_middle for value in values[1:3]]
        return x, values[3:]

    def store(i, velocity):
        base = todo[0, i] * (3 * tiles)
        start = row_base(todo[1, i], tiles)
        places = [pl.ds(start + c * plane, tiles, stride=8) for c in range(3)]
        added = [acc[places[c], :] + velocity[c][tiles:] for c in range(3)]
        for c in range(3):
            acc[places[c], :] = added[c]
            reply[pl.ds(base + c * tiles, tiles), :] = velocity[c][:tiles]

    def several(numbers):
        cells = [load(i) for i in numbers]
        results = pair_velocities(cells, first, feats, grams, totals)
        for i, result in zip(numbers, results):
            store(i, result)

    def four(i, _):
        several([4 * i + j for j in range(4)])
        return 0

    lax.fori_loop(0, number // 4, four, 0)
    left = lax.rem(number, 4)

    @pl.when(left >= 2)
    def _():
        several([number - left, number - left + 1])

    @pl.when(lax.rem(left, 2) == 1)
    def _():
        several([number - 1])


def add_kernel(sizes, where, acc, mine, *refs):
    n_space, n_pairs, share, cell_dev, tiles = sizes
    replies, out = refs[:-1], refs[-1]
    plane = cell_dev * tiles
    last = share * 6 * tiles
    table = mine[0, last + 1 : last + 2, 0 : 3 * n_pairs * share].astype(jnp.int32)
    out[...] = acc[...]
    for m, (operand, block) in enumerate(where):
        for k in range(share):
            a = table[0, m * share + k]
            live = a >= 0
            base = row_base(jnp.maximum(a, 0), tiles)
            places = [pl.ds(base + c * plane, tiles, stride=8) for c in range(3)]
            totals = []
            for c in range(3):
                row = (k * 3 + c) * tiles
                term = jnp.where(live, replies[operand][block, row : row + tiles, :], 0.0)
                totals.append(out[places[c], :] + term)
            for c in range(3):
                out[places[c], :] = totals[c]


def flat_rows(cells):
    count, _, points = cells.shape
    value = jnp.transpose(cells, (1, 0, 2)).reshape(3, count // 8, 8, points // LANES, LANES)
    return jnp.transpose(value, (0, 1, 3, 2, 4)).reshape(-1, LANES)


def cell_rows(rows, count, points):
    value = rows.reshape(3, count // 8, points // LANES, 8, LANES)
    value = jnp.transpose(value, (0, 1, 3, 2, 4)).reshape(3, count, points)
    return jnp.transpose(value, (1, 0, 2))


def body(positions, forces, pair_cells, pair_count):
    n_space = lax.axis_size("space")
    n_pairs = lax.axis_size("pairs")
    cell_dev, _, points = positions.shape
    n_slots = pair_cells.shape[1]
    share = n_slots // (3 * n_pairs)
    tiles = points // LANES
    sizes = (n_space, n_pairs, share, cell_dev, tiles)
    rows_in = share * 6 * tiles
    rows_out = share * 3 * tiles
    pos = flat_rows(positions)
    frc = flat_rows(forces)
    vmem = pl.BlockSpec(memory_space=pltpu.VMEM)
    smem = pl.BlockSpec(memory_space=pltpu.SMEM)
    hbm = pl.BlockSpec(memory_space=pltpu.HBM)
    message = jax.ShapeDtypeStruct((3, rows_in + 8, LANES), f32)
    total = jax.ShapeDtypeStruct((3 * cell_dev * tiles, LANES), f32)

    def across(value, turn):
        return lax.ppermute(value, "pairs", [(j, j ^ turn) for j in range(n_pairs)])

    def beyond(value, kind):
        moves = [(i, (i + away_of(kind, i % 2)) % n_space) for i in range(n_space)]
        return lax.ppermute(value, "space", moves)

    sent = pl.pallas_call(
        functools.partial(pack_kernel, sizes),
        out_shape=[message] * n_pairs,
        in_specs=[hbm, smem, hbm, hbm],
        out_specs=[vmem] * n_pairs,
        scratch_shapes=[
            pltpu.VMEM(pair_cells.shape, jnp.int32),
            pltpu.VMEM(total.shape, f32),
            pltpu.VMEM(total.shape, f32),
            pltpu.SemaphoreType.DMA((3,)),
        ],
        compiler_params=pltpu.CompilerParams(vmem_limit_bytes=60 * 1024 * 1024),
        name="pack",
    )(pair_cells, pair_count, pos, frc)
    got = [sent[0]] + [across(sent[turn], turn) for turn in range(1, n_pairs)]

    def pairs(arrived, before, marked=False):
        kinds = [(kind, turns) for kind, turns, _ in arrived]
        values = [value for _, _, value in arrived]
        n = len(values)
        blocks = sum(value.shape[0] for value in values)
        return pl.pallas_call(
            functools.partial(pair_kernel, sizes, kinds, len(before), marked),
            out_shape=[total, jax.ShapeDtypeStruct((blocks * rows_out, LANES), f32)]
            + [jax.ShapeDtypeStruct((1, LANES), f32)] * marked,
            in_specs=[vmem] * (n + 2 + len(before)),
            out_specs=[vmem] * (2 + marked),
            scratch_shapes=[
                pltpu.VMEM((blocks * rows_in, LANES), f32),
                pltpu.VMEM((4, 2 * tiles * FEATURES, LANES), f32),
                pltpu.VMEM((4, 2 * tiles * GRAM, LANES), f32),
                pltpu.VMEM((4, 2 * tiles * FEATURES, LANES), f32),
                pltpu.SMEM((2, blocks * share + 1), jnp.int32),
                pltpu.SMEM((2, blocks * share + 1), f32),
            ],
            input_output_aliases={n + 2: 0} if before else {},
            compiler_params=pltpu.CompilerParams(vmem_limit_bytes=48 * 1024 * 1024),
            cost_estimate=pl.CostEstimate(
                flops=blocks * 1_000_000_000, bytes_accessed=2_000_000, transcendentals=2_000_000
            ),
            name="pairs",
        )(*values, pos, frc, *before)

    near, far = range(2), range(2, n_pairs)
    own = [sent[0][kind : kind + 1] for kind in range(3)]
    core = [got[1][kind : kind + 1] for kind in range(3)]
    out_1n = beyond(jnp.concatenate([own[1], core[1]]), 1)
    acc, reply_0n, nothing = pairs([(0, (0,), own[0]), (0, (1,), core[0])], [], True)
    rest = [got[turn] + nothing[None] for turn in far]
    out_1f = beyond(jnp.stack([value[1] for value in rest]), 1)
    out_2 = beyond(jnp.concatenate([own[2], core[2]] + [value[2:] for value in rest]), 2)
    acc, reply_m = pairs(
        [(1, near, out_1n)] + [(0, (turn,), got[turn][0:1]) for turn in far], [acc]
    )
    acc, reply_f = pairs([(1, far, out_1f), (2, range(n_pairs), out_2)], [acc])
    reply_0n, reply_m, reply_f = (
        value.reshape(-1, rows_out, LANES) for value in (reply_0n, reply_m, reply_f)
    )
    cut = n_pairs - 2
    back_0 = jnp.concatenate([reply_0n, reply_m[2:]])
    back_1 = beyond(jnp.concatenate([reply_m[:2], reply_f[:cut]]), 1)
    back_2 = beyond(reply_f[cut:], 2)
    replies = []
    for turn in range(n_pairs):
        value = jnp.stack([back_0[turn], back_1[turn], back_2[turn]])
        replies.append(across(value, turn) if turn else value)
    where = [(turn, kind) for kind in range(3) for turn in range(n_pairs)]
    velocity = pl.pallas_call(
        functools.partial(add_kernel, sizes, where),
        out_shape=total,
        in_specs=[vmem] * (2 + len(replies)),
        out_specs=vmem,
        compiler_params=pltpu.CompilerParams(vmem_limit_bytes=48 * 1024 * 1024),
        name="add",
    )(acc, own[0], *replies)
    return cell_rows(velocity, cell_dev, points)


def solution(mesh):
    placed = (
        P(("space", "pairs"), None, None),
        P(("space", "pairs"), None, None),
        P(None, ("space", "pairs")),
        P(("space", "pairs")),
    )
    return jax.shard_map(
        body,
        mesh=mesh,
        in_specs=placed,
        out_specs=P(("space", "pairs"), None, None),
        check_vma=False,
    )
```

```python
import functools
import math

import jax
import jax.numpy as jnp
from jax import lax
from jax.experimental import pallas as pl
from jax.experimental.pallas import tpu as pltpu
from jax.sharding import PartitionSpec as P

stokes_coef = 1.0 / (8.0 * math.pi)
eps_sq = 0.01
slab_width = 3.0
across_middle = 1.0
LANES = 128
FEATURES = 16
GRAM = 8
SPARE = 64
TILE = 8

f32 = jnp.float32
bf16 = jnp.bfloat16


def split(value, terms):
    parts = []
    for _ in range(terms - 1):
        part = value.astype(bf16).astype(f32)
        parts.append(part)
        value = value - part
    parts.append(value)
    return parts


def matrix(ref, cell, height, tiles):
    first = cell * tiles
    return jnp.concatenate(
        [ref[(first + t) * height : (first + t + 1) * height, :] for t in range(tiles)], axis=1
    )


def lay_out(x, f, first, feat, gram):
    rows = x[0].shape[0]
    norm = x[0] * x[0] + x[1] * x[1] + x[2] * x[2]
    along = x[0] * f[0] + x[1] * f[1] + x[2] * f[2]
    columns = list(f) + [x[k] * f[c] for k in range(3) for c in range(3)]
    columns += [norm * f[c] + x[c] * along for c in range(3)]
    for number, value in enumerate(columns):
        feat[pl.ds(number, rows, stride=FEATURES), :] = value
    scale = jnp.where(first, 1.0, -2.0)
    terms = [x[c] * scale for c in range(3)]
    terms += [jnp.where(first, norm, 1.0), jnp.where(first, 1.0, norm + eps_sq)]
    for number, value in enumerate(terms):
        gram[pl.ds(number, rows, stride=GRAM), :] = value
    return norm


def combine(sums, x, norm):
    rows = norm.shape[0]
    at = [sums[pl.ds(number, rows, stride=FEATURES), :] for number in range(15)]
    force, second = at[0:3], at[12:15]
    moment = [at[3 + 3 * k : 6 + 3 * k] for k in range(3)]
    trace = moment[0][0] + moment[1][1] + moment[2][2]
    along = x[0] * force[0] + x[1] * force[1] + x[2] * force[2] - trace
    size = norm + 2.0 * eps_sq
    out = []
    for c in range(3):
        mixed = x[0] * moment[0][c] + x[1] * moment[1][c] + x[2] * moment[2][c]
        turned = x[0] * moment[c][0] + x[1] * moment[c][1] + x[2] * moment[c][2]
        value = size * force[c] + second[c] - 2.0 * mixed - turned + x[c] * along
        out.append(value * stokes_coef)
    return out


def gram_product(gram, tiles):
    left = split(matrix(gram, 0, GRAM, tiles), 3)
    right = split(matrix(gram, 1, GRAM, tiles), 3)
    order = ((0, 0), (0, 1), (1, 0), (0, 2), (1, 1), (2, 0))
    return dot(
        jnp.concatenate([left[p] for p, _ in order], axis=0).astype(bf16),
        jnp.concatenate([right[q] for _, q in order], axis=0).astype(bf16),
        0,
        0,
    )


def feature_rows(feat, cell, tiles):
    parts = split(matrix(feat, cell, FEATURES, tiles), 3)
    return jnp.concatenate([part.astype(bf16) for part in parts], axis=0)


def dot(left, right, left_dim, right_dim):
    return lax.dot_general(
        left, right, (((left_dim,), (right_dim,)), ((), ())), preferred_element_type=f32
    )


def fold(high, low):
    third = high[2 * FEATURES :]
    both = high[: 2 * FEATURES] + low
    return both[:FEATURES] + both[FEATURES:] + third


def weights(dist_sq):
    inverse = lax.rsqrt(dist_sq)
    cubed = inverse * inverse * inverse
    high = cubed.astype(bf16)
    low = (cubed - high.astype(f32)).astype(bf16)
    return high, low


def pair_velocities(cells, first, feats, grams, totals):
    tiles = cells[0][0][0].shape[0] // 2
    n = len(cells)
    norms = [lay_out(x, f, first, feats.at[i], grams.at[i]) for i, (x, f) in enumerate(cells)]
    squares = [gram_product(grams.at[i], tiles) for i in range(n)]
    rows = [[feature_rows(feats.at[i], cell, tiles) for cell in range(2)] for i in range(n)]
    results = []
    waiting = []

    def finish():
        i, sums = waiting.pop(0)
        for cell in range(2):
            value = fold(*sums[cell])
            for t in range(tiles):
                place = (cell * tiles + t) * FEATURES
                totals[i, place : place + FEATURES, :] = value[:, t * LANES : (t + 1) * LANES]
        results.append(combine(totals.at[i], cells[i][0], norms[i]))

    for i in range(n):
        high, low = weights(squares[i])
        of_b = dot(rows[i][0], high, 1, 0), dot(rows[i][0][: 2 * FEATURES], low, 1, 0)
        of_a = dot(rows[i][1], high, 1, 1), dot(rows[i][1][: 2 * FEATURES], low, 1, 1)
        waiting.append((i, (of_a, of_b)))
        if len(waiting) > 1:
            finish()
    finish()
    return results


def row_base(cell, tiles):
    return cell // 8 * (8 * tiles) + lax.rem(cell, 8)


def away_of(kind, odd):
    return (0, 1 - 2 * odd, 2 * odd - 1)[kind]


def pack_kernel(sizes, cells_hbm, count, pos_hbm, frc_hbm, *refs):
    n_space, n_pairs, share, cell_dev, tiles = sizes
    outs = refs[:n_pairs]
    cells, pos, frc, sems = refs[n_pairs:]
    fetches = [
        pltpu.make_async_copy(cells_hbm, cells, sems.at[0]),
        pltpu.make_async_copy(pos_hbm, pos.at[pl.ds(0, pos_hbm.shape[0])], sems.at[1]),
        pltpu.make_async_copy(frc_hbm, frc.at[pl.ds(0, frc_hbm.shape[0])], sems.at[2]),
    ]
    for fetch in fetches:
        fetch.start()
    fetches.pop(0).wait()
    n_slots = cells.shape[1]
    shape = (n_slots, n_slots)
    down = lax.broadcasted_iota(jnp.int32, shape, 0)
    along = lax.broadcasted_iota(jnp.int32, shape, 1)
    here = lax.axis_index("space")
    here_turn = lax.axis_index("pairs")

    def bucket(cell):
        there = cell >> (cell_dev * n_pairs).bit_length() - 1
        turn = (cell >> cell_dev.bit_length() - 1) & (n_pairs - 1) ^ here_turn
        kind = jnp.where(there == here, 0, jnp.where(there >> 1 == here >> 1, 1, 2))
        return kind * n_pairs + turn

    def column(row):
        return jnp.sum(jnp.where(down == along, row, 0), axis=1, keepdims=True)

    second = column(cells[1:2, :])
    same = (bucket(second) == bucket(cells[1:2, :])) & (along < down)
    rank = jnp.sum(jnp.where(same, 1, 0), axis=1, keepdims=True)
    live = lax.broadcasted_iota(jnp.int32, (n_slots, 1), 0) < count[0]
    chosen = bucket(second) * share + rank == along

    def by_place(values):
        local = jnp.where(live, values & (cell_dev - 1), -1)
        return jnp.sum(jnp.where(chosen, local, 0), axis=0, keepdims=True)

    label = by_place(second)
    table = by_place(column(cells[0:1, :]))
    last = share * 6 * tiles
    plane = cell_dev * tiles
    for fetch in fetches:
        fetch.wait()
    for m in range(3 * n_pairs):
        kind, turn = m // n_pairs, m % n_pairs
        out = outs[turn]
        for k in range(share):
            base = row_base(jnp.maximum(table[0, m * share + k], 0), tiles)
            for c in range(6):
                source = pos if c < 3 else frc
                row = (k * 6 + c) * tiles
                out[kind, row : row + tiles, :] = source[
                    pl.ds(base + c % 3 * plane, tiles, stride=8), :
                ]
        out[kind, last : last + 1, 0:n_slots] = label.astype(f32)
    outs[0][0, last + 1 : last + 2, 0:n_slots] = table.astype(f32)


def pair_kernel(sizes, kinds, started, marked, *refs):
    n_space, n_pairs, share, cell_dev, tiles = sizes
    n = len(kinds)
    messages, (pos_in, frc_in) = refs[:n], refs[n : n + 2]
    outs = refs[n + 2 + started :]
    (acc, reply), (inbox, pos, frc, feats, grams, totals, todo, middles) = outs[:2], outs[-8:]
    pos[0 : pos_in.shape[0], :] = pos_in[...]
    frc[0 : frc_in.shape[0], :] = frc_in[...]
    feats[...] = jnp.zeros_like(feats)
    grams[...] = jnp.zeros_like(grams)
    rows_in = share * 6 * tiles
    n_slots = 3 * n_pairs * share
    plane = cell_dev * tiles
    if not started:
        acc[...] = jnp.zeros_like(acc)
    if marked:
        outs[2][...] = jnp.zeros_like(outs[2])
    here = lax.axis_index("space")
    number = jnp.int32(0)
    first = 0
    for (kind, turns), message in zip(kinds, messages):
        away = jnp.int32(away_of(kind, lax.rem(here, 2)))
        there = lax.rem(here + away + n_space, n_space)
        half = 0.5 * slab_width * away.astype(f32)
        middle_a = slab_width * (there.astype(f32) + 0.5) - half
        middle_b = slab_width * (here.astype(f32) + 0.5) + half
        for block, turn in enumerate(turns):
            inbox[first * rows_in : (first + 1) * rows_in, :] = message[block, 0:rows_in, :]
            label = message[block, rows_in : rows_in + 1, 0:n_slots].astype(jnp.int32)
            for k in range(share):
                b = label[0, (kind * n_pairs + turn) * share + k]
                todo[0, number] = first * share + k
                todo[1, number] = b
                middles[0, number] = middle_a
                middles[1, number] = middle_b
                number = number + jnp.where(b >= 0, 1, 0)
            first += 1

    first = lax.broadcasted_iota(jnp.int32, (2 * tiles, LANES), 0) < tiles

    def load(i):
        base = todo[0, i] * (6 * tiles)
        start = row_base(todo[1, i], tiles)
        values = []
        for c in range(6):
            ref = pos if c < 3 else frc
            values.append(
                jnp.concatenate(
                    [
                        inbox[pl.ds(base + c * tiles, tiles), :],
                        ref[pl.ds(start + c % 3 * plane, tiles, stride=8), :],
                    ],
                    axis=0,
                )
            )
        x = [values[0] - jnp.where(first, middles[0, i], middles[1, i])]
        x += [value - across_middle for value in values[1:3]]
        return x, values[3:]

    def store(i, velocity):
        base = todo[0, i] * (3 * tiles)
        start = row_base(todo[1, i], tiles)
        places = [pl.ds(start + c * plane, tiles, stride=8) for c in range(3)]
        added = [acc[places[c], :] + velocity[c][tiles:] for c in range(3)]
        for c in range(3):
            acc[places[c], :] = added[c]
            reply[pl.ds(base + c * tiles, tiles), :] = velocity[c][:tiles]

    def several(numbers):
        cells = [load(i) for i in numbers]
        results = pair_velocities(cells, first, feats, grams, totals)
        for i, result in zip(numbers, results):
            store(i, result)

    def four(i, _):
        several([4 * i + j for j in range(4)])
        return 0

    lax.fori_loop(0, number // 4, four, 0)
    left = lax.rem(number, 4)

    @pl.when(left >= 2)
    def _():
        several([number - left, number - left + 1])

    @pl.when(lax.rem(left, 2) == 1)
    def _():
        several([number - 1])


def add_kernel(sizes, where, acc, mine, *refs):
    n_space, n_pairs, share, cell_dev, tiles = sizes
    replies, (out, kept) = refs[:-2], refs[-2:]
    plane = cell_dev * tiles
    last = share * 6 * tiles
    table = mine[0, last + 1 : last + 2, 0 : 3 * n_pairs * share].astype(jnp.int32)
    kept[...] = acc[...]
    for m, (operand, block) in enumerate(where):
        for k in range(share):
            a = table[0, m * share + k]
            live = a >= 0
            base = row_base(jnp.maximum(a, 0), tiles)
            places = [pl.ds(base + c * plane, tiles, stride=8) for c in range(3)]
            totals = []
            for c in range(3):
                row = (k * 3 + c) * tiles
                term = jnp.where(live, replies[operand][block, row : row + tiles, :], 0.0)
                totals.append(kept[places[c], :] + term)
            for c in range(3):
                kept[places[c], :] = totals[c]
    out[...] = kept[0 : out.shape[0], :]


def flat_rows(cells):
    count, _, points = cells.shape
    value = jnp.transpose(cells, (1, 0, 2)).reshape(3, count // 8, 8, points // LANES, LANES)
    return jnp.transpose(value, (0, 1, 3, 2, 4)).reshape(-1, LANES)


def cell_rows(rows, count, points):
    value = rows.reshape(3, count // 8, points // LANES, 8, LANES)
    value = jnp.transpose(value, (0, 1, 3, 2, 4)).reshape(3, count, points)
    return jnp.transpose(value, (1, 0, 2))


def body(positions, forces, pair_cells, pair_count):
    n_space = lax.axis_size("space")
    n_pairs = lax.axis_size("pairs")
    cell_dev, _, points = positions.shape
    n_slots = pair_cells.shape[1]
    share = n_slots // (3 * n_pairs)
    tiles = points // LANES
    sizes = (n_space, n_pairs, share, cell_dev, tiles)
    rows_in = share * 6 * tiles
    rows_out = share * 3 * tiles
    pos = flat_rows(positions)
    frc = flat_rows(forces)
    vmem = pl.BlockSpec(memory_space=pltpu.VMEM)
    smem = pl.BlockSpec(memory_space=pltpu.SMEM)
    hbm = pl.BlockSpec(memory_space=pltpu.HBM)
    message = jax.ShapeDtypeStruct((3, rows_in + 8, LANES), f32)
    total = jax.ShapeDtypeStruct((3 * cell_dev * tiles + SPARE, LANES), f32)
    result = jax.ShapeDtypeStruct((3 * cell_dev * tiles, LANES), f32)

    def across(value, turn):
        return lax.ppermute(value, "pairs", [(j, j ^ turn) for j in range(n_pairs)])

    def beyond(value, kind):
        moves = [(i, (i + away_of(kind, i % 2)) % n_space) for i in range(n_space)]
        return lax.ppermute(value, "space", moves)

    sent = pl.pallas_call(
        functools.partial(pack_kernel, sizes),
        out_shape=[message] * n_pairs,
        in_specs=[hbm, smem, hbm, hbm],
        out_specs=[vmem] * n_pairs,
        scratch_shapes=[
            pltpu.VMEM(pair_cells.shape, jnp.int32),
            pltpu.VMEM(total.shape, f32),
            pltpu.VMEM(total.shape, f32),
            pltpu.SemaphoreType.DMA((3,)),
        ],
        compiler_params=pltpu.CompilerParams(vmem_limit_bytes=60 * 1024 * 1024),
        name="pack",
    )(pair_cells, pair_count, pos, frc)
    got = [sent[0]] + [across(sent[turn], turn) for turn in range(1, n_pairs)]

    def pairs(arrived, before, marked=False):
        kinds = [(kind, turns) for kind, turns, _ in arrived]
        values = [value for _, _, value in arrived]
        n = len(values)
        blocks = sum(value.shape[0] for value in values)
        return pl.pallas_call(
            functools.partial(pair_kernel, sizes, kinds, len(before), marked),
            out_shape=[total, jax.ShapeDtypeStruct((blocks * rows_out, LANES), f32)]
            + [jax.ShapeDtypeStruct((1, LANES), f32)] * marked,
            in_specs=[vmem] * (n + 2 + len(before)),
            out_specs=[vmem] * (2 + marked),
            scratch_shapes=[
                pltpu.VMEM((blocks * rows_in + TILE, LANES), f32),
                pltpu.VMEM(total.shape, f32),
                pltpu.VMEM(total.shape, f32),
                pltpu.VMEM((4, 2 * tiles * FEATURES + FEATURES, LANES), f32),
                pltpu.VMEM((4, 2 * tiles * GRAM + GRAM, LANES), f32),
                pltpu.VMEM((4, 2 * tiles * FEATURES + FEATURES, LANES), f32),
                pltpu.SMEM((2, blocks * share + 1), jnp.int32),
                pltpu.SMEM((2, blocks * share + 1), f32),
            ],
            input_output_aliases={n + 2: 0} if before else {},
            compiler_params=pltpu.CompilerParams(vmem_limit_bytes=48 * 1024 * 1024),
            cost_estimate=pl.CostEstimate(
                flops=blocks * 1_000_000_000, bytes_accessed=2_000_000, transcendentals=2_000_000
            ),
            name="pairs",
        )(*values, pos, frc, *before)

    near, far = range(2), range(2, n_pairs)
    own = [sent[0][kind : kind + 1] for kind in range(3)]
    core = [got[1][kind : kind + 1] for kind in range(3)]
    out_1n = beyond(jnp.concatenate([own[1], core[1]]), 1)
    acc, reply_0n, nothing = pairs([(0, (0,), own[0]), (0, (1,), core[0])], [], True)
    rest = [got[turn] + nothing[None] for turn in far]
    out_1f = beyond(jnp.stack([value[1] for value in rest]), 1)
    out_2 = beyond(jnp.concatenate([own[2], core[2]] + [value[2:] for value in rest]), 2)
    acc, reply_m = pairs(
        [(1, near, out_1n)] + [(0, (turn,), got[turn][0:1]) for turn in far], [acc]
    )
    acc, reply_f = pairs([(1, far, out_1f), (2, range(n_pairs), out_2)], [acc])
    reply_0n, reply_m, reply_f = (
        value.reshape(-1, rows_out, LANES) for value in (reply_0n, reply_m, reply_f)
    )
    cut = n_pairs - 2
    back_0 = jnp.concatenate([reply_0n, reply_m[2:]])
    back_1 = beyond(jnp.concatenate([reply_m[:2], reply_f[:cut]]), 1)
    back_2 = beyond(reply_f[cut:], 2)
    replies = []
    for turn in range(n_pairs):
        value = jnp.stack([back_0[turn], back_1[turn], back_2[turn]])
        replies.append(across(value, turn) if turn else value)
    where = [(turn, kind) for kind in range(3) for turn in range(n_pairs)]
    velocity = pl.pallas_call(
        functools.partial(add_kernel, sizes, where),
        out_shape=result,
        in_specs=[vmem] * (2 + len(replies)),
        out_specs=vmem,
        scratch_shapes=[pltpu.VMEM(total.shape, f32)],
        compiler_params=pltpu.CompilerParams(vmem_limit_bytes=48 * 1024 * 1024),
        name="add",
    )(acc, own[0], *replies)
    return cell_rows(velocity, cell_dev, points)


def solution(mesh):
    placed = (
        P(("space", "pairs"), None, None),
        P(("space", "pairs"), None, None),
        P(None, ("space", "pairs")),
        P(("space", "pairs")),
    )
    return jax.shard_map(
        body,
        mesh=mesh,
        in_specs=placed,
        out_specs=P(("space", "pairs"), None, None),
        check_vma=False,
    )
```

```python
import functools
import math

import jax
import jax.numpy as jnp
from jax import lax
from jax.experimental import pallas as pl
from jax.experimental.pallas import tpu as pltpu
from jax.sharding import PartitionSpec as P

stokes_coef = 1.0 / (8.0 * math.pi)
eps_sq = 0.01
slab_width = 3.0
across_middle = 1.0
LANES = 128
FEATURES = 16
GRAM = 8
SPARE = 64
TILE = 8

f32 = jnp.float32
bf16 = jnp.bfloat16


def split(value, terms):
    parts = []
    for _ in range(terms - 1):
        part = value.astype(bf16).astype(f32)
        parts.append(part)
        value = value - part
    parts.append(value)
    return parts


def matrix(ref, cell, height, tiles):
    first = cell * tiles
    return jnp.concatenate(
        [ref[(first + t) * height : (first + t + 1) * height, :] for t in range(tiles)], axis=1
    )


def lay_out(x, f, first, feat, gram):
    rows = x[0].shape[0]
    norm = x[0] * x[0] + x[1] * x[1] + x[2] * x[2]
    along = x[0] * f[0] + x[1] * f[1] + x[2] * f[2]
    columns = list(f) + [x[k] * f[c] for k in range(3) for c in range(3)]
    columns += [norm * f[c] + x[c] * along for c in range(3)]
    for number, value in enumerate(columns):
        feat[pl.ds(number, rows, stride=FEATURES), :] = value
    scale = jnp.where(first, 1.0, -2.0)
    terms = [x[c] * scale for c in range(3)]
    terms += [jnp.where(first, norm, 1.0), jnp.where(first, 1.0, norm + eps_sq)]
    for number, value in enumerate(terms):
        gram[pl.ds(number, rows, stride=GRAM), :] = value
    return norm


def combine(sums, x, norm):
    rows = norm.shape[0]
    at = [sums[pl.ds(number, rows, stride=FEATURES), :] for number in range(15)]
    force, second = at[0:3], at[12:15]
    moment = [at[3 + 3 * k : 6 + 3 * k] for k in range(3)]
    trace = moment[0][0] + moment[1][1] + moment[2][2]
    along = x[0] * force[0] + x[1] * force[1] + x[2] * force[2] - trace
    size = norm + 2.0 * eps_sq
    out = []
    for c in range(3):
        mixed = x[0] * moment[0][c] + x[1] * moment[1][c] + x[2] * moment[2][c]
        turned = x[0] * moment[c][0] + x[1] * moment[c][1] + x[2] * moment[c][2]
        value = size * force[c] + second[c] - 2.0 * mixed - turned + x[c] * along
        out.append(value * stokes_coef)
    return out


def gram_product(gram, tiles):
    left = split(matrix(gram, 0, GRAM, tiles), 3)
    right = split(matrix(gram, 1, GRAM, tiles), 3)
    order = ((0, 0), (0, 1), (1, 0), (0, 2), (1, 1), (2, 0))
    return dot(
        jnp.concatenate([left[p] for p, _ in order], axis=0).astype(bf16),
        jnp.concatenate([right[q] for _, q in order], axis=0).astype(bf16),
        0,
        0,
    )


def feature_rows(feat, cell, tiles):
    parts = split(matrix(feat, cell, FEATURES, tiles), 3)
    return jnp.concatenate([part.astype(bf16) for part in parts], axis=0)


def dot(left, right, left_dim, right_dim):
    return lax.dot_general(
        left, right, (((left_dim,), (right_dim,)), ((), ())), preferred_element_type=f32
    )


def fold(high, low):
    third = high[2 * FEATURES :]
    both = high[: 2 * FEATURES] + low
    return both[:FEATURES] + both[FEATURES:] + third


def weights(dist_sq):
    inverse = lax.rsqrt(dist_sq)
    cubed = inverse * inverse * inverse
    high = cubed.astype(bf16)
    low = (cubed - high.astype(f32)).astype(bf16)
    return high, low


def pair_velocities(cells, first, feats, grams, totals):
    tiles = cells[0][0][0].shape[0] // 2
    n = len(cells)
    norms = [lay_out(x, f, first, feats.at[i], grams.at[i]) for i, (x, f) in enumerate(cells)]
    squares = [gram_product(grams.at[i], tiles) for i in range(n)]
    rows = [[feature_rows(feats.at[i], cell, tiles) for cell in range(2)] for i in range(n)]
    results = []
    waiting = []

    def finish():
        i, sums = waiting.pop(0)
        for cell in range(2):
            value = fold(*sums[cell])
            for t in range(tiles):
                place = (cell * tiles + t) * FEATURES
                totals[i, place : place + FEATURES, :] = value[:, t * LANES : (t + 1) * LANES]
        results.append(combine(totals.at[i], cells[i][0], norms[i]))

    for i in range(n):
        high, low = weights(squares[i])
        of_b = dot(rows[i][0], high, 1, 0), dot(rows[i][0][: 2 * FEATURES], low, 1, 0)
        of_a = dot(rows[i][1], high, 1, 1), dot(rows[i][1][: 2 * FEATURES], low, 1, 1)
        waiting.append((i, (of_a, of_b)))
        if len(waiting) > 1:
            finish()
    finish()
    return results


def row_base(cell, tiles):
    return cell // 8 * (8 * tiles) + lax.rem(cell, 8)


def away_of(kind, odd):
    return (0, 1 - 2 * odd, 2 * odd - 1)[kind]


def pack_kernel(sizes, cells_hbm, count, pos_hbm, frc_hbm, *refs):
    n_space, n_pairs, share, cell_dev, tiles = sizes
    outs = refs[:n_pairs]
    cells, pos, frc, sems = refs[n_pairs:]
    fetches = [
        pltpu.make_async_copy(cells_hbm, cells, sems.at[0]),
        pltpu.make_async_copy(pos_hbm, pos.at[pl.ds(0, pos_hbm.shape[0])], sems.at[1]),
        pltpu.make_async_copy(frc_hbm, frc.at[pl.ds(0, frc_hbm.shape[0])], sems.at[2]),
    ]
    for fetch in fetches:
        fetch.start()
    fetches.pop(0).wait()
    n_slots = cells.shape[1]
    shape = (n_slots, n_slots)
    down = lax.broadcasted_iota(jnp.int32, shape, 0)
    along = lax.broadcasted_iota(jnp.int32, shape, 1)
    here = lax.axis_index("space")
    here_turn = lax.axis_index("pairs")

    def bucket(cell):
        there = cell >> (cell_dev * n_pairs).bit_length() - 1
        turn = (cell >> cell_dev.bit_length() - 1) & (n_pairs - 1) ^ here_turn
        kind = jnp.where(there == here, 0, jnp.where(there >> 1 == here >> 1, 1, 2))
        return kind * n_pairs + turn

    def column(row):
        return jnp.sum(jnp.where(down == along, row, 0), axis=1, keepdims=True)

    second = column(cells[1:2, :])
    same = (bucket(second) == bucket(cells[1:2, :])) & (along < down)
    rank = jnp.sum(jnp.where(same, 1, 0), axis=1, keepdims=True)
    live = lax.broadcasted_iota(jnp.int32, (n_slots, 1), 0) < count[0]
    chosen = bucket(second) * share + rank == along

    def by_place(values):
        local = jnp.where(live, values & (cell_dev - 1), -1)
        return jnp.sum(jnp.where(chosen, local, 0), axis=0, keepdims=True)

    label = by_place(second)
    table = by_place(column(cells[0:1, :]))
    last = share * 6 * tiles
    plane = cell_dev * tiles
    for fetch in fetches:
        fetch.wait()
    for m in range(3 * n_pairs):
        kind, turn = m // n_pairs, m % n_pairs
        out = outs[turn]
        for k in range(share):
            base = row_base(jnp.maximum(table[0, m * share + k], 0), tiles)
            for c in range(6):
                source = pos if c < 3 else frc
                row = (k * 6 + c) * tiles
                out[kind, row : row + tiles, :] = source[
                    pl.ds(base + c % 3 * plane, tiles, stride=8), :
                ]
        out[kind, last : last + 1, 0:n_slots] = label.astype(f32)
    outs[0][0, last + 1 : last + 2, 0:n_slots] = table.astype(f32)


def pair_kernel(sizes, kinds, started, marked, *refs):
    n_space, n_pairs, share, cell_dev, tiles = sizes
    n = len(kinds)
    messages, (pos_in, frc_in) = refs[:n], refs[n : n + 2]
    outs = refs[n + 2 + started :]
    (acc, reply), (inbox, pos, frc, feats, grams, totals, todo, middles) = outs[:2], outs[-8:]
    pos[0 : pos_in.shape[0], :] = pos_in[...]
    frc[0 : frc_in.shape[0], :] = frc_in[...]
    feats[...] = jnp.zeros_like(feats)
    grams[...] = jnp.zeros_like(grams)
    rows_in = share * 6 * tiles
    n_slots = 3 * n_pairs * share
    plane = cell_dev * tiles
    if not started:
        acc[...] = jnp.zeros_like(acc)
    if marked:
        outs[2][...] = jnp.zeros_like(outs[2])
    here = lax.axis_index("space")
    number = jnp.int32(0)
    first = 0
    for (kind, turns), message in zip(kinds, messages):
        away = jnp.int32(away_of(kind, lax.rem(here, 2)))
        there = lax.rem(here + away + n_space, n_space)
        half = 0.5 * slab_width * away.astype(f32)
        middle_a = slab_width * (there.astype(f32) + 0.5) - half
        middle_b = slab_width * (here.astype(f32) + 0.5) + half
        for block, turn in enumerate(turns):
            inbox[first * rows_in : (first + 1) * rows_in, :] = message[block, 0:rows_in, :]
            label = message[block, rows_in : rows_in + 1, 0:n_slots].astype(jnp.int32)
            for k in range(share):
                b = label[0, (kind * n_pairs + turn) * share + k]
                todo[0, number] = first * share + k
                todo[1, number] = b
                middles[0, number] = middle_a
                middles[1, number] = middle_b
                number = number + jnp.where(b >= 0, 1, 0)
            first += 1

    first = lax.broadcasted_iota(jnp.int32, (2 * tiles, LANES), 0) < tiles

    def load(i):
        base = todo[0, i] * (6 * tiles)
        start = row_base(todo[1, i], tiles)
        values = []
        for c in range(6):
            ref = pos if c < 3 else frc
            values.append(
                jnp.concatenate(
                    [
                        inbox[pl.ds(base + c * tiles, tiles), :],
                        ref[pl.ds(start + c % 3 * plane, tiles, stride=8), :],
                    ],
                    axis=0,
                )
            )
        x = [values[0] - jnp.where(first, middles[0, i], middles[1, i])]
        x += [value - across_middle for value in values[1:3]]
        return x, values[3:]

    def store(i, velocity):
        base = todo[0, i] * (3 * tiles)
        start = row_base(todo[1, i], tiles)
        places = [pl.ds(start + c * plane, tiles, stride=8) for c in range(3)]
        added = [acc[places[c], :] + velocity[c][tiles:] for c in range(3)]
        for c in range(3):
            acc[places[c], :] = added[c]
            reply[pl.ds(base + c * tiles, tiles), :] = velocity[c][:tiles]

    def several(numbers):
        cells = [load(i) for i in numbers]
        results = pair_velocities(cells, first, feats, grams, totals)
        for i, result in zip(numbers, results):
            store(i, result)

    def four(i, _):
        several([4 * i + j for j in range(4)])
        return 0

    lax.fori_loop(0, number // 4, four, 0)
    left = lax.rem(number, 4)

    for size in range(1, 4):

        @pl.when(left == size)
        def _(size=size):
            several([number - size + j for j in range(size)])


def add_kernel(sizes, where, acc, mine, *refs):
    n_space, n_pairs, share, cell_dev, tiles = sizes
    replies, (out, kept) = refs[:-2], refs[-2:]
    plane = cell_dev * tiles
    last = share * 6 * tiles
    table = mine[0, last + 1 : last + 2, 0 : 3 * n_pairs * share].astype(jnp.int32)
    kept[...] = acc[...]
    for m, (operand, block) in enumerate(where):
        for k in range(share):
            a = table[0, m * share + k]
            live = a >= 0
            base = row_base(jnp.maximum(a, 0), tiles)
            places = [pl.ds(base + c * plane, tiles, stride=8) for c in range(3)]
            totals = []
            for c in range(3):
                row = (k * 3 + c) * tiles
                term = jnp.where(live, replies[operand][block, row : row + tiles, :], 0.0)
                totals.append(kept[places[c], :] + term)
            for c in range(3):
                kept[places[c], :] = totals[c]
    out[...] = kept[0 : out.shape[0], :]


def flat_rows(cells):
    count, _, points = cells.shape
    value = jnp.transpose(cells, (1, 0, 2)).reshape(3, count // 8, 8, points // LANES, LANES)
    return jnp.transpose(value, (0, 1, 3, 2, 4)).reshape(-1, LANES)


def cell_rows(rows, count, points):
    value = rows.reshape(3, count // 8, points // LANES, 8, LANES)
    value = jnp.transpose(value, (0, 1, 3, 2, 4)).reshape(3, count, points)
    return jnp.transpose(value, (1, 0, 2))


def body(positions, forces, pair_cells, pair_count):
    n_space = lax.axis_size("space")
    n_pairs = lax.axis_size("pairs")
    cell_dev, _, points = positions.shape
    n_slots = pair_cells.shape[1]
    share = n_slots // (3 * n_pairs)
    tiles = points // LANES
    sizes = (n_space, n_pairs, share, cell_dev, tiles)
    rows_in = share * 6 * tiles
    rows_out = share * 3 * tiles
    pos = flat_rows(positions)
    frc = flat_rows(forces)
    vmem = pl.BlockSpec(memory_space=pltpu.VMEM)
    smem = pl.BlockSpec(memory_space=pltpu.SMEM)
    hbm = pl.BlockSpec(memory_space=pltpu.HBM)
    message = jax.ShapeDtypeStruct((3, rows_in + 8, LANES), f32)
    total = jax.ShapeDtypeStruct((3 * cell_dev * tiles + SPARE, LANES), f32)
    result = jax.ShapeDtypeStruct((3 * cell_dev * tiles, LANES), f32)

    def across(value, turn):
        return lax.ppermute(value, "pairs", [(j, j ^ turn) for j in range(n_pairs)])

    def beyond(value, kind):
        moves = [(i, (i + away_of(kind, i % 2)) % n_space) for i in range(n_space)]
        return lax.ppermute(value, "space", moves)

    sent = pl.pallas_call(
        functools.partial(pack_kernel, sizes),
        out_shape=[message] * n_pairs,
        in_specs=[hbm, smem, hbm, hbm],
        out_specs=[vmem] * n_pairs,
        scratch_shapes=[
            pltpu.VMEM(pair_cells.shape, jnp.int32),
            pltpu.VMEM(total.shape, f32),
            pltpu.VMEM(total.shape, f32),
            pltpu.SemaphoreType.DMA((3,)),
        ],
        compiler_params=pltpu.CompilerParams(vmem_limit_bytes=60 * 1024 * 1024),
        name="pack",
    )(pair_cells, pair_count, pos, frc)
    got = [sent[0]] + [across(sent[turn], turn) for turn in range(1, n_pairs)]

    def pairs(arrived, before, marked=False):
        kinds = [(kind, turns) for kind, turns, _ in arrived]
        values = [value for _, _, value in arrived]
        n = len(values)
        blocks = sum(value.shape[0] for value in values)
        return pl.pallas_call(
            functools.partial(pair_kernel, sizes, kinds, len(before), marked),
            out_shape=[total, jax.ShapeDtypeStruct((blocks * rows_out, LANES), f32)]
            + [jax.ShapeDtypeStruct((1, LANES), f32)] * marked,
            in_specs=[vmem] * (n + 2 + len(before)),
            out_specs=[vmem] * (2 + marked),
            scratch_shapes=[
                pltpu.VMEM((blocks * rows_in + TILE, LANES), f32),
                pltpu.VMEM(total.shape, f32),
                pltpu.VMEM(total.shape, f32),
                pltpu.VMEM((4, 2 * tiles * FEATURES + FEATURES, LANES), f32),
                pltpu.VMEM((4, 2 * tiles * GRAM + GRAM, LANES), f32),
                pltpu.VMEM((4, 2 * tiles * FEATURES + FEATURES, LANES), f32),
                pltpu.SMEM((2, blocks * share + 1), jnp.int32),
                pltpu.SMEM((2, blocks * share + 1), f32),
            ],
            input_output_aliases={n + 2: 0} if before else {},
            compiler_params=pltpu.CompilerParams(vmem_limit_bytes=48 * 1024 * 1024),
            cost_estimate=pl.CostEstimate(
                flops=blocks * 1_000_000_000, bytes_accessed=2_000_000, transcendentals=2_000_000
            ),
            name="pairs",
        )(*values, pos, frc, *before)

    near, far = range(2), range(2, n_pairs)
    own = [sent[0][kind : kind + 1] for kind in range(3)]
    core = [got[1][kind : kind + 1] for kind in range(3)]
    out_1n = beyond(jnp.concatenate([own[1], core[1]]), 1)
    acc, reply_0n, nothing = pairs([(0, (0,), own[0]), (0, (1,), core[0])], [], True)
    rest = [got[turn] + nothing[None] for turn in far]
    out_1f = beyond(jnp.stack([value[1] for value in rest]), 1)
    out_2 = beyond(jnp.concatenate([own[2], core[2]] + [value[2:] for value in rest]), 2)
    acc, reply_m = pairs(
        [(1, near, out_1n)] + [(0, (turn,), got[turn][0:1]) for turn in far], [acc]
    )
    acc, reply_f = pairs([(1, far, out_1f), (2, range(n_pairs), out_2)], [acc])
    reply_0n, reply_m, reply_f = (
        value.reshape(-1, rows_out, LANES) for value in (reply_0n, reply_m, reply_f)
    )
    cut = n_pairs - 2
    back_0 = jnp.concatenate([reply_0n, reply_m[2:]])
    back_1 = beyond(jnp.concatenate([reply_m[:2], reply_f[:cut]]), 1)
    back_2 = beyond(reply_f[cut:], 2)
    replies = []
    for turn in range(n_pairs):
        value = jnp.stack([back_0[turn], back_1[turn], back_2[turn]])
        replies.append(across(value, turn) if turn else value)
    where = [(turn, kind) for kind in range(3) for turn in range(n_pairs)]
    velocity = pl.pallas_call(
        functools.partial(add_kernel, sizes, where),
        out_shape=result,
        in_specs=[vmem] * (2 + len(replies)),
        out_specs=vmem,
        scratch_shapes=[pltpu.VMEM(total.shape, f32)],
        compiler_params=pltpu.CompilerParams(vmem_limit_bytes=48 * 1024 * 1024),
        name="add",
    )(acc, own[0], *replies)
    return cell_rows(velocity, cell_dev, points)


def solution(mesh):
    placed = (
        P(("space", "pairs"), None, None),
        P(("space", "pairs"), None, None),
        P(None, ("space", "pairs")),
        P(("space", "pairs")),
    )
    return jax.shard_map(
        body,
        mesh=mesh,
        in_specs=placed,
        out_specs=P(("space", "pairs"), None, None),
        check_vma=False,
    )
```
